256 devices in a mesh: wide: 128 (over z, y, x), narrow: 2 (over core).
Axes of the slice: x: 4, y: 4, z: 8, core: 2. Of those that a mesh axis runs over, the one named last changes fastest.
Arguments:
- features: bfloat16 [512, 96, 512], P(('wide', 'narrow')), may hold values from -6 to 6
- occupancy: int32 [512, 512], P(('wide', 'narrow')), may hold values 0 or 1
- conv1_weight: bfloat16 [27, 96, 96], replicated, may hold values from -0.125 to 0.125
- conv2_weight: bfloat16 [27, 96, 96], replicated, may hold values from -0.125 to 0.125
- out_grad: bfloat16 [512, 96, 512], P(('wide', 'narrow')), may hold values from -6 to 6
- neighbour_slots: int32 [512, 27], P(('wide', 'narrow')), may hold values from 0 to 14, as said below
- send_blocks: int32 [256, 3, 2, 2], P(('wide', 'narrow')), may hold values from 0 to 2, as said below
Outputs:
- output: bfloat16 [512, 96, 512], P(('wide', 'narrow'))
- feature_grad: bfloat16 [512, 96, 512], P(('wide', 'narrow'))
- conv1_grad: float32 [27, 96, 96], replicated
- conv2_grad: float32 [27, 96, 96], replicated
The draws below stay inside these ranges and needn't reach their ends.
Inputs may be any that keep to these rules, and one draw needn't show every extreme that they name: `neighbour_slots`: direction 13 of block t names t's own local index. A value under 2 is an own block, 14 an empty neighbour, and other values name only halo slots that the sending device fills. `send_blocks`: entry [d, g, m, c] is the local block that device d sends as slot c to the device at wide index w + g - 1 and narrow index m; 2 means none. Entries that would leave the wide axis, and those of a device to itself, are 2; every other pair of devices at most one wide step apart has slot 0 filled, and slots of one pair name distinct blocks.
All inputs are finite; a program needn't handle non-finite values. No bound on the sum of `occupancy` on one device may be relied on, other than what follows from the above.
Results may differ from the reference program's by a relative error of at most 0.0045.
Values may be sent and summed in bfloat16 or wider, within the bound.
A program may use at most 128 MiB of HBM per device.

```python
import jax
import jax.numpy as jnp
from jax import lax

C = 96
V = 512
CAP = 2
B_DEV = 2
TB = 512
HALO = 12
N_WIDE = 128
N_NARROW = 2
DEVICES = 256


def slot_sources(key):
    subkeys = jax.random.split(key, 3)
    grid_shape = (N_WIDE, N_NARROW, 3, N_NARROW, CAP)
    first_block = jax.random.randint(subkeys[0], grid_shape, 0, B_DEV)[..., :1]
    advance = jax.random.randint(subkeys[1], grid_shape, 0, B_DEV - 1)
    coin_flip = jax.random.randint(subkeys[2], grid_shape, 0, 2)
    place_index = lax.broadcasted_iota(jnp.int32, grid_shape, 4)
    chosen = jnp.where(place_index == 0, first_block, (first_block + 1 + advance) % B_DEV)
    wide_index = lax.broadcasted_iota(jnp.int32, grid_shape, 0)
    narrow_index = lax.broadcasted_iota(jnp.int32, grid_shape, 1)
    group_index = lax.broadcasted_iota(jnp.int32, grid_shape, 2)
    narrow_source = lax.broadcasted_iota(jnp.int32, grid_shape, 3)
    wide_source = wide_index - (group_index - 1)
    used_slot = (wide_source >= 0) & (wide_source < N_WIDE)
    used_slot = used_slot & jnp.logical_not((group_index == 1) & (narrow_source == narrow_index))
    used_slot = used_slot & ((place_index == 0) | (coin_flip == 1))
    return jnp.where(used_slot, chosen, B_DEV).astype(jnp.int32)


def draw_send_blocks(key, part):
    sources = slot_sources(key)
    grid_shape = (N_WIDE, N_NARROW, 3, N_NARROW, CAP)
    wide_index = lax.broadcasted_iota(jnp.int32, grid_shape, 0)
    narrow_index = lax.broadcasted_iota(jnp.int32, grid_shape, 1)
    group_index = lax.broadcasted_iota(jnp.int32, grid_shape, 2)
    target_narrow = lax.broadcasted_iota(jnp.int32, grid_shape, 3)
    place_index = lax.broadcasted_iota(jnp.int32, grid_shape, 4)
    wide_target = wide_index + group_index - 1
    picked = sources[jnp.clip(wide_target, 0, N_WIDE - 1), target_narrow, group_index, narrow_index, place_index]
    inside = (wide_target >= 0) & (wide_target < N_WIDE)
    return jnp.where(inside, picked, B_DEV).reshape(DEVICES, 3, N_NARROW, CAP).astype(jnp.int32)


def draw_neighbour_slots(key, part):
    sources = slot_sources(key)
    key = jax.random.fold_in(key, 7)
    used_slot = (sources < B_DEV).reshape(DEVICES, HALO)
    subkeys = jax.random.split(key, 3)
    grid_shape = (DEVICES, B_DEV, 27)
    category = jax.random.randint(subkeys[0], grid_shape, 0, 4)
    own_block = jax.random.randint(subkeys[1], grid_shape, 0, B_DEV)
    slot_index = jax.random.randint(subkeys[2], grid_shape, 0, HALO)
    live_slot = jnp.take_along_axis(used_slot, slot_index.reshape(DEVICES, B_DEV * 27), axis=1).reshape(grid_shape)
    halo_entry = jnp.where(live_slot, B_DEV + slot_index, B_DEV + HALO)
    chosen = jnp.where(category == 0, own_block, jnp.where(category == 3, B_DEV + HALO, halo_entry))
    direction = lax.broadcasted_iota(jnp.int32, grid_shape, 2)
    block_index = lax.broadcasted_iota(jnp.int32, grid_shape, 1)
    chosen = jnp.where(direction == 13, block_index, chosen)
    return chosen.reshape(TB, 27).astype(jnp.int32)


def with_ends(values, rng, least, high):
    longest = values.shape.index(max(values.shape))
    spots = []
    for shift in (0, 1):
        where = [jax.random.randint(jax.random.fold_in(rng, axis), (), 0, length) for axis, length in enumerate(values.shape)]
        where[longest] = (where[longest] + shift) % values.shape[longest]
        spots.append(tuple(where))
    return values.at[spots[0]].set(least).at[spots[1]].set(high)


def levels(stream_key, shape, cuts, least, largest):
    level, own = 1.0, jax.random.fold_in(stream_key, 6)
    for axis_at, shards_of in cuts:
        steps = jnp.exp(jax.random.uniform(jax.random.fold_in(own, axis_at), (shards_of,), jnp.float32, least / len(cuts), largest / len(cuts)))
        level = level * jnp.repeat(steps, shape[axis_at] // shards_of).reshape([-1 if axis == axis_at else 1 for axis in range(len(shape))])
    return level


def bell_draw(own_key, dims, scale, bound, cuts=(), held_as=jnp.bfloat16):
    array = jax.random.normal(own_key, dims, jnp.float32) * scale
    if len(cuts) > 0:
        array = levels(own_key, dims, cuts, -0.22, 0.18) * array
    return jnp.clip(array, min=-bound, max=bound).astype(held_as)


def setup_inputs(seed: int = 0) -> dict:
    arg_keys = jax.random.split(jax.random.key(seed), 8)
    return {
        "features": bell_draw(arg_keys[0], (TB, C, V), 1.0, 6.0, ((0, 256),)),
        "occupancy": with_ends((jax.random.randint(arg_keys[1], (TB, V), 0, 4) < 3).astype(jnp.int32), jax.random.fold_in(arg_keys[1], 1), 0, 1),
        "conv1_weight": bell_draw(arg_keys[2], (27, C, C), (27 * C) ** -0.5, 0.125),
        "conv2_weight": bell_draw(arg_keys[3], (27, C, C), (27 * C) ** -0.5, 0.125),
        "out_grad": bell_draw(arg_keys[4], (TB, C, V), 1.0, 6.0, ((0, 256),)),
        "neighbour_slots": draw_neighbour_slots(jax.random.fold_in(arg_keys[7], 71), 0),
        "send_blocks": draw_send_blocks(jax.random.fold_in(arg_keys[7], 71), 0),
    }


def offset_list():
    return [shift_x * 100 + shift_y * 10 + shift_z for shift_x in (-1, 0, 1) for shift_y in (-1, 0, 1) for shift_z in (-1, 0, 1)]

def build_padded(rows):
    block_count = rows.shape[0]
    channels = rows.shape[2]
    blocks_cube = rows.reshape(block_count, 3, 3, 3, channels, 8, 8, 8)
    along_x = jnp.concatenate([blocks_cube[:, 0, :, :, :, 7:8], blocks_cube[:, 1], blocks_cube[:, 2, :, :, :, 0:1]], axis=4)
    along_y = jnp.concatenate([along_x[:, 0, :, :, :, 7:8], along_x[:, 1], along_x[:, 2, :, :, :, 0:1]], axis=4)
    along_z = jnp.concatenate([along_y[:, 0, :, :, :, 7:8], along_y[:, 1], along_y[:, 2, :, :, :, 0:1]], axis=4)
    return along_z.reshape(block_count, channels, 1000)

def unfold(flat, starts, length):
    return jnp.stack([lax.slice_in_dim(flat, start, start + length, axis=2) for start in starts], axis=1)

def interior(full):
    block_count, channels, _ = full.shape
    padded = jnp.pad(full, ((0, 0), (0, 0), (0, 22)))
    return padded.reshape(block_count, channels, 8, 10, 10)[:, :, :, :8, :8].reshape(block_count, channels, 512)

def extend(block_grad):
    block_count, channels, _ = block_grad.shape
    cube = jnp.pad(block_grad.reshape(block_count, channels, 8, 8, 8), ((0, 0), (0, 0), (1, 1), (1, 1), (1, 1)))
    return jnp.pad(cube.reshape(block_count, channels, 1000), ((0, 0), (0, 0), (111, 111)))

def output_layout(block_grad):
    block_count, channels, _ = block_grad.shape
    cube = jnp.pad(block_grad.reshape(block_count, channels, 8, 8, 8), ((0, 0), (0, 0), (0, 0), (0, 2), (0, 2)))
    return cube.reshape(block_count, channels, 800)[:, :, :778]

def global_ids(neighbour_slots, send_blocks):
    all_blocks = neighbour_slots.shape[0]
    halo_count = 3 * N_NARROW * CAP
    owner_dev = (jnp.arange(all_blocks, dtype=jnp.int32) // B_DEV)[:, None]
    entry = neighbour_slots
    slot_index = jnp.clip(entry - B_DEV, 0, halo_count - 1)
    group_index = slot_index // (N_NARROW * CAP)
    source_narrow = slot_index // CAP % N_NARROW
    place_index = slot_index % CAP
    wide_here = owner_dev // N_NARROW
    narrow_here = owner_dev % N_NARROW
    wide_source = wide_here - (group_index - 1)
    inside = (wide_source >= 0) & (wide_source < N_WIDE)
    sender = jnp.clip(wide_source, 0, N_WIDE - 1) * N_NARROW + source_narrow
    picked = send_blocks[sender, group_index, jnp.broadcast_to(narrow_here, entry.shape), place_index]
    remote = jnp.where(inside & (picked < B_DEV), sender * B_DEV + picked, all_blocks)
    own_block = owner_dev * B_DEV + entry
    chosen = jnp.where(entry < B_DEV, own_block, jnp.where(entry < B_DEV + halo_count, remote, all_blocks))
    return chosen.astype(jnp.int32)

def with_zero(source):
    return jnp.concatenate([source, jnp.zeros((1,) + source.shape[1:], source.dtype)])

def forward_all(source, block_ids, weights):
    source_table = with_zero(source)
    starts = [111 + offset for offset in offset_list()]

    def one_group(group_ids):
        columns = unfold(build_padded(source_table[group_ids]), starts, 778).astype(jnp.float32)
        return interior(jnp.einsum('oab,mobq->maq', weights.astype(jnp.float32), columns))
    result = lax.map(one_group, block_ids.reshape(DEVICES, B_DEV, 27))
    return result.reshape(TB, C, V)

def weight_all(block_grad, source, block_ids):
    source_table = with_zero(source)
    starts = [111 + offset for offset in offset_list()]

    def one_group(running, inputs_pair):
        group_ids, group_grad = inputs_pair
        columns = unfold(build_padded(source_table[group_ids]), starts, 778).astype(jnp.float32)
        layout = output_layout(group_grad).astype(jnp.float32)
        return (running + jnp.einsum('maq,mobq->oab', layout, columns), None)
    start_value = jnp.zeros((27, C, C), jnp.float32)
    summed, _ = lax.scan(one_group, start_value, (block_ids.reshape(DEVICES, B_DEV, 27), block_grad.reshape(DEVICES, B_DEV, C, V)))
    return summed

def transpose_all(block_grad, block_ids, weights):
    starts = [111 - offset for offset in offset_list()]

    def one_group(running, inputs_pair):
        group_ids, group_grad = inputs_pair
        columns = unfold(extend(group_grad), starts, 1000).astype(jnp.float32)
        spread = jnp.einsum('oab,moaq->mbq', weights.astype(jnp.float32), columns)
        zero_rows = jnp.zeros((B_DEV, 27, C, V), jnp.float32)
        _, pullback = jax.vjp(build_padded, zero_rows)
        row_grads = pullback(spread)[0]
        return (running.at[group_ids].add(row_grads), None)
    start_value = jnp.zeros((TB + 1, C, V), jnp.float32)
    summed, _ = lax.scan(one_group, start_value, (block_ids.reshape(DEVICES, B_DEV, 27), block_grad.reshape(DEVICES, B_DEV, C, V)))
    return summed[:TB]

def reference(features, occupancy, conv1_weight, conv2_weight, out_grad, neighbour_slots, send_blocks):
    block_ids = global_ids(neighbour_slots, send_blocks)
    occupied = occupancy.astype(jnp.bfloat16)[:, None, :]
    occupied_float = occupancy.astype(jnp.float32)[:, None, :]
    active = features * occupied
    first_pre = forward_all(active, block_ids, conv1_weight)
    hidden = (jax.nn.silu(first_pre) * occupied_float).astype(jnp.bfloat16)
    second_pre = forward_all(hidden, block_ids, conv2_weight)
    output = ((active.astype(jnp.float32) + second_pre) * occupied_float).astype(jnp.bfloat16)
    grad_scale = 1.0 / jnp.sqrt(jnp.float32(TB * V))
    masked_grad = out_grad * occupied
    conv2_grad = weight_all(masked_grad, hidden, block_ids) * grad_scale
    hidden_grad = transpose_all(masked_grad, block_ids, conv2_weight)
    sigmoid_value = jax.nn.sigmoid(first_pre)
    pre_grad = (hidden_grad * occupied_float * sigmoid_value * (1.0 + first_pre * (1.0 - sigmoid_value))).astype(jnp.bfloat16)
    conv1_grad = weight_all(pre_grad, active, block_ids) * grad_scale
    input_grad = masked_grad.astype(jnp.float32) + transpose_all(pre_grad, block_ids, conv1_weight)
    feature_grad = (input_grad * occupied_float).astype(jnp.bfloat16)
    return (output, feature_grad, conv1_grad, conv2_grad)
```

```python
import functools

import jax
import jax.numpy as jnp
from jax import lax
from jax.experimental import pallas as pl
from jax.experimental.pallas import tpu as pltpu
from jax.sharding import PartitionSpec as P

MESH = pl.DeviceIdType.MESH
F32 = jnp.float32
BF16 = jnp.bfloat16
C = 96
L = 128
V = 512
B = 2
SLOTS = 12
EMPTY = 14
SHELL = 320
OFFSETS = [(a, b, e) for a in (-1, 0, 1) for b in (-1, 0, 1) for e in (-1, 0, 1)]
PAIRS = [(a, b) for a in (-1, 0, 1) for b in (-1, 0, 1)]
PLACE = {-1: slice(0, 1), 0: slice(1, 9), 1: slice(9, 10)}
LAYER = {-1: slice(7, 8), 0: slice(0, 8), 1: slice(0, 1)}
ROWS = 4096
WG = 27 * C
THIRD = 1296
VMEM_LIMIT = 56 * 1024 * 1024


def direction(a, b, e):
    return 9 * (a + 1) + 3 * (b + 1) + e + 1


def depth_index(shape):
    return lax.broadcasted_iota(jnp.int32, shape, len(shape) - 2)


def roll_depth(value, shift):
    return pltpu.roll(value, shift % 8, value.ndim - 2)


def to_rows(value):
    wide = jnp.concatenate([value, jnp.zeros((L - C, V), F32)], axis=0)
    return wide.T


def pack_shell(table, entry, shell, once):
    shell[0:8] = table[entry, 0]
    shell[8:16] = table[entry, 7]
    shell[16:22] = table[entry, 1:7, 0]
    shell[22:28] = table[entry, 1:7, 7]
    for at, z in ((28, 0), (34, 7)):
        plane = table[entry, 1:7, :, z, :]
        if once:
            y = depth_index(plane.shape)
            plane = jnp.where((y > 0) & (y < 7), plane, 0.0)
        shell[at : at + 6] = plane
    return shell[...].reshape(SHELL, L).astype(BF16)


def unpack_shell(rows, table, entry):
    shell = rows.astype(F32).reshape(SHELL // 8, 8, L)
    table[entry, 0] = shell[0:8]
    table[entry, 7] = shell[8:16]
    table[entry, 1:7, 0] = shell[16:22]
    table[entry, 1:7, 7] = shell[22:28]
    table[entry, 1:7, :, 0, :] = shell[28:34]
    table[entry, 1:7, :, 7, :] = shell[34:40]


def add_shell(rows, table, entry):
    shell = rows.astype(F32).reshape(SHELL // 8, 8, L)
    table[entry, 0] += shell[0:8]
    table[entry, 7] += shell[8:16]
    table[entry, 1:7, 0] += shell[16:22]
    table[entry, 1:7, 7] += shell[22:28]
    table[entry, 1:7, :, 0, :] += shell[28:34]
    table[entry, 1:7, :, 7, :] += shell[34:40]


def pack_sends(plan, table, shell, both, out):
    for t in range(B):
        both[t] = pack_shell(table, t, shell, False)

    def one(j, carry):
        out[j] = both[jnp.minimum(plan[j], B - 1)]
        return carry

    lax.fori_loop(0, SLOTS, one, 0)


def pack_gradients(grads, shell, out):
    def one(j, carry):
        out[j] = pack_shell(grads, B + j, shell, True)
        return carry

    lax.fori_loop(0, SLOTS, one, 0)


def fill_table(table, own, halo):
    for t in range(B):
        table[t] = own[t].astype(F32).reshape(8, 8, 8, L)

    def one(j, carry):
        unpack_shell(halo[j], table, B + j)
        return carry

    lax.fori_loop(0, SLOTS, one, 0)
    table[EMPTY] = jnp.zeros((8, 8, 8, L), F32)


def build_columns(slots, table, shifted, columns):
    def one(t, carry):
        for a, b in PAIRS:
            def source(e):
                return table[slots[t, direction(a, b, e)], LAYER[a], LAYER[b]]

            here = source(0)
            z = depth_index(here.shape)
            shifted[1, PLACE[a], PLACE[b]] = here
            shifted[0, PLACE[a], PLACE[b]] = roll_depth(jnp.where(z == 7, source(-1), here), 1)
            shifted[2, PLACE[a], PLACE[b]] = roll_depth(jnp.where(z == 0, source(1), here), -1)
        rows = pl.ds(pl.multiple_of(t * V, V), V)
        for o, (a, b, e) in enumerate(OFFSETS):
            part = shifted[e + 1, a + 1 : a + 9, b + 1 : b + 9]
            columns[rows, o * L : (o + 1) * L] = part.reshape(V, L).astype(BF16)
        return carry

    lax.fori_loop(0, B, one, 0)


def side_weights(weights, side):
    side[...] = jnp.zeros_like(side)
    for o in range(27):
        side[0:C, o * L : o * L + C] = weights[o]


def back_weights(weights, back):
    back[...] = jnp.zeros_like(back)
    for o in range(27):
        k, e = o // 3, o % 3
        back[k * L : k * L + C, e * L : e * L + C] = weights[o]


def spread(slots, padded, around, back, grads):
    grads[...] = jnp.zeros_like(grads)

    def one(t, carry):
        for k, (a, b) in enumerate(PAIRS):
            part = padded[t, 1 - a : 11 - a, 1 - b : 11 - b]
            around[:, k * L : (k + 1) * L] = part.reshape(800, L).astype(BF16)
        by_depth = jnp.dot(around[...], back[...], preferred_element_type=F32).reshape(10, 10, 8, 3 * L)
        low = roll_depth(by_depth[..., 0:L], -1)
        high = roll_depth(by_depth[..., 2 * L : 3 * L], 1)
        z = depth_index(low.shape)
        parts = {
            -1: jnp.where(z == 7, low, 0.0),
            0: by_depth[..., L : 2 * L] + jnp.where(z != 0, high, 0.0) + jnp.where(z != 7, low, 0.0),
            1: jnp.where(z == 0, high, 0.0),
        }
        for a, b, e in OFFSETS:
            entry = slots[t, direction(a, b, e)]
            grads[entry, LAYER[a], LAYER[b]] += parts[e][PLACE[a], PLACE[b]]
        return carry

    lax.fori_loop(0, B, one, 0)


def first_kernel(slots, plan, features, occupancy, out_grad, weights,
                 active, mask, send_active, send_grads, own_grads,
                 table, padded, around, back, grads, shell, both):
    padded[...] = jnp.zeros_like(padded)
    for t in range(B):
        seen = occupancy[t : t + 1, :].astype(F32)
        rows = to_rows(features[t].astype(F32) * seen)
        active[t] = rows.astype(BF16)
        table[t] = rows.reshape(8, 8, 8, L)
        mask[t] = jnp.broadcast_to(seen, (L, V)).T.astype(BF16)
        padded[t, 2:10, 2:10] = to_rows(out_grad[t].astype(F32) * seen).reshape(8, 8, 8, L)
    pack_sends(plan, table, shell, both, send_active)
    back_weights(weights, back)
    spread(slots, padded, around, back, grads)
    pack_gradients(grads, shell, send_grads)
    for t in range(B):
        own_grads[t] = grads[t].reshape(V, L)


def second_kernel(slots, plan, active, mask, halo, own_grads, arrived, weights,
                  hidden, send_hidden, send_grads, own_out, weight_grad,
                  table, shifted, columns, side, padded, around, back, grads, shell, both, pre):
    fill_table(table, active, halo)
    build_columns(slots, table, shifted, columns)
    side_weights(weights, side)
    for t in range(B):
        grads[t] = own_grads[t].reshape(8, 8, 8, L)

    def give(j, carry):
        add_shell(arrived[j], grads, plan[j])
        return carry

    lax.fori_loop(0, SLOTS, give, 0)
    padded[...] = jnp.zeros_like(padded)
    for t in range(B):
        value = lax.dot_general(
            columns[t * V : (t + 1) * V, :], side[...], (((1,), (1,)), ((), ())), preferred_element_type=F32
        )
        seen = mask[t].astype(F32)
        gate = jax.nn.sigmoid(value)
        out = (value * gate * seen).astype(BF16)
        hidden[t] = out
        table[t] = out.astype(F32).reshape(8, 8, 8, L)
        grad = grads[t].reshape(V, L) * seen * gate * (1.0 + value * (1.0 - gate))
        padded[t, 2:10, 2:10] = grad.reshape(8, 8, 8, L)
        pre[:, t * V : (t + 1) * V] = grad.T.astype(BF16)
    pack_sends(plan, table, shell, both, send_hidden)
    back_weights(weights, back)
    spread(slots, padded, around, back, grads)
    pack_gradients(grads, shell, send_grads)
    for t in range(B):
        own_out[t] = grads[t].reshape(V, L)
    weight_sums(pre, columns, weight_grad, 0)


def weight_sums(left, columns, out, at):
    for o in range(0, 27, 3):
        sums = jnp.dot(left[...], columns[:, o * L : (o + 3) * L], preferred_element_type=F32)
        for i in range(3):
            row = at + (o + i) * C
            out[row : row + C] = sums[0:C, i * L : (i + 1) * L]


def third_kernel(slots, plan, hidden, halo, own_grads, arrived, features, occupancy, out_grad, weights, first_sums,
                 output, feature_grad, packed,
                 table, shifted, columns, side, grads, masked, sums):
    fill_table(table, hidden, halo)
    build_columns(slots, table, shifted, columns)
    side_weights(weights, side)
    for t in range(B):
        grads[t] = own_grads[t].reshape(8, 8, 8, L)

    def give(j, carry):
        add_shell(arrived[j], grads, plan[j])
        return carry

    lax.fori_loop(0, SLOTS, give, 0)
    for t in range(B):
        seen = occupancy[t : t + 1, :].astype(F32)
        value = lax.dot_general(
            side[...], columns[t * V : (t + 1) * V, :], (((1,), (1,)), ((), ())), preferred_element_type=F32
        )
        output[t] = ((features[t].astype(F32) * seen + value[0:C]) * seen).astype(BF16)
        own = out_grad[t].astype(F32) * seen
        masked[0:C, t * V : (t + 1) * V] = own.astype(BF16)
        back = grads[t].reshape(V, L).T
        feature_grad[t] = ((own + back[0:C]) * seen).astype(BF16)
    masked[C:L] = jnp.zeros((L - C, B * V), BF16)
    sums[0:WG] = first_sums[...]
    weight_sums(masked, columns, sums, WG)
    last = sums[3 * THIRD : 4 * THIRD]
    lane = lax.broadcasted_iota(jnp.int32, (THIRD, L), 1)
    for i in range(3):
        moved = pltpu.roll(last, C - 32 * i, 1)
        packed[i * THIRD : (i + 1) * THIRD] = jnp.where(lane < C, sums[i * THIRD : (i + 1) * THIRD], moved)
    packed[3 * THIRD : ROWS] = jnp.zeros((ROWS - 3 * THIRD, L), F32)


def last_kernel(scale, packed, first, second):
    lane = lax.broadcasted_iota(jnp.int32, (THIRD, L), 1)
    last = jnp.zeros((THIRD, L), F32)
    for i in range(3):
        part = packed[i * THIRD : (i + 1) * THIRD].astype(F32) * scale
        last = jnp.where(lane // 32 == i, pltpu.roll(part, 32 + 32 * i, 1), last)
    for r in range(0, 2 * WG, 48):
        out, o, at = (first, r // C, r % C) if r < WG else (second, (r - WG) // C, r % C)
        if r < 3 * THIRD:
            rows = packed[r : r + 48].astype(F32) * scale
        else:
            rows = last[r - 3 * THIRD : r - 3 * THIRD + 48]
        out[o, at : at + 48, :] = rows[:, 0:C]


def exchange_kernel(n_wide, send_near, send_back, near, returned, send_sem, recv_sem):
    w, n = lax.axis_index("wide"), lax.axis_index("narrow")
    ahead, behind = lax.rem(w + 1, n_wide), lax.rem(w + n_wide - 1, n_wide)
    peers = [(behind, 0), (behind, 1), (ahead, 0), (ahead, 1), (w, 1 - n)]
    barrier = pltpu.get_barrier_semaphore()
    for peer in peers:
        pl.semaphore_signal(barrier, inc=1, device_id=peer, device_id_type=MESH)
    pl.semaphore_wait(barrier, 5)
    copies = []
    for i, (peer, g) in enumerate(zip(peers, (0, 0, 2, 2, 1))):
        back_group = 2 - g
        for k, (source, dest, group) in enumerate(((send_near, near, g), (send_back, returned, back_group))):
            copy = pltpu.make_async_remote_copy(
                src_ref=source.at[group, peer[1]],
                dst_ref=dest.at[group, n],
                send_sem=send_sem.at[2 * i + k],
                recv_sem=recv_sem.at[group, n, k],
                device_id=peer,
                device_id_type=MESH,
            )
            copy.start()
            copies.append((copy, group, peer[1], k, dest))
    for copy, group, m, k, dest in copies:
        copy.wait_send()
        pltpu.make_async_remote_copy(
            src_ref=dest.at[group, m], dst_ref=dest.at[group, m], send_sem=send_sem.at[0],
            recv_sem=recv_sem.at[group, m, k], device_id=(w, 1 - n), device_id_type=MESH,
        ).wait_recv()


def reduce_kernel(nz, nxy, src, out, half, sums, got1, got2, got3, whole, s1, r1, s2, r2, s3, r3, s4, r4, s5, r5, s6, r6):
    w, n = lax.axis_index("wide"), lax.axis_index("narrow")
    z, xy = w // nxy, lax.rem(w, nxy)
    halves, plane = ROWS // 2, ROWS // 2 // nxy
    piece = plane // nz
    partner = (w, 1 - n)
    in_plane = [(z * nxy + lax.rem(xy + d, nxy), n) for d in range(1, nxy)]
    in_column = [(lax.rem(z + d, nz) * nxy + xy, n) for d in range(1, nz)]
    everyone = [partner] + in_plane + in_column
    barrier = pltpu.get_barrier_semaphore()
    for peer in everyone:
        pl.semaphore_signal(barrier, inc=1, device_id=peer, device_id_type=MESH)
    pl.semaphore_wait(barrier, len(everyone))

    def start(source, dest, send, recv, peer):
        copy = pltpu.make_async_remote_copy(
            src_ref=source, dst_ref=dest, send_sem=send, recv_sem=recv, device_id=peer, device_id_type=MESH
        )
        copy.start()
        return copy

    def rows(at, size):
        return pl.ds(pl.multiple_of(at, size), size)

    mine = rows(n * halves, halves)
    copy = start(src.at[rows((1 - n) * halves, halves)], got1, s1, r1, partner)
    copy.wait()
    half[...] = (src[mine, :] + got1[...]).astype(BF16)

    copies = []
    for d, peer in enumerate(in_plane):
        to = lax.rem(xy + d + 1, nxy)
        copies.append(start(half.at[rows(to * plane, plane)], got2.at[d], s2.at[d], r2.at[d], peer))
    total = half[rows(xy * plane, plane), :].astype(F32)
    for d, copy in enumerate(copies):
        copy.wait()
        total += got2[d].astype(F32)
    sums[...] = total

    copies = []
    for d, peer in enumerate(in_column):
        to = lax.rem(z + d + 1, nz)
        copies.append(start(sums.at[rows(to * piece, piece)], got3.at[d], s3.at[d], r3.at[d], peer))
    total = sums[rows(z * piece, piece), :]
    for d, copy in enumerate(copies):
        copy.wait()
        total += got3[d]
    base = n * halves + xy * plane
    own = rows(base + z * piece, piece)
    whole[own, :] = total.astype(BF16)

    copies = [start(whole.at[own], whole.at[own], s4.at[d], r4.at[d], peer) for d, peer in enumerate(in_column)]
    for copy in copies:
        copy.wait()
    own = rows(base, plane)
    copies = [start(whole.at[own], whole.at[own], s5.at[d], r5.at[d], peer) for d, peer in enumerate(in_plane)]
    across = [start(whole.at[own], whole.at[own], s6.at[0], r6.at[0], partner)]
    for d, copy in enumerate(copies):
        copy.wait()
        origin = lax.rem(xy + nxy - d - 1, nxy)
        got = rows(n * halves + origin * plane, plane)
        across.append(start(whole.at[got], whole.at[got], s6.at[d + 1], r6.at[d + 1], partner))
    for copy in across:
        copy.wait()
    out[...] = whole[...]


VMEM_SPEC = pl.BlockSpec(memory_space=pltpu.VMEM)
SMEM_SPEC = pl.BlockSpec(memory_space=pltpu.SMEM)
ANY_SPEC = pl.BlockSpec(memory_space=pl.ANY)


def shape(dims, dtype):
    return jax.ShapeDtypeStruct(dims, dtype)


def local_call(body, outs, scratch, scalars, *args):
    specs = [SMEM_SPEC] * scalars + [VMEM_SPEC] * (len(args) - scalars)
    return pl.pallas_call(
        body,
        out_shape=outs,
        in_specs=specs,
        out_specs=[VMEM_SPEC] * len(outs),
        scratch_shapes=[pltpu.VMEM(dims, dtype) for dims, dtype in scratch],
        compiler_params=pltpu.CompilerParams(vmem_limit_bytes=VMEM_LIMIT),
    )(*args)


def exchange(n_wide, collective_id, near, back):
    dims = (3, 2, 2 * SHELL, L)
    near, back = pl.pallas_call(
        functools.partial(exchange_kernel, n_wide),
        out_shape=[shape(dims, BF16)] * 2,
        in_specs=[ANY_SPEC] * 2,
        out_specs=[ANY_SPEC] * 2,
        scratch_shapes=[pltpu.SemaphoreType.DMA((10,)), pltpu.SemaphoreType.DMA((3, 2, 2))],
        compiler_params=pltpu.CompilerParams(collective_id=collective_id, has_side_effects=True),
    )(near.reshape(dims), back.reshape(dims))
    return near.reshape(SLOTS, SHELL, L), back.reshape(SLOTS, SHELL, L)


def reduce_all(nz, nxy, packed):
    dma = pltpu.SemaphoreType.DMA
    halves, plane = ROWS // 2, ROWS // 2 // nxy
    return pl.pallas_call(
        functools.partial(reduce_kernel, nz, nxy),
        out_shape=shape((ROWS, L), BF16),
        in_specs=[VMEM_SPEC],
        out_specs=VMEM_SPEC,
        scratch_shapes=[
            pltpu.VMEM((halves, L), BF16),
            pltpu.VMEM((plane, L), F32),
            pltpu.VMEM((halves, L), F32),
            pltpu.VMEM((nxy - 1, plane, L), BF16),
            pltpu.VMEM((nz - 1, plane // nz, L), F32),
            pltpu.VMEM((ROWS, L), BF16),
            dma, dma,
            dma((nxy - 1,)), dma((nxy - 1,)),
            dma((nz - 1,)), dma((nz - 1,)),
            dma((nz - 1,)), dma((nz - 1,)),
            dma((nxy - 1,)), dma((nxy - 1,)),
            dma((nxy,)), dma((nxy,)),
        ],
        compiler_params=pltpu.CompilerParams(
            collective_id=2, has_side_effects=True, vmem_limit_bytes=VMEM_LIMIT
        ),
    )(packed)


BLOCK = (8, 8, 8, L)
SHELLS = shape((SLOTS, SHELL, L), BF16)
OWN = shape((B, V, L), F32)
ROWS16 = shape((B, V, L), BF16)
TABLE = ((EMPTY + 1,) + BLOCK, F32)
GRADS = ((EMPTY + 1,) + BLOCK, F32)
OWN_GRADS = ((B + 1,) + BLOCK, F32)
PADDED = ((B, 12, 12, 8, L), F32)
AROUND = ((800, 9 * L), BF16)
BACK = ((9 * L, 3 * L), BF16)
SHIFTED = ((3, 10, 10, 8, L), F32)
COLUMNS = ((B * V, 27 * L), BF16)
SIDE = ((L, 27 * L), BF16)
SHELL32 = ((SHELL // 8, 8, L), F32)
BOTH = ((B, SHELL, L), BF16)
LEFT = ((L, B * V), BF16)


def local(nz, nxy, features, occupancy, conv1_weight, conv2_weight, out_grad, slots, send_blocks):
    n_wide = nz * nxy
    plan = send_blocks.reshape(SLOTS)
    active, mask, send_active, send_grads, own = local_call(
        first_kernel,
        [ROWS16, ROWS16, SHELLS, SHELLS, OWN],
        [((B,) + BLOCK, F32), PADDED, AROUND, BACK, GRADS, SHELL32, BOTH],
        2, slots, plan, features, occupancy, out_grad, conv2_weight,
    )
    halo, arrived = exchange(n_wide, 0, send_active, send_grads)
    hidden, send_hidden, send_grads, own, sums = local_call(
        second_kernel,
        [ROWS16, SHELLS, SHELLS, OWN, shape((WG, L), F32)],
        [TABLE, SHIFTED, COLUMNS, SIDE, PADDED, AROUND, BACK, GRADS, SHELL32, BOTH, LEFT],
        2, slots, plan, active, mask, halo, own, arrived, conv1_weight,
    )
    halo, arrived = exchange(n_wide, 1, send_hidden, send_grads)
    output, feature_grad, packed = local_call(
        third_kernel,
        [shape((B, C, V), BF16), shape((B, C, V), BF16), shape((ROWS, L), F32)],
        [TABLE, SHIFTED, COLUMNS, SIDE, OWN_GRADS, LEFT, ((2 * WG, L), F32)],
        2, slots, plan, hidden, halo, own, arrived, features, occupancy, out_grad, conv2_weight, sums,
    )
    packed = reduce_all(nz, nxy, packed)
    scale = (B * V * 2 * n_wide) ** -0.5
    first, second = local_call(
        functools.partial(last_kernel, scale),
        [shape((27, C, C), F32)] * 2, [], 0, packed,
    )
    return output, feature_grad, first, second


def solution(mesh):
    both = ("wide", "narrow")
    n_wide = mesh.shape["wide"]
    nxy = 16 if n_wide % 16 == 0 else n_wide // 2
    return jax.shard_map(
        functools.partial(local, n_wide // nxy, nxy),
        mesh=mesh,
        in_specs=(P(both, None, None), P(both, None), P(), P(), P(both, None, None), P(both, None),
                  P(both, None, None, None)),
        out_specs=(P(both, None, None), P(both, None, None), P(), P()),
        check_vma=False,
    )
```

```python
import functools

import jax
import jax.numpy as jnp
from jax import lax
from jax.experimental import pallas as pl
from jax.experimental.pallas import tpu as pltpu
from jax.sharding import PartitionSpec as P

MESH = pl.DeviceIdType.MESH
F32 = jnp.float32
BF16 = jnp.bfloat16
C = 96
L = 128
V = 512
B = 2
SLOTS = 12
EMPTY = 14
SHELL = 320
OFFSETS = [(a, b, e) for a in (-1, 0, 1) for b in (-1, 0, 1) for e in (-1, 0, 1)]
PAIRS = [(a, b) for a in (-1, 0, 1) for b in (-1, 0, 1)]
PLACE = {-1: slice(0, 1), 0: slice(1, 9), 1: slice(9, 10)}
LAYER = {-1: slice(7, 8), 0: slice(0, 8), 1: slice(0, 1)}
ROWS = 2048
WG = 27 * C
QUARTER = WG // 4
MESSAGE = 2 * SHELL + 16
VMEM_LIMIT = 56 * 1024 * 1024


def direction(a, b, e):
    return 9 * (a + 1) + 3 * (b + 1) + e + 1


def depth_index(shape):
    return lax.broadcasted_iota(jnp.int32, shape, len(shape) - 2)


def roll_depth(value, shift):
    return pltpu.roll(value, shift % 8, value.ndim - 2)


def to_rows(value):
    wide = jnp.concatenate([value, jnp.zeros((L - C, V), F32)], axis=0)
    return wide.T


def pack_shell(table, entry, shell, once):
    shell[0:8] = table[entry, 0]
    shell[8:16] = table[entry, 7]
    shell[16:22] = table[entry, 1:7, 0]
    shell[22:28] = table[entry, 1:7, 7]
    for at, z in ((28, 0), (34, 7)):
        plane = table[entry, 1:7, :, z, :]
        if once:
            y = depth_index(plane.shape)
            plane = jnp.where((y > 0) & (y < 7), plane, 0.0)
        shell[at : at + 6] = plane
    return shell[...]


def unpack_shell(shell, table, entry):
    table[entry, 0] = shell[0:8]
    table[entry, 7] = shell[8:16]
    table[entry, 1:7, 0] = shell[16:22]
    table[entry, 1:7, 7] = shell[22:28]
    table[entry, 1:7, :, 0, :] = shell[28:34]
    table[entry, 1:7, :, 7, :] = shell[34:40]


def add_shell(rows, table, entry):
    shell = rows.astype(F32).reshape(SHELL // 8, 8, L)
    table[entry, 0] += shell[0:8]
    table[entry, 7] += shell[8:16]
    table[entry, 1:7, 0] += shell[16:22]
    table[entry, 1:7, 7] += shell[22:28]
    table[entry, 1:7, :, 0, :] += shell[28:34]
    table[entry, 1:7, :, 7, :] += shell[34:40]


def pack_own(table, shell, out):
    for t in range(B):
        out[t * SHELL : (t + 1) * SHELL] = pack_shell(table, t, shell, False).reshape(SHELL, L).astype(BF16)


def pack_gradients(grads, shell, out):
    def one(j, carry):
        out[j] = pack_shell(grads, B + j, shell, True).reshape(SHELL, L).astype(BF16)
        return carry

    lax.fori_loop(0, SLOTS, one, 0)


def gather_gradients(grads, chosen, shell, out):
    def one(source, carry):
        sums = [0.0, 0.0]
        for c in range(2):
            slot = 2 * source + c
            part = pack_shell(grads, B + slot, shell, True)
            sums = [total + jnp.where(chosen[slot] == float(t), part, 0.0) for t, total in enumerate(sums)]
        for t in range(B):
            out[source, t * SHELL : (t + 1) * SHELL] = sums[t].reshape(SHELL, L).astype(BF16)
        return carry

    lax.fori_loop(0, SLOTS // 2, one, 0)


def own_entries(table, own):
    for t in range(B):
        table[t] = own[t].astype(F32).reshape(8, 8, 8, L)
    table[EMPTY] = jnp.zeros((8, 8, 8, L), F32)


def halo_entries(table, halo, chosen, sources):
    for source in sources:
        blocks = [halo[source, t * SHELL : (t + 1) * SHELL].astype(F32).reshape(SHELL // 8, 8, L) for t in range(B)]
        for c in range(2):
            slot = 2 * source + c
            unpack_shell(jnp.where(chosen[slot] == 0.0, blocks[0], blocks[1]), table, B + slot)


def build_columns(slots, table, shifted, columns):
    def one(t, carry):
        for a, b in PAIRS:
            def source(e):
                return table[slots[t, direction(a, b, e)], LAYER[a], LAYER[b]]

            here = source(0)
            z = depth_index(here.shape)
            shifted[1, PLACE[a], PLACE[b]] = here
            shifted[0, PLACE[a], PLACE[b]] = roll_depth(jnp.where(z == 7, source(-1), here), 1)
            shifted[2, PLACE[a], PLACE[b]] = roll_depth(jnp.where(z == 0, source(1), here), -1)
        rows = pl.ds(pl.multiple_of(t * V, V), V)
        for o, (a, b, e) in enumerate(OFFSETS):
            part = shifted[e + 1, a + 1 : a + 9, b + 1 : b + 9]
            columns[rows, o * L : (o + 1) * L] = part.reshape(V, L).astype(BF16)
        return carry

    lax.fori_loop(0, B, one, 0)


def side_weights(weights, side):
    side[...] = jnp.zeros_like(side)
    for o in range(27):
        side[0:C, o * L : o * L + C] = weights[o]


def back_weights(weights, back):
    back[...] = jnp.zeros_like(back)
    for o in range(27):
        k, e = o // 3, o % 3
        back[k * L : k * L + C, e * L : e * L + C] = weights[o]


def spread(slots, padded, around, back, grads):
    grads[...] = jnp.zeros_like(grads)

    def one(t, carry):
        for k, (a, b) in enumerate(PAIRS):
            part = padded[t, 1 - a : 11 - a, 1 - b : 11 - b]
            around[:, k * L : (k + 1) * L] = part.reshape(800, L).astype(BF16)
        by_depth = jnp.dot(around[...], back[...], preferred_element_type=F32).reshape(10, 10, 8, 3 * L)
        low = roll_depth(by_depth[..., 0:L], -1)
        high = roll_depth(by_depth[..., 2 * L : 3 * L], 1)
        z = depth_index(low.shape)
        parts = {
            -1: jnp.where(z == 7, low, 0.0),
            0: by_depth[..., L : 2 * L] + jnp.where(z != 0, high, 0.0) + jnp.where(z != 7, low, 0.0),
            1: jnp.where(z == 0, high, 0.0),
        }
        for a, b, e in OFFSETS:
            entry = slots[t, direction(a, b, e)]
            grads[entry, LAYER[a], LAYER[b]] += parts[e][PLACE[a], PLACE[b]]
        return carry

    lax.fori_loop(0, B, one, 0)


def first_kernel(slots, plan, features, occupancy, out_grad, weights,
                 active, mask, messages, send_grads, own_grads,
                 table, padded, around, back, grads, shell):
    padded[...] = jnp.zeros_like(padded)
    for t in range(B):
        seen = occupancy[t : t + 1, :].astype(F32)
        rows = to_rows(features[t].astype(F32) * seen)
        active[t] = rows.astype(BF16)
        table[t] = rows.reshape(8, 8, 8, L)
        mask[t] = jnp.broadcast_to(seen, (L, V)).T.astype(BF16)
        padded[t, 2:10, 2:10] = to_rows(out_grad[t].astype(F32) * seen).reshape(8, 8, 8, L)
    row = lax.broadcasted_iota(jnp.int32, (16, L), 0)
    pack_own(table, shell, messages.at[0])
    for g in range(3):
        if g > 0:
            messages[g, 0 : 2 * SHELL] = messages[0, 0 : 2 * SHELL]
        rows = jnp.zeros((16, L), F32)
        for i in range(4):
            rows = jnp.where(row == i, plan[4 * g + i].astype(F32), rows)
        messages[g, 2 * SHELL : MESSAGE] = rows.astype(BF16)
    back_weights(weights, back)
    spread(slots, padded, around, back, grads)
    pack_gradients(grads, shell, send_grads)
    for t in range(B):
        own_grads[t] = grads[t].reshape(V, L)


def second_kernel(slots, plan, active, mask, halo, own_grads, arrived, weights,
                  hidden, send_hidden, send_grads, own_out, packed, chosen,
                  table, shifted, columns, side, padded, around, back, grads, shell, pre, sums):
    n = lax.axis_index("narrow")
    for source in range(SLOTS // 2):
        rows = halo[source, 2 * SHELL : MESSAGE].astype(F32)
        for c in range(2):
            row = jnp.where(n == 0, rows[c : c + 1], rows[2 + c : 3 + c])
            chosen[2 * source + c] = jnp.broadcast_to(row, (8, L))
    own_entries(table, active)
    halo_entries(table, halo, chosen, range(SLOTS // 2))
    build_columns(slots, table, shifted, columns)
    side_weights(weights, side)
    for t in range(B):
        grads[t] = own_grads[t].reshape(8, 8, 8, L)

    def give(j, carry):
        add_shell(arrived[j], grads, plan[j])
        return carry

    lax.fori_loop(0, SLOTS, give, 0)
    padded[...] = jnp.zeros_like(padded)
    for t in range(B):
        value = lax.dot_general(
            columns[t * V : (t + 1) * V, :], side[...], (((1,), (1,)), ((), ())), preferred_element_type=F32
        )
        seen = mask[t].astype(F32)
        gate = jax.nn.sigmoid(value)
        out = (value * gate * seen).astype(BF16)
        hidden[t] = out
        table[t] = out.astype(F32).reshape(8, 8, 8, L)
        grad = grads[t].reshape(V, L) * seen * gate * (1.0 + value * (1.0 - gate))
        padded[t, 2:10, 2:10] = grad.reshape(8, 8, 8, L)
        pre[:, t * V : (t + 1) * V] = grad.T.astype(BF16)
    pack_own(table, shell, send_hidden)
    back_weights(weights, back)
    spread(slots, padded, around, back, grads)
    gather_gradients(grads, chosen, shell, send_grads)
    for t in range(B):
        own_out[t] = grads[t].reshape(V, L)
    weight_sums(pre, columns, sums)
    pack_sums(sums, packed)


def weight_sums(left, columns, out):
    for o in range(0, 27, 3):
        sums = jnp.dot(left[...], columns[:, o * L : (o + 3) * L], preferred_element_type=F32)
        for i in range(3):
            row = (o + i) * C
            out[row : row + C] = sums[0:C, i * L : (i + 1) * L]


def pack_sums(sums, packed):
    last = sums[3 * QUARTER : WG]
    lane = lax.broadcasted_iota(jnp.int32, (QUARTER, L), 1)
    for i in range(3):
        moved = pltpu.roll(last, C - 32 * i, 1)
        rows = slice(i * QUARTER, (i + 1) * QUARTER)
        packed[rows] = jnp.where(lane < C, sums[rows], moved)
    packed[3 * QUARTER : ROWS] = jnp.zeros((ROWS - 3 * QUARTER, L), F32)


def last_kernel(scale, packed, first, second):
    lane = lax.broadcasted_iota(jnp.int32, (QUARTER, L), 1)
    for at, out in ((0, first), (ROWS, second)):
        whole = packed[at : at + ROWS].astype(F32) * scale
        last = jnp.zeros((QUARTER, L), F32)
        for i in range(3):
            part = whole[i * QUARTER : (i + 1) * QUARTER]
            last = jnp.where(lane // 32 == i, pltpu.roll(part, 32 + 32 * i, 1), last)
        for r in range(0, WG, 24):
            rows = whole[r : r + 24] if r < 3 * QUARTER else last[r - 3 * QUARTER : r - 3 * QUARTER + 24]
            out[r // C, r % C : r % C + 24, :] = rows[:, 0:C]


def send(source, dest, sems, peer):
    copy = pltpu.make_async_remote_copy(
        src_ref=source, dst_ref=dest, send_sem=sems[0], recv_sem=sems[1], device_id=peer, device_id_type=MESH
    )
    copy.start()
    return copy


def meet(peers):
    barrier = pltpu.get_barrier_semaphore()
    for peer in peers:
        pl.semaphore_signal(barrier, inc=1, device_id=peer, device_id_type=MESH)
    pl.semaphore_wait(barrier, len(peers))


def neighbours(n_wide):
    w, n = lax.axis_index("wide"), lax.axis_index("narrow")
    ahead, behind = lax.rem(w + 1, n_wide), lax.rem(w + n_wide - 1, n_wide)
    return w, n, ahead, behind


def exchange_kernel(n_wide, messages, send_back, near, returned, near_sems, across_sems, back_sems):
    w, n, ahead, behind = neighbours(n_wide)
    partner = (w, 1 - n)
    meet([(behind, 0), (behind, 1), (ahead, 0), (ahead, 1), partner])
    nears = [
        send(messages.at[g], near.at[g, n], (near_sems.at[0, g], near_sems.at[1, g]), peer)
        for g, peer in enumerate([(behind, n), partner, (ahead, n)])
    ]
    backs = []
    for k, (g, to, m) in enumerate([(2, behind, n), (2, behind, 1 - n), (0, ahead, n), (0, ahead, 1 - n), (1, w, 1 - n)]):
        sems = (back_sems.at[0, k], back_sems.at[1, k])
        backs.append(send(send_back.at[g, m], returned.at[g, n], sems, (to, m)))
    across = []
    for g in (0, 2):
        nears[g].wait()
        sems = (across_sems.at[0, g], across_sems.at[1, g])
        across.append(send(near.at[g, n], near.at[g, n], sems, partner))
    nears[1].wait()
    for copy in across + backs:
        copy.wait()


class Sum:
    def __init__(self, nz, nxy, src, whole, at, scratch):
        self.nz, self.nxy, self.src, self.whole, self.at = nz, nxy, src, whole, at
        (self.half, self.sums, self.fixed, self.got1, self.got2, self.got3,
         self.sem1, self.sem2, self.sem3, self.sem4, self.sem5, self.sem6) = scratch
        w, self.n = lax.axis_index("wide"), lax.axis_index("narrow")
        self.z, self.xy = w // nxy, lax.rem(w, nxy)
        self.halves, self.plane = ROWS // 2, ROWS // 2 // nxy
        self.piece = self.plane // nz
        self.partner = (w, 1 - self.n)
        self.in_plane = [(self.z * nxy + lax.rem(self.xy + d, nxy), self.n) for d in range(1, nxy)]
        self.in_column = [(lax.rem(self.z + d, nz) * nxy + self.xy, self.n) for d in range(1, nz)]

    def peers(self):
        return [self.partner] + self.in_plane + self.in_column

    def rows(self, at, size):
        return pl.ds(pl.multiple_of(at, size), size)

    def pair(self, sems, d):
        return sems.at[0, d], sems.at[1, d]

    def cores(self):
        theirs = self.src.at[self.rows((1 - self.n) * self.halves, self.halves)]
        self.copies = [send(theirs, self.got1, self.pair(self.sem1, 0), self.partner)]

    def wait(self):
        for copy in self.copies:
            copy.wait()

    def planes(self):
        self.wait()
        mine = self.src[self.rows(self.n * self.halves, self.halves), :]
        self.half[...] = (mine + self.got1[...]).astype(BF16)
        self.copies = []
        for d, peer in enumerate(self.in_plane):
            to = lax.rem(self.xy + d + 1, self.nxy)
            part = self.half.at[self.rows(to * self.plane, self.plane)]
            self.copies.append(send(part, self.got2.at[d], self.pair(self.sem2, d), peer))

    def columns(self):
        self.wait()
        total = self.half[self.rows(self.xy * self.plane, self.plane), :].astype(F32)
        for d in range(self.nxy - 1):
            total += self.got2[d].astype(F32)
        self.sums[...] = total
        self.copies = []
        for d, peer in enumerate(self.in_column):
            to = lax.rem(self.z + d + 1, self.nz)
            part = self.sums.at[self.rows(to * self.piece, self.piece)]
            self.copies.append(send(part, self.got3.at[d], self.pair(self.sem3, d), peer))

    def columns_back(self):
        self.wait()
        own = self.rows(self.z * self.piece, self.piece)
        total = self.sums[own, :]
        for d in range(self.nz - 1):
            total += self.got3[d]
        self.fixed[own, :] = total
        self.copies = [
            send(self.fixed.at[own], self.fixed.at[own], self.pair(self.sem4, d), peer)
            for d, peer in enumerate(self.in_column)
        ]

    def planes_back(self):
        self.wait()
        own = self.rows(self.at + self.n * self.halves + self.xy * self.plane, self.plane)
        self.whole[own, :] = self.fixed[...].astype(BF16)
        self.copies = [
            send(self.whole.at[own], self.whole.at[own], self.pair(self.sem5, d), peer)
            for d, peer in enumerate(self.in_plane)
        ]
        self.across = [send(self.whole.at[own], self.whole.at[own], self.pair(self.sem6, self.nxy - 1), self.partner)]

    def cores_back(self):
        for d, copy in enumerate(self.copies):
            copy.wait()
            origin = lax.rem(self.xy + self.nxy - d - 1, self.nxy)
            got = self.rows(self.at + self.n * self.halves + origin * self.plane, self.plane)
            self.across.append(send(self.whole.at[got], self.whole.at[got], self.pair(self.sem6, d), self.partner))

    def end(self):
        for copy in self.across:
            copy.wait()


def sum_scratch(nz, nxy):
    halves, plane = ROWS // 2, ROWS // 2 // nxy
    sems = [pltpu.SemaphoreType.DMA((2, count)) for count in (1, nxy - 1, nz - 1, nz - 1, nxy - 1, nxy)]
    return [
        pltpu.VMEM((halves, L), BF16),
        pltpu.VMEM((plane, L), F32),
        pltpu.VMEM((plane, L), F32),
        pltpu.VMEM((halves, L), F32),
        pltpu.VMEM((nxy - 1, plane, L), BF16),
        pltpu.VMEM((nz - 1, plane // nz, L), F32),
    ] + sems


def third_kernel(nz, nxy, slots, hidden, shells, own_grads, send_grads, features, occupancy, out_grad, weights,
                 first_packed, chosen,
                 output, feature_grad, reduced,
                 table, shifted, columns, side, grads, masked, sums, second_packed, halo, halo_grads, joined, arrived,
                 whole, halo_sems, across_sems, core_sems, back_sems, *scratch):
    n_wide = nz * nxy
    w, n, ahead, behind = neighbours(n_wide)
    partner = (w, 1 - n)
    first = Sum(nz, nxy, first_packed, whole, 0, scratch[: len(scratch) // 2])
    second = Sum(nz, nxy, second_packed, whole, ROWS, scratch[len(scratch) // 2 :])
    meet([(behind, n), (ahead, n)] + first.peers())

    def pair(sems, i):
        return sems.at[0, i], sems.at[1, i]

    nears = [
        send(shells, halo.at[g, n], pair(halo_sems, g), peer)
        for g, peer in enumerate([(behind, n), partner, (ahead, n)])
    ]
    joins = [send(send_grads.at[g, 1 - n], halo_grads.at[i], pair(core_sems, i), partner) for i, g in enumerate((0, 2))]
    backs = [send(send_grads.at[1, 1 - n], arrived.at[1], pair(back_sems, 1), partner)]
    first.cores()
    for i, g in enumerate((0, 2)):
        joins[i].wait()
        joined[i] = (send_grads[g, n].astype(F32) + halo_grads[i].astype(F32)).astype(BF16)
        backs.append(send(joined.at[i], arrived.at[g], pair(back_sems, g), ((ahead, n), (behind, n))[i]))
    first.planes()
    own_entries(table, hidden)
    side_weights(weights, side)
    for t in range(B):
        seen = occupancy[t : t + 1, :].astype(F32)
        masked[0:C, t * V : (t + 1) * V] = (out_grad[t].astype(F32) * seen).astype(BF16)
        grads[t] = own_grads[t].reshape(8, 8, 8, L)
    masked[C:L] = jnp.zeros((L - C, B * V), BF16)
    across = []
    for i, g in enumerate((0, 2)):
        nears[g].wait()
        across.append(send(halo.at[g, n], halo.at[g, n], pair(across_sems, i), partner))
    nears[1].wait()
    for copy in across:
        copy.wait()
    flat = halo.reshape(SLOTS // 2, 2 * SHELL, L)
    halo_entries(table, flat, chosen, range(SLOTS // 2))
    build_columns(slots, table, shifted, columns)
    first.columns()
    weight_sums(masked, columns, sums)
    pack_sums(sums, second_packed)
    second.cores()
    first.columns_back()
    second.planes()

    def forward(t):
        seen = occupancy[t : t + 1, :].astype(F32)
        value = lax.dot_general(
            side[...], columns[t * V : (t + 1) * V, :], (((1,), (1,)), ((), ())), preferred_element_type=F32
        )
        output[t] = ((features[t].astype(F32) * seen + value[0:C]) * seen).astype(BF16)

    forward(0)
    first.planes_back()
    forward(1)
    second.columns()
    for copy in backs:
        copy.wait()
    for t in range(B):
        for g in range(3):
            add_shell(arrived[g, t * SHELL : (t + 1) * SHELL], grads, t)
        seen = occupancy[t : t + 1, :].astype(F32)
        back = grads[t].reshape(V, L).T
        feature_grad[t] = ((out_grad[t].astype(F32) * seen + back[0:C]) * seen).astype(BF16)
    second.columns_back()
    first.cores_back()
    second.planes_back()
    first.end()
    second.cores_back()
    second.end()
    reduced[...] = whole[...]


VMEM_SPEC = pl.BlockSpec(memory_space=pltpu.VMEM)
SMEM_SPEC = pl.BlockSpec(memory_space=pltpu.SMEM)
ANY_SPEC = pl.BlockSpec(memory_space=pl.ANY)


def shape(dims, dtype):
    return jax.ShapeDtypeStruct(dims, dtype)


def local_call(body, outs, scratch, scalars, *args):
    specs = [SMEM_SPEC] * scalars + [VMEM_SPEC] * (len(args) - scalars)
    return pl.pallas_call(
        body,
        out_shape=outs,
        in_specs=specs,
        out_specs=[VMEM_SPEC] * len(outs),
        scratch_shapes=[pltpu.VMEM(dims, dtype) for dims, dtype in scratch],
        compiler_params=pltpu.CompilerParams(vmem_limit_bytes=VMEM_LIMIT),
    )(*args)


def exchange(n_wide, messages, back):
    dma = pltpu.SemaphoreType.DMA
    return pl.pallas_call(
        functools.partial(exchange_kernel, n_wide),
        out_shape=[shape((3, 2, MESSAGE, L), BF16), shape((3, 2, 2 * SHELL, L), BF16)],
        in_specs=[ANY_SPEC] * 2,
        out_specs=[ANY_SPEC] * 2,
        scratch_shapes=[dma((2, 3)), dma((2, 3)), dma((2, 5))],
        compiler_params=pltpu.CompilerParams(collective_id=0, has_side_effects=True),
    )(messages, back.reshape(3, 2, 2 * SHELL, L))


BLOCK = (8, 8, 8, L)
SHELLS = shape((SLOTS, SHELL, L), BF16)
OWN = shape((B, V, L), F32)
ROWS16 = shape((B, V, L), BF16)
TABLE = ((EMPTY + 1,) + BLOCK, F32)
GRADS = ((EMPTY + 1,) + BLOCK, F32)
OWN_GRADS = ((B + 1,) + BLOCK, F32)
PADDED = ((B, 12, 12, 8, L), F32)
AROUND = ((800, 9 * L), BF16)
BACK = ((9 * L, 3 * L), BF16)
SHIFTED = ((3, 10, 10, 8, L), F32)
COLUMNS = ((B * V, 27 * L), BF16)
SIDE = ((L, 27 * L), BF16)
SHELL32 = ((SHELL // 8, 8, L), F32)
SUMS = ((WG, L), F32)
LEFT = ((L, B * V), BF16)


def local(nz, nxy, features, occupancy, conv1_weight, conv2_weight, out_grad, slots, send_blocks):
    n_wide = nz * nxy
    dma = pltpu.SemaphoreType.DMA
    plan = send_blocks.reshape(SLOTS)
    active, mask, messages, send_grads, own = local_call(
        first_kernel,
        [ROWS16, ROWS16, shape((3, MESSAGE, L), BF16), SHELLS, OWN],
        [((B,) + BLOCK, F32), PADDED, AROUND, BACK, GRADS, SHELL32],
        2, slots, plan, features, occupancy, out_grad, conv2_weight,
    )
    halo, arrived = exchange(n_wide, messages, send_grads)
    hidden, shells, send_grads, own, packed, chosen = local_call(
        second_kernel,
        [ROWS16, shape((2 * SHELL, L), BF16), shape((SLOTS // 2, 2 * SHELL, L), BF16), OWN, shape((ROWS, L), F32),
         shape((SLOTS, 8, L), F32)],
        [TABLE, SHIFTED, COLUMNS, SIDE, PADDED, AROUND, BACK, GRADS, SHELL32, LEFT, SUMS],
        2, slots, plan, active, mask, halo.reshape(SLOTS // 2, MESSAGE, L), own, arrived.reshape(SLOTS, SHELL, L),
        conv1_weight,
    )
    scratch = [TABLE, SHIFTED, COLUMNS, SIDE, ((B,) + BLOCK, F32), LEFT, SUMS, ((ROWS, L), F32),
               ((3, 2, 2 * SHELL, L), BF16), ((2, 2 * SHELL, L), BF16), ((2, 2 * SHELL, L), BF16),
               ((3, 2 * SHELL, L), BF16), ((2 * ROWS, L), BF16)]
    output, feature_grad, reduced = pl.pallas_call(
        functools.partial(third_kernel, nz, nxy),
        out_shape=[shape((B, C, V), BF16), shape((B, C, V), BF16), shape((2 * ROWS, L), BF16)],
        in_specs=[SMEM_SPEC] + [VMEM_SPEC] * 10,
        out_specs=[VMEM_SPEC] * 3,
        scratch_shapes=[pltpu.VMEM(dims, dtype) for dims, dtype in scratch]
        + [dma((2, 3)), dma((2, 2)), dma((2, 2)), dma((2, 3))] + 2 * sum_scratch(nz, nxy),
        compiler_params=pltpu.CompilerParams(
            collective_id=1, has_side_effects=True, vmem_limit_bytes=VMEM_LIMIT
        ),
    )(slots, hidden, shells, own, send_grads.reshape(3, 2, 2 * SHELL, L), features, occupancy, out_grad, conv2_weight,
      packed, chosen)
    scale = (B * V * 2 * n_wide) ** -0.5
    first, second = local_call(
        functools.partial(last_kernel, scale),
        [shape((27, C, C), F32)] * 2, [], 0, reduced,
    )
    return output, feature_grad, first, second


def solution(mesh):
    both = ("wide", "narrow")
    n_wide = mesh.shape["wide"]
    nxy = 16 if n_wide % 16 == 0 else n_wide // 2
    return jax.shard_map(
        functools.partial(local, n_wide // nxy, nxy),
        mesh=mesh,
        in_specs=(P(both, None, None), P(both, None), P(), P(), P(both, None, None), P(both, None),
                  P(both, None, None, None)),
        out_specs=(P(both, None, None), P(both, None, None), P(), P()),
        check_vma=False,
    )
```

```python
import functools

import jax
import jax.numpy as jnp
from jax import lax
from jax.experimental import pallas as pl
from jax.experimental.pallas import tpu as pltpu
from jax.sharding import PartitionSpec as P

MESH = pl.DeviceIdType.MESH
F32 = jnp.float32
BF16 = jnp.bfloat16
C = 96
L = 128
V = 512
B = 2
SLOTS = 12
EMPTY = 14
SHELL = 320
OFFSETS = [(a, b, e) for a in (-1, 0, 1) for b in (-1, 0, 1) for e in (-1, 0, 1)]
PAIRS = [(a, b) for a in (-1, 0, 1) for b in (-1, 0, 1)]
PLACE = {-1: slice(0, 1), 0: slice(1, 9), 1: slice(9, 10)}
LAYER = {-1: slice(7, 8), 0: slice(0, 8), 1: slice(0, 1)}
HALF = 1024
ROWS = 2 * HALF
WG = 27 * C
QUARTER = WG // 4
MESSAGE = 2 * SHELL + 16
FACES = 384
VMEM_LIMIT = 56 * 1024 * 1024


def direction(a, b, e):
    return 9 * (a + 1) + 3 * (b + 1) + e + 1


def depth_index(shape):
    return lax.broadcasted_iota(jnp.int32, shape, len(shape) - 2)


def roll_depth(value, shift):
    return pltpu.roll(value, shift % 8, value.ndim - 2)


def to_rows(value):
    wide = jnp.concatenate([value, jnp.zeros((L - C, V), F32)], axis=0)
    return wide.T


def pack_shell(table, entry, shell):
    shell[0:8] = table[entry, 0]
    shell[8:16] = table[entry, 7]
    shell[16:22] = table[entry, 1:7, 0]
    shell[22:28] = table[entry, 1:7, 7]
    for at, z in ((28, 0), (34, 7)):
        shell[at : at + 6] = table[entry, 1:7, :, z, :]
    return shell[...].reshape(SHELL, L).astype(BF16)


def unpack_shell(shell, table, entry):
    table[entry, 0] = shell[0:8]
    table[entry, 7] = shell[8:16]
    table[entry, 1:7, 0] = shell[16:22]
    table[entry, 1:7, 7] = shell[22:28]
    table[entry, 1:7, :, 0, :] = shell[28:34]
    table[entry, 1:7, :, 7, :] = shell[34:40]


def add_faces(faces, grads, t):
    grads[t, 0] += faces[0:8]
    grads[t, 7] += faces[8:16]
    grads[t, :, 0] += faces[16:24]
    grads[t, :, 7] += faces[24:32]
    grads[t, :, :, 0, :] += faces[32:40]
    grads[t, :, :, 7, :] += faces[40:48]


def pack_own(table, shell, out):
    for t in range(B):
        out[t * SHELL : (t + 1) * SHELL] = pack_shell(table, t, shell)


def gather_gradients(faces, chosen, out):
    for g in range(3):
        for m in range(2):
            for t in range(B):
                total = 0.0
                for c in range(2):
                    slot = 4 * g + 2 * m + c
                    total += jnp.where(chosen[slot] == float(t), faces[B + slot], 0.0)
                out[g, m, t * FACES : (t + 1) * FACES] = total.reshape(FACES, L).astype(BF16)


def halo_entries(table, halo, chosen):
    for source in range(SLOTS // 2):
        blocks = [halo[source // 2, source % 2, t * SHELL : (t + 1) * SHELL].astype(F32).reshape(SHELL // 8, 8, L) for t in range(B)]
        for c in range(2):
            slot = 2 * source + c
            unpack_shell(jnp.where(chosen[slot] == 0.0, blocks[0], blocks[1]), table, B + slot)


def build_columns(slots, table, shifted, columns):
    def one(t, carry):
        for a, b in PAIRS:
            def source(e):
                return table[slots[t, direction(a, b, e)], LAYER[a], LAYER[b]]

            here = source(0)
            z = depth_index(here.shape)
            shifted[1, PLACE[a], PLACE[b]] = here
            shifted[0, PLACE[a], PLACE[b]] = roll_depth(jnp.where(z == 7, source(-1), here), 1)
            shifted[2, PLACE[a], PLACE[b]] = roll_depth(jnp.where(z == 0, source(1), here), -1)
        rows = pl.ds(pl.multiple_of(t * V, V), V)
        for o, (a, b, e) in enumerate(OFFSETS):
            part = shifted[e + 1, a + 1 : a + 9, b + 1 : b + 9]
            columns[rows, o * L : (o + 1) * L] = part.reshape(V, L).astype(BF16)
        return carry

    lax.fori_loop(0, B, one, 0)


def side_weights(weights, side):
    side[...] = jnp.zeros_like(side)
    for o in range(27):
        side[0:C, o * L : o * L + C] = weights[o]


def back_weights(weights, back):
    back[...] = jnp.zeros_like(back)
    for o in range(27):
        k, e = o // 3, o % 3
        back[k * L : k * L + C, e * L : e * L + C] = weights[o]


def spread(t, padded, around, back, middle, low, high, planes, edges):
    for k, (a, b) in enumerate(PAIRS):
        part = padded[t, 1 - a : 11 - a, 1 - b : 11 - b]
        around[:, k * L : (k + 1) * L] = part.reshape(800, L).astype(BF16)
    by_depth = jnp.dot(around[...], back[...], preferred_element_type=F32).reshape(10, 10, 8, 3 * L)
    low[...] = by_depth[..., 0:L]
    high[...] = by_depth[..., 2 * L : 3 * L]
    down = roll_depth(low[...], -1)
    up = roll_depth(high[...], 1)
    z = depth_index(up.shape)
    middle[...] = by_depth[..., L : 2 * L] + jnp.where(z != 0, up, 0.0) + jnp.where(z != 7, down, 0.0)
    y = depth_index((10, 8, L))
    for i, (source, at) in enumerate(((low, 0), (high, 7))):
        planes[i] = source[:, 1:9, at, :]
        for j, (column, row) in enumerate(((0, 7), (9, 0))):
            edge = source[:, column, at : at + 1, :]
            edges[i, j] = jnp.where(y == row, edge, 0.0)


def scatter(t, slots, middle, planes, edges, faces):
    def one(entry, carry):
        def weight(a, b, e):
            return (slots[t, direction(a, b, e)] == entry).astype(F32)

        for x, (a, px) in ((0, (1, 9)), (8, (-1, 0))):
            faces[entry, x : x + 8] += weight(a, 0, 0) * middle[px, 1:9]
            faces[entry, x] += weight(a, 1, 0) * middle[px, 9]
            faces[entry, x + 7] += weight(a, -1, 0) * middle[px, 0]
        faces[entry, 16:24] += weight(0, 1, 0) * middle[1:9, 9]
        faces[entry, 24:32] += weight(0, -1, 0) * middle[1:9, 0]
        for at, e, i in ((32, 1, 1), (40, -1, 0)):
            for a, x, px in ((0, slice(at, at + 8), slice(1, 9)), (1, at, 9), (-1, at + 7, 0)):
                total = weight(a, 0, e) * planes[i, px]
                total += weight(a, -1, e) * edges[i, 0, px] + weight(a, 1, e) * edges[i, 1, px]
                faces[entry, x] += total
        return carry

    lax.fori_loop(0, EMPTY, one, 0)


def weight_sums(left, columns, out):
    for o in range(0, 27, 3):
        sums = jnp.dot(left[...], columns[:, o * L : (o + 3) * L], preferred_element_type=F32)
        for i in range(3):
            row = (o + i) * C
            out[row : row + C] = sums[0:C, i * L : (i + 1) * L]


def pack_sums(sums, packed, at):
    last = sums[3 * QUARTER : WG]
    lane = lax.broadcasted_iota(jnp.int32, (QUARTER, L), 1)
    for i in range(3):
        moved = pltpu.roll(last, C - 32 * i, 1)
        rows = slice(i * QUARTER, (i + 1) * QUARTER)
        packed[at + i * QUARTER : at + (i + 1) * QUARTER] = jnp.where(lane < C, sums[rows], moved)
    packed[at + 3 * QUARTER : at + ROWS] = jnp.zeros((ROWS - 3 * QUARTER, L), F32)


def last_kernel(scale, packed, output, grad, output_out, grad_out, first, second):
    output_out[...] = output[...]
    grad_out[...] = grad[...]
    lane = lax.broadcasted_iota(jnp.int32, (QUARTER, L), 1)
    for at, out in ((0, first), (HALF, second)):
        parts = [packed[ROWS * n + at : ROWS * n + at + HALF] for n in range(2)]
        whole = jnp.concatenate(parts, axis=0).astype(F32) * scale
        last = jnp.zeros((QUARTER, L), F32)
        for i in range(3):
            part = whole[i * QUARTER : (i + 1) * QUARTER]
            last = jnp.where(lane // 32 == i, pltpu.roll(part, 32 + 32 * i, 1), last)
        for r in range(0, WG, 24):
            rows = whole[r : r + 24] if r < 3 * QUARTER else last[r - 3 * QUARTER : r - 3 * QUARTER + 24]
            out[r // C, r % C : r % C + 24, :] = rows[:, 0:C]


def send(source, dest, sems, peer):
    copy = pltpu.make_async_remote_copy(
        src_ref=source, dst_ref=dest, send_sem=sems[0], recv_sem=sems[1], device_id=peer, device_id_type=MESH
    )
    copy.start()
    return copy


def greet(peers):
    barrier = pltpu.get_barrier_semaphore()
    for peer in peers:
        pl.semaphore_signal(barrier, inc=1, device_id=peer, device_id_type=MESH)


def neighbours(n_wide):
    w, n = lax.axis_index("wide"), lax.axis_index("narrow")
    ahead, behind = lax.rem(w + 1, n_wide), lax.rem(w + n_wide - 1, n_wide)
    return w, n, ahead, behind


class Shells:
    def __init__(self, n_wide, halo, sems):
        self.w, self.n, ahead, behind = neighbours(n_wide)
        self.partner = (self.w, 1 - self.n)
        self.peers = [(behind, self.n), self.partner, (ahead, self.n)]
        self.halo, self.sems = halo, sems

    def start(self, sources):
        self.copies = [
            send(sources[g], self.halo.at[g, self.n], (self.sems.at[0, g], self.sems.at[1, g]), self.peers[g])
            for g in range(3)
        ]

    def finish(self):
        across = []
        for g in (0, 2):
            self.copies[g].wait()
            got = self.halo.at[g, self.n]
            across.append(send(got, got, (self.sems.at[0, 3 + g], self.sems.at[1, 3 + g]), self.partner))
        self.copies[1].wait()
        for copy in across:
            copy.wait()


class Returns:
    def __init__(self, n_wide, out, got, joined, arrived, sems):
        self.w, self.n, ahead, behind = neighbours(n_wide)
        self.partner = (self.w, 1 - self.n)
        self.to = {0: (ahead, self.n), 2: (behind, self.n)}
        self.out, self.got, self.joined, self.arrived, self.sems = out, got, joined, arrived, sems

    def pair(self, i):
        return self.sems.at[0, i], self.sems.at[1, i]

    def start(self):
        self.joins = [
            send(self.out.at[g, 1 - self.n], self.got.at[i], self.pair(i), self.partner) for i, g in enumerate((0, 2))
        ]
        self.backs = [send(self.out.at[1, 1 - self.n], self.arrived.at[1], self.pair(2), self.partner)]

    def join(self):
        for i, g in enumerate((0, 2)):
            self.joins[i].wait()
            self.joined[i] = (self.out[g, self.n].astype(F32) + self.got[i].astype(F32)).astype(BF16)
            self.backs.append(send(self.joined.at[i], self.arrived.at[g], self.pair(3 + i), self.to[g]))

    def add(self, grads):
        for copy in self.backs:
            copy.wait()
        for t in range(B):
            for g in range(3):
                faces = self.arrived[g, t * FACES : (t + 1) * FACES].astype(F32)
                add_faces(faces.reshape(FACES // 8, 8, L), grads, t)


class Sum:
    def __init__(self, nz, nxy, src, whole, scratch):
        self.nz, self.nxy, self.src, self.whole = nz, nxy, src, whole
        (self.half, self.sums, self.fixed, self.got1, self.got2, self.got3,
         self.sem1, self.sem2, self.sem3, self.sem4, self.sem5, self.sem6) = scratch
        w, self.n = lax.axis_index("wide"), lax.axis_index("narrow")
        self.z, self.xy = w // nxy, lax.rem(w, nxy)
        self.plane = ROWS // nxy
        self.piece = self.plane // nz
        self.partner = (w, 1 - self.n)
        self.in_plane = [(self.z * nxy + lax.rem(self.xy + d, nxy), self.n) for d in range(1, nxy)]
        self.in_column = [(lax.rem(self.z + d, nz) * nxy + self.xy, self.n) for d in range(1, nz)]
        self.crossing = []

    def peers(self):
        return [self.partner] + self.in_plane + self.in_column

    def rows(self, at, size):
        return pl.ds(pl.multiple_of(at, size), size)

    def pair(self, sems, d):
        return sems.at[0, d], sems.at[1, d]

    def cores(self, i):
        theirs = self.src.at[self.rows(i * ROWS + (1 - self.n) * HALF, HALF)]
        self.crossing.append(send(theirs, self.got1.at[i], self.pair(self.sem1, i), self.partner))

    def wait(self):
        for copy in self.copies:
            copy.wait()

    def planes(self):
        for i, copy in enumerate(self.crossing):
            copy.wait()
            mine = self.src[self.rows(i * ROWS + self.n * HALF, HALF), :]
            self.half[i * HALF : (i + 1) * HALF] = (mine + self.got1[i]).astype(BF16)
        self.copies = []
        for d, peer in enumerate(self.in_plane):
            to = lax.rem(self.xy + d + 1, self.nxy)
            part = self.half.at[self.rows(to * self.plane, self.plane)]
            self.copies.append(send(part, self.got2.at[d], self.pair(self.sem2, d), peer))

    def columns(self):
        self.wait()
        total = self.half[self.rows(self.xy * self.plane, self.plane), :].astype(F32)
        for d in range(self.nxy - 1):
            total += self.got2[d].astype(F32)
        self.sums[...] = total
        self.copies = []
        for d, peer in enumerate(self.in_column):
            to = lax.rem(self.z + d + 1, self.nz)
            part = self.sums.at[self.rows(to * self.piece, self.piece)]
            self.copies.append(send(part, self.got3.at[d], self.pair(self.sem3, d), peer))

    def columns_back(self):
        self.wait()
        own = self.rows(self.z * self.piece, self.piece)
        total = self.sums[own, :]
        for d in range(self.nz - 1):
            total += self.got3[d]
        self.fixed[own, :] = total
        self.copies = [
            send(self.fixed.at[own], self.fixed.at[own], self.pair(self.sem4, d), peer)
            for d, peer in enumerate(self.in_column)
        ]

    def planes_back(self):
        self.wait()
        own = self.rows(self.n * ROWS + self.xy * self.plane, self.plane)
        self.whole[own, :] = self.fixed[...].astype(BF16)
        self.copies = [
            send(self.whole.at[own], self.whole.at[own], self.pair(self.sem5, d), peer)
            for d, peer in enumerate(self.in_plane)
        ]
        self.across = [send(self.whole.at[own], self.whole.at[own], self.pair(self.sem6, self.nxy - 1), self.partner)]

    def cores_back(self):
        for d, copy in enumerate(self.copies):
            copy.wait()
            origin = lax.rem(self.xy + self.nxy - d - 1, self.nxy)
            got = self.rows(self.n * ROWS + origin * self.plane, self.plane)
            self.across.append(send(self.whole.at[got], self.whole.at[got], self.pair(self.sem6, d), self.partner))

    def end(self):
        for copy in self.across:
            copy.wait()


def sum_scratch(nz, nxy):
    plane = ROWS // nxy
    sems = [pltpu.SemaphoreType.DMA((2, count)) for count in (2, nxy - 1, nz - 1, nz - 1, nxy - 1, nxy)]
    return [
        pltpu.VMEM((ROWS, L), BF16),
        pltpu.VMEM((plane, L), F32),
        pltpu.VMEM((plane, L), F32),
        pltpu.VMEM((2, HALF, L), F32),
        pltpu.VMEM((nxy - 1, plane, L), BF16),
        pltpu.VMEM((nz - 1, plane // nz, L), F32),
    ] + sems


def main_kernel(nz, nxy, slots, plan, features, occupancy, out_grad, weights1, weights2,
                output, feature_grad, reduced,
                table, shifted, columns, side, back, around, padded, middle, low, high, planes, edges, faces, grads,
                mask, slope, chosen, shell, masked, pre, sums, packed, whole,
                messages, near, hidden_shells, hidden_near,
                out1, got1, joined1, arrived1, out2, got2, joined2, arrived2,
                near_sems, hidden_sems, back_sems1, back_sems2, *scratch):
    n_wide = nz * nxy
    n = lax.axis_index("narrow")
    actives = Shells(n_wide, near, near_sems)
    hiddens = Shells(n_wide, hidden_near, hidden_sems)
    returns1 = Returns(n_wide, out1, got1, joined1, arrived1, back_sems1)
    returns2 = Returns(n_wide, out2, got2, joined2, arrived2, back_sems2)
    total = Sum(nz, nxy, packed, whole, scratch)
    everyone = [actives.peers[0], actives.peers[2]] + total.peers()
    greet(everyone)

    for t in range(B):
        seen = occupancy[t : t + 1, :].astype(F32)
        table[t] = to_rows(features[t].astype(F32) * seen).reshape(8, 8, 8, L)
    row = lax.broadcasted_iota(jnp.int32, (16, L), 0)
    pack_own(table, shell, messages.at[0])
    for g in range(3):
        if g > 0:
            messages[g, 0 : 2 * SHELL] = messages[0, 0 : 2 * SHELL]
        rows = jnp.zeros((16, L), F32)
        for i in range(4):
            rows = jnp.where(row == i, plan[0, g, i // 2, i % 2].astype(F32), rows)
        messages[g, 2 * SHELL : MESSAGE] = rows.astype(BF16)
    pl.semaphore_wait(pltpu.get_barrier_semaphore(), len(everyone))
    actives.start([messages.at[g] for g in range(3)])

    padded[...] = jnp.zeros_like(padded)
    masked[C:L] = jnp.zeros((L - C, B * V), BF16)
    for t in range(B):
        seen = occupancy[t : t + 1, :].astype(F32)
        mask[t] = jnp.broadcast_to(seen, (L, V)).T
        own = out_grad[t].astype(F32) * seen
        masked[0:C, t * V : (t + 1) * V] = own.astype(BF16)
        padded[t, 2:10, 2:10] = to_rows(own).reshape(8, 8, 8, L)

    def transpose(weights):
        back_weights(weights, back)
        faces[...] = jnp.zeros_like(faces)

        def one(t, carry):
            spread(t, padded, around, back, middle, low, high, planes, edges)
            scatter(t, slots, middle, planes, edges, faces)
            grads[t] = middle[1:9, 1:9]
            return carry

        lax.fori_loop(0, B, one, 0)
        for t in range(B):
            add_faces(faces[t], grads, t)

    transpose(weights2)
    side_weights(weights1, side)
    table[EMPTY] = jnp.zeros((8, 8, 8, L), F32)
    actives.finish()
    for source in range(SLOTS // 2):
        rows = near[source // 2, source % 2, 2 * SHELL : MESSAGE].astype(F32)
        for c in range(2):
            row = jnp.where(n == 0, rows[c : c + 1], rows[2 + c : 3 + c])
            chosen[2 * source + c] = jnp.broadcast_to(row, (8, L))
    gather_gradients(faces, chosen, out1)
    returns1.start()

    halo_entries(table, near, chosen)
    returns1.join()
    build_columns(slots, table, shifted, columns)
    for t in range(B):
        value = lax.dot_general(
            columns[t * V : (t + 1) * V, :], side[...], (((1,), (1,)), ((), ())), preferred_element_type=F32
        )
        seen = mask[t]
        gate = jax.nn.sigmoid(value)
        table[t] = (value * gate * seen).astype(BF16).astype(F32).reshape(8, 8, 8, L)
        slope[t] = seen * gate * (1.0 + value * (1.0 - gate))
    pack_own(table, shell, hidden_shells)
    hiddens.start([hidden_shells] * 3)
    side_weights(weights2, side)
    returns1.add(grads)
    for t in range(B):
        grad = grads[t].reshape(V, L) * slope[t]
        padded[t, 2:10, 2:10] = grad.reshape(8, 8, 8, L)
        pre[:, t * V : (t + 1) * V] = grad.T.astype(BF16)
    weight_sums(pre, columns, sums)
    pack_sums(sums, packed, 0)
    total.cores(0)

    hiddens.finish()
    halo_entries(table, hidden_near, chosen)
    build_columns(slots, table, shifted, columns)
    weight_sums(masked, columns, sums)
    pack_sums(sums, packed, ROWS)
    total.cores(1)
    total.planes()
    transpose(weights1)
    gather_gradients(faces, chosen, out2)
    returns2.start()
    total.columns()
    returns2.join()

    def forward(t):
        seen = occupancy[t : t + 1, :].astype(F32)
        value = lax.dot_general(
            side[...], columns[t * V : (t + 1) * V, :], (((1,), (1,)), ((), ())), preferred_element_type=F32
        )
        output[t] = ((features[t].astype(F32) * seen + value[0:C]) * seen).astype(BF16)

    forward(0)
    total.columns_back()
    forward(1)
    total.planes_back()
    returns2.add(grads)
    for t in range(B):
        seen = occupancy[t : t + 1, :].astype(F32)
        own = grads[t].reshape(V, L).T
        feature_grad[t] = ((out_grad[t].astype(F32) * seen + own[0:C]) * seen).astype(BF16)
    total.cores_back()
    total.end()
    reduced[...] = whole[...]


VMEM_SPEC = pl.BlockSpec(memory_space=pltpu.VMEM)
SMEM_SPEC = pl.BlockSpec(memory_space=pltpu.SMEM)


def shape(dims, dtype):
    return jax.ShapeDtypeStruct(dims, dtype)


def local_call(body, outs, scratch, scalars, *args):
    specs = [SMEM_SPEC] * scalars + [VMEM_SPEC] * (len(args) - scalars)
    return pl.pallas_call(
        body,
        out_shape=outs,
        in_specs=specs,
        out_specs=[VMEM_SPEC] * len(outs),
        scratch_shapes=[pltpu.VMEM(dims, dtype) for dims, dtype in scratch],
        compiler_params=pltpu.CompilerParams(vmem_limit_bytes=VMEM_LIMIT),
    )(*args)


BLOCK = (8, 8, 8, L)
SCRATCH = [
    ((EMPTY + 1,) + BLOCK, F32),
    ((3, 10, 10, 8, L), F32),
    ((B * V, 27 * L), BF16),
    ((L, 27 * L), BF16),
    ((9 * L, 3 * L), BF16),
    ((800, 9 * L), BF16),
    ((B, 12, 12, 8, L), F32),
    ((10, 10, 8, L), F32),
    ((10, 10, 8, L), F32),
    ((10, 10, 8, L), F32),
    ((2, 10, 8, L), F32),
    ((2, 2, 10, 8, L), F32),
    ((EMPTY, FACES // 8, 8, L), F32),
    ((B,) + BLOCK, F32),
    ((B, V, L), F32),
    ((B, V, L), F32),
    ((SLOTS, 8, L), F32),
    ((SHELL // 8, 8, L), F32),
    ((L, B * V), BF16),
    ((L, B * V), BF16),
    ((WG, L), F32),
    ((2 * ROWS, L), F32),
    ((2 * ROWS, L), BF16),
    ((3, MESSAGE, L), BF16),
    ((3, 2, MESSAGE, L), BF16),
    ((2 * SHELL, L), BF16),
    ((3, 2, 2 * SHELL, L), BF16),
] + 2 * [
    ((3, 2, 2 * FACES, L), BF16),
    ((2, 2 * FACES, L), BF16),
    ((2, 2 * FACES, L), BF16),
    ((3, 2 * FACES, L), BF16),
]


def local(nz, nxy, features, occupancy, conv1_weight, conv2_weight, out_grad, slots, send_blocks):
    dma = pltpu.SemaphoreType.DMA
    blocks = shape((B, C, V), BF16)
    output, feature_grad, reduced = pl.pallas_call(
        functools.partial(main_kernel, nz, nxy),
        out_shape=[blocks, blocks, shape((2 * ROWS, L), BF16)],
        in_specs=[SMEM_SPEC] * 2 + [VMEM_SPEC] * 5,
        out_specs=[VMEM_SPEC] * 3,
        scratch_shapes=[pltpu.VMEM(dims, dtype) for dims, dtype in SCRATCH]
        + [dma((2, 6)), dma((2, 6)), dma((2, 5)), dma((2, 5))] + sum_scratch(nz, nxy),
        compiler_params=pltpu.CompilerParams(
            collective_id=0, has_side_effects=True, vmem_limit_bytes=VMEM_LIMIT
        ),
    )(slots, send_blocks, features, occupancy, out_grad, conv1_weight, conv2_weight)
    scale = (B * V * 2 * nz * nxy) ** -0.5
    return pl.pallas_call(
        functools.partial(last_kernel, scale),
        out_shape=[blocks, blocks] + [shape((27, C, C), F32)] * 2,
        in_specs=[VMEM_SPEC] * 3,
        out_specs=[VMEM_SPEC] * 4,
        compiler_params=pltpu.CompilerParams(vmem_limit_bytes=VMEM_LIMIT),
    )(reduced, output, feature_grad)


def solution(mesh):
    both = ("wide", "narrow")
    n_wide = mesh.shape["wide"]
    nxy = 16 if n_wide % 16 == 0 else n_wide // 2
    return jax.shard_map(
        functools.partial(local, n_wide // nxy, nxy),
        mesh=mesh,
        in_specs=(P(both, None, None), P(both, None), P(), P(), P(both, None, None), P(both, None),
                  P(both, None, None, None)),
        out_specs=(P(both, None, None), P(both, None, None), P(), P()),
        check_vma=False,
    )
```

```python
import functools

import jax
import jax.numpy as jnp
from jax import lax
from jax.experimental import pallas as pl
from jax.experimental.pallas import tpu as pltpu
from jax.sharding import PartitionSpec as P

MESH = pl.DeviceIdType.MESH
F32 = jnp.float32
BF16 = jnp.bfloat16
C = 96
L = 128
V = 512
B = 2
SLOTS = 12
EMPTY = 14
SHELL = 320
TIGHT = SHELL * 3 // 4
OFFSETS = [(a, b, e) for a in (-1, 0, 1) for b in (-1, 0, 1) for e in (-1, 0, 1)]
PAIRS = [(a, b) for a in (-1, 0, 1) for b in (-1, 0, 1)]
PLACE = {-1: slice(0, 1), 0: slice(1, 9), 1: slice(9, 10)}
LAYER = {-1: slice(7, 8), 0: slice(0, 8), 1: slice(0, 1)}
HALF = 1024
ROWS = 2 * HALF
WG = 27 * C
QUARTER = WG // 4
MESSAGE = 2 * TIGHT + 16
FACES = 384
TIGHT_FACES = FACES * 3 // 4
VMEM_LIMIT = 56 * 1024 * 1024


def direction(a, b, e):
    return 9 * (a + 1) + 3 * (b + 1) + e + 1


def depth_index(shape):
    return lax.broadcasted_iota(jnp.int32, shape, len(shape) - 2)


def roll_depth(value, shift):
    return pltpu.roll(value, shift % 8, value.ndim - 2)


def to_rows(value):
    wide = jnp.concatenate([value, jnp.zeros((L - C, V), F32)], axis=0)
    return wide.T


def squeeze(rows):
    q = rows.shape[0] // 4
    lane = lax.broadcasted_iota(jnp.int32, (q, L), 1)
    last = rows[3 * q :]
    parts = [jnp.where(lane < C, rows[i * q : (i + 1) * q], pltpu.roll(last, C - 32 * i, 1)) for i in range(3)]
    return jnp.concatenate(parts, axis=0)


def stretch(rows):
    q = rows.shape[0] // 3
    lane = lax.broadcasted_iota(jnp.int32, (q, L), 1)
    parts, last = [], jnp.zeros((q, L), F32)
    for i in range(3):
        part = rows[i * q : (i + 1) * q]
        parts.append(jnp.where(lane < C, part, 0.0))
        last = jnp.where(lane // 32 == i, pltpu.roll(part, 32 + 32 * i, 1), last)
    return jnp.concatenate(parts + [last], axis=0)


def pack_shell(table, entry, shell):
    shell[0:8] = table[entry, 0]
    shell[8:16] = table[entry, 7]
    shell[16:22] = table[entry, 1:7, 0]
    shell[22:28] = table[entry, 1:7, 7]
    for at, z in ((28, 0), (34, 7)):
        shell[at : at + 6] = table[entry, 1:7, :, z, :]
    return squeeze(shell[...].reshape(SHELL, L)).astype(BF16)


def unpack_shell(shell, table, entry):
    table[entry, 0] = shell[0:8]
    table[entry, 7] = shell[8:16]
    table[entry, 1:7, 0] = shell[16:22]
    table[entry, 1:7, 7] = shell[22:28]
    table[entry, 1:7, :, 0, :] = shell[28:34]
    table[entry, 1:7, :, 7, :] = shell[34:40]


def add_faces(faces, grads, t):
    grads[t, 0] += faces[0:8]
    grads[t, 7] += faces[8:16]
    grads[t, :, 0] += faces[16:24]
    grads[t, :, 7] += faces[24:32]
    grads[t, :, :, 0, :] += faces[32:40]
    grads[t, :, :, 7, :] += faces[40:48]


def pack_own(table, shell, out, t):
    out[t * TIGHT : (t + 1) * TIGHT] = pack_shell(table, t, shell)


def gather_gradients(faces, chosen, out):
    for g in range(3):
        for m in range(2):
            for t in range(B):
                total = 0.0
                for c in range(2):
                    slot = 4 * g + 2 * m + c
                    total += jnp.where(chosen[slot] == float(t), faces[B + slot], 0.0)
                out[g, m, t * TIGHT_FACES : (t + 1) * TIGHT_FACES] = squeeze(total.reshape(FACES, L)).astype(BF16)


def halo_entries(table, halo, chosen):
    for source in range(SLOTS // 2):
        blocks = []
        for t in range(B):
            rows = halo[source // 2, source % 2, t * TIGHT : (t + 1) * TIGHT].astype(F32)
            blocks.append(stretch(rows).reshape(SHELL // 8, 8, L))
        for c in range(2):
            slot = 2 * source + c
            unpack_shell(jnp.where(chosen[slot] == 0.0, blocks[0], blocks[1]), table, B + slot)


def build_columns(slots, table, shifted, columns):
    def one(t, carry):
        for a, b in PAIRS:
            def source(e):
                return table[slots[t, direction(a, b, e)], LAYER[a], LAYER[b]]

            here = source(0)
            z = depth_index(here.shape)
            shifted[1, PLACE[a], PLACE[b]] = here
            shifted[0, PLACE[a], PLACE[b]] = roll_depth(jnp.where(z == 7, source(-1), here), 1)
            shifted[2, PLACE[a], PLACE[b]] = roll_depth(jnp.where(z == 0, source(1), here), -1)
        rows = pl.ds(pl.multiple_of(t * V, V), V)
        for o, (a, b, e) in enumerate(OFFSETS):
            part = shifted[e + 1, a + 1 : a + 9, b + 1 : b + 9]
            columns[rows, o * L : (o + 1) * L] = part.reshape(V, L).astype(BF16)
        return carry

    lax.fori_loop(0, B, one, 0)


def side_weights(weights, side):
    side[...] = jnp.zeros_like(side)
    for o in range(27):
        side[0:C, o * L : o * L + C] = weights[o]


def back_weights(weights, back):
    back[...] = jnp.zeros_like(back)
    for o in range(27):
        k, e = o // 3, o % 3
        back[k * L : k * L + C, e * L : e * L + C] = weights[o]


def spread(t, padded, around, back, middle, low, high, planes, edges):
    for k, (a, b) in enumerate(PAIRS):
        part = padded[t, 1 - a : 11 - a, 1 - b : 11 - b]
        around[:, k * L : (k + 1) * L] = part.reshape(800, L).astype(BF16)
    by_depth = jnp.dot(around[...], back[...], preferred_element_type=F32).reshape(10, 10, 8, 3 * L)
    low[...] = by_depth[..., 0:L]
    high[...] = by_depth[..., 2 * L : 3 * L]
    down = roll_depth(low[...], -1)
    up = roll_depth(high[...], 1)
    z = depth_index(up.shape)
    middle[...] = by_depth[..., L : 2 * L] + jnp.where(z != 0, up, 0.0) + jnp.where(z != 7, down, 0.0)
    y = depth_index((10, 8, L))
    for i, (source, at) in enumerate(((low, 0), (high, 7))):
        planes[i] = source[:, 1:9, at, :]
        for j, (column, row) in enumerate(((0, 7), (9, 0))):
            edge = source[:, column, at : at + 1, :]
            edges[i, j] = jnp.where(y == row, edge, 0.0)


def scatter(t, slots, middle, planes, edges, faces):
    def one(entry, carry):
        def weight(a, b, e):
            return (slots[t, direction(a, b, e)] == entry).astype(F32)

        for x, (a, px) in ((0, (1, 9)), (8, (-1, 0))):
            faces[entry, x : x + 8] += weight(a, 0, 0) * middle[px, 1:9]
            faces[entry, x] += weight(a, 1, 0) * middle[px, 9]
            faces[entry, x + 7] += weight(a, -1, 0) * middle[px, 0]
        faces[entry, 16:24] += weight(0, 1, 0) * middle[1:9, 9]
        faces[entry, 24:32] += weight(0, -1, 0) * middle[1:9, 0]
        for at, e, i in ((32, 1, 1), (40, -1, 0)):
            for a, x, px in ((0, slice(at, at + 8), slice(1, 9)), (1, at, 9), (-1, at + 7, 0)):
                total = weight(a, 0, e) * planes[i, px]
                total += weight(a, -1, e) * edges[i, 0, px] + weight(a, 1, e) * edges[i, 1, px]
                faces[entry, x] += total
        return carry

    lax.fori_loop(0, EMPTY, one, 0)


def weight_sums(left, columns, out):
    for o in range(0, 27, 3):
        sums = jnp.dot(left[...], columns[:, o * L : (o + 3) * L], preferred_element_type=F32)
        for i in range(3):
            row = (o + i) * C
            out[row : row + C] = sums[0:C, i * L : (i + 1) * L]


def pack_sums(sums, packed, at):
    last = sums[3 * QUARTER : WG]
    lane = lax.broadcasted_iota(jnp.int32, (QUARTER, L), 1)
    for i in range(3):
        moved = pltpu.roll(last, C - 32 * i, 1)
        rows = slice(i * QUARTER, (i + 1) * QUARTER)
        packed[at + i * QUARTER : at + (i + 1) * QUARTER] = jnp.where(lane < C, sums[rows], moved)
    packed[at + 3 * QUARTER : at + ROWS] = jnp.zeros((ROWS - 3 * QUARTER, L), F32)


def last_kernel(scale, packed, output, grad, output_out, grad_out, first, second):
    output_out[...] = output[...]
    grad_out[...] = grad[...]
    lane = lax.broadcasted_iota(jnp.int32, (QUARTER, L), 1)
    for i, out in enumerate((first, second)):
        whole = packed[i * ROWS : (i + 1) * ROWS].astype(F32) * scale
        last = jnp.zeros((QUARTER, L), F32)
        for k in range(3):
            part = whole[k * QUARTER : (k + 1) * QUARTER]
            last = jnp.where(lane // 32 == k, pltpu.roll(part, 32 + 32 * k, 1), last)
        for r in range(0, WG, 24):
            part = whole[r : r + 24] if r < 3 * QUARTER else last[r - 3 * QUARTER : r - 3 * QUARTER + 24]
            out[r // C, r % C : r % C + 24, :] = part[:, 0:C]


def send(source, dest, sems, peer):
    copy = pltpu.make_async_remote_copy(
        src_ref=source, dst_ref=dest, send_sem=sems[0], recv_sem=sems[1], device_id=peer, device_id_type=MESH
    )
    copy.start()
    return copy


def greet(peers):
    barrier = pltpu.get_barrier_semaphore()
    for peer in peers:
        pl.semaphore_signal(barrier, inc=1, device_id=peer, device_id_type=MESH)


def neighbours(n_wide):
    w, n = lax.axis_index("wide"), lax.axis_index("narrow")
    ahead, behind = lax.rem(w + 1, n_wide), lax.rem(w + n_wide - 1, n_wide)
    return w, n, ahead, behind


class Shells:
    def __init__(self, n_wide, halo, sems):
        self.w, self.n, ahead, behind = neighbours(n_wide)
        self.partner = (self.w, 1 - self.n)
        self.peers = [(behind, self.n), self.partner, (ahead, self.n)]
        self.halo, self.sems, self.copies = halo, sems, {}

    def pair(self, k, i):
        return self.sems.at[0, k, i], self.sems.at[1, k, i]

    def rows(self, k):
        return pl.ds(k * TIGHT, TIGHT if k == 0 else self.halo.shape[2] - TIGHT)

    def start(self, sources, k):
        self.copies[k] = [
            send(sources[g].at[self.rows(k)], self.halo.at[g, self.n, self.rows(k)], self.pair(k, g), self.peers[g])
            for g in range(3)
        ]

    def forward(self):
        self.across = []
        for k in range(B):
            for g in (0, 2):
                self.copies[k][g].wait()
                got = self.halo.at[g, self.n, self.rows(k)]
                self.across.append(send(got, got, self.pair(k, 3 + g), self.partner))

    def settle(self):
        for k in range(B):
            self.copies[k][1].wait()
        for copy in self.across:
            copy.wait()


class Returns:
    def __init__(self, n_wide, out, got, joined, arrived, sems):
        self.w, self.n, ahead, behind = neighbours(n_wide)
        self.partner = (self.w, 1 - self.n)
        self.to = {0: (ahead, self.n), 2: (behind, self.n)}
        self.out, self.got, self.joined, self.arrived, self.sems = out, got, joined, arrived, sems

    def pair(self, i):
        return self.sems.at[0, i], self.sems.at[1, i]

    def start(self):
        self.joins = [
            send(self.out.at[g, 1 - self.n], self.got.at[i], self.pair(i), self.partner) for i, g in enumerate((0, 2))
        ]
        self.backs = [send(self.out.at[1, 1 - self.n], self.arrived.at[1], self.pair(2), self.partner)]

    def join(self):
        for i, g in enumerate((0, 2)):
            self.joins[i].wait()
            self.joined[i] = (self.out[g, self.n].astype(F32) + self.got[i].astype(F32)).astype(BF16)
            self.backs.append(send(self.joined.at[i], self.arrived.at[g], self.pair(3 + i), self.to[g]))

    def add(self, grads):
        for copy in self.backs:
            copy.wait()
        for t in range(B):
            for g in range(3):
                faces = stretch(self.arrived[g, t * TIGHT_FACES : (t + 1) * TIGHT_FACES].astype(F32))
                add_faces(faces.reshape(FACES // 8, 8, L), grads, t)


class Sum:
    def __init__(self, nz, nxy, src, whole, at, scratch):
        self.nz, self.nxy, self.src, self.whole, self.at = nz, nxy, src, whole, at
        (self.half, self.got1, self.got2, self.got3,
         self.sem1, self.sem2, self.sem3, self.sem4, self.sem5) = scratch
        w, self.n = lax.axis_index("wide"), lax.axis_index("narrow")
        self.z, self.xy = w // nxy, lax.rem(w, nxy)
        self.plane = HALF // nxy
        self.partner = (w, 1 - self.n)
        self.in_plane = [(self.z * nxy + lax.rem(self.xy + d, nxy), self.n) for d in range(1, nxy)]
        self.in_column = [(lax.rem(self.z + d, nz) * nxy + self.xy, self.n) for d in range(1, nz)]

    def peers(self):
        return [self.partner] + self.in_plane + self.in_column

    def rows(self, at, size):
        return pl.ds(pl.multiple_of(at, size), size)

    def pair(self, sems, d):
        return sems.at[0, d], sems.at[1, d]

    def cores(self):
        theirs = self.src.at[self.rows((1 - self.n) * HALF, HALF)]
        self.copies = [send(theirs, self.got1, self.pair(self.sem1, 0), self.partner)]

    def wait(self):
        for copy in self.copies:
            copy.wait()

    def planes(self):
        self.wait()
        mine = self.src[self.rows(self.n * HALF, HALF), :]
        self.half[...] = (mine + self.got1[...]).astype(BF16)
        self.copies = []
        for d, peer in enumerate(self.in_plane):
            to = lax.rem(self.xy + d + 1, self.nxy)
            part = self.half.at[self.rows(to * self.plane, self.plane)]
            self.copies.append(send(part, self.got2.at[d], self.pair(self.sem2, d), peer))

    def column(self):
        self.wait()
        total = self.half[self.rows(self.xy * self.plane, self.plane), :].astype(F32)
        for d in range(self.nxy - 1):
            total += self.got2[d].astype(F32)
        own = self.got3.at[self.z]
        own[...] = total.astype(BF16)
        self.copies = [send(own, own, self.pair(self.sem3, d), peer) for d, peer in enumerate(self.in_column)]

    def planes_back(self):
        self.wait()
        total = self.got3[0].astype(F32)
        for z in range(1, self.nz):
            total += self.got3[z].astype(F32)
        own = self.rows(self.at + self.n * HALF + self.xy * self.plane, self.plane)
        self.whole[own, :] = total.astype(BF16)
        own = self.whole.at[own]
        self.copies = [send(own, own, self.pair(self.sem4, d), peer) for d, peer in enumerate(self.in_plane)]
        self.across = [send(own, own, self.pair(self.sem5, self.nxy - 1), self.partner)]

    def cores_back(self):
        for d, copy in enumerate(self.copies):
            copy.wait()
            origin = lax.rem(self.xy + self.nxy - d - 1, self.nxy)
            got = self.whole.at[self.rows(self.at + self.n * HALF + origin * self.plane, self.plane)]
            self.across.append(send(got, got, self.pair(self.sem5, d), self.partner))

    def end(self):
        for copy in self.across:
            copy.wait()


def sum_scratch(nz, nxy):
    plane = HALF // nxy
    sems = [pltpu.SemaphoreType.DMA((2, count)) for count in (1, nxy - 1, nz - 1, nxy - 1, nxy)]
    return [
        pltpu.VMEM((HALF, L), BF16),
        pltpu.VMEM((HALF, L), F32),
        pltpu.VMEM((nxy - 1, plane, L), BF16),
        pltpu.VMEM((nz, plane, L), BF16),
    ] + sems


def main_kernel(nz, nxy, slots, plan, features, occupancy, out_grad, far_weights1, far_weights2,
                output, feature_grad, reduced,
                table, shifted, columns, side, back, around, padded, middle, low, high, planes, edges, faces, grads,
                mask, slope, chosen, shell, masked, pre, sums, packed1, packed2, weights1, weights2,
                messages, near, hidden_shells, hidden_near,
                out1, got1, joined1, arrived1, out2, got2, joined2, arrived2,
                near_sems, hidden_sems, back_sems1, back_sems2, load_sems, *scratch):
    n_wide = nz * nxy
    n = lax.axis_index("narrow")
    actives = Shells(n_wide, near, near_sems)
    hiddens = Shells(n_wide, hidden_near, hidden_sems)
    returns1 = Returns(n_wide, out1, got1, joined1, arrived1, back_sems1)
    returns2 = Returns(n_wide, out2, got2, joined2, arrived2, back_sems2)
    total1 = Sum(nz, nxy, packed1, reduced, 0, scratch[: len(scratch) // 2])
    total2 = Sum(nz, nxy, packed2, reduced, ROWS, scratch[len(scratch) // 2 :])
    everyone = [actives.peers[0], actives.peers[2]] + total1.peers()
    greet(everyone)
    load1 = pltpu.make_async_copy(far_weights1, weights1, load_sems.at[0])
    load2 = pltpu.make_async_copy(far_weights2, weights2, load_sems.at[1])
    load2.start()
    load1.start()

    for t in range(B):
        seen = occupancy[t : t + 1, :].astype(F32)
        table[t] = to_rows(features[t].astype(F32) * seen).reshape(8, 8, 8, L)
    row = lax.broadcasted_iota(jnp.int32, (16, L), 0)
    for t in range(B):
        pack_own(table, shell, messages.at[0], t)
    for g in range(3):
        if g > 0:
            messages[g, 0 : 2 * TIGHT] = messages[0, 0 : 2 * TIGHT]
        rows = jnp.zeros((16, L), F32)
        for i in range(4):
            rows = jnp.where(row == i, plan[i, g].astype(F32), rows)
        messages[g, 2 * TIGHT : MESSAGE] = rows.astype(BF16)
    pl.semaphore_wait(pltpu.get_barrier_semaphore(), len(everyone))
    for t in range(B):
        actives.start([messages.at[g] for g in range(3)], t)

    padded[...] = jnp.zeros_like(padded)
    masked[C:L] = jnp.zeros((L - C, B * V), BF16)
    for t in range(B):
        seen = occupancy[t : t + 1, :].astype(F32)
        mask[t] = jnp.broadcast_to(seen, (L, V)).T
        own = out_grad[t].astype(F32) * seen
        masked[0:C, t * V : (t + 1) * V] = own.astype(BF16)
        padded[t, 2:10, 2:10] = to_rows(own).reshape(8, 8, 8, L)

    def transpose(weights):
        back_weights(weights, back)
        faces[...] = jnp.zeros_like(faces)

        def one(t, carry):
            spread(t, padded, around, back, middle, low, high, planes, edges)
            scatter(t, slots, middle, planes, edges, faces)
            grads[t] = middle[1:9, 1:9]
            return carry

        lax.fori_loop(0, B, one, 0)
        for t in range(B):
            add_faces(faces[t], grads, t)

    load2.wait()
    transpose(weights2)
    load1.wait()
    side_weights(weights1, side)
    table[EMPTY] = jnp.zeros((8, 8, 8, L), F32)
    actives.forward()
    actives.settle()
    for source in range(SLOTS // 2):
        rows = near[source // 2, source % 2, 2 * TIGHT : MESSAGE].astype(F32)
        for c in range(2):
            row = jnp.where(n == 0, rows[c : c + 1], rows[2 + c : 3 + c])
            chosen[2 * source + c] = jnp.broadcast_to(row, (8, L))
    gather_gradients(faces, chosen, out1)
    returns1.start()

    halo_entries(table, near, chosen)
    returns1.join()
    build_columns(slots, table, shifted, columns)
    for t in range(B):
        value = lax.dot_general(
            columns[t * V : (t + 1) * V, :], side[...], (((1,), (1,)), ((), ())), preferred_element_type=F32
        )
        seen = mask[t]
        gate = jax.nn.sigmoid(value)
        table[t] = (value * gate * seen).astype(BF16).astype(F32).reshape(8, 8, 8, L)
        pack_own(table, shell, hidden_shells, t)
        hiddens.start([hidden_shells] * 3, t)
        slope[t] = seen * gate * (1.0 + value * (1.0 - gate))
    side_weights(weights2, side)
    returns1.add(grads)
    for t in range(B):
        grad = grads[t].reshape(V, L) * slope[t]
        padded[t, 2:10, 2:10] = grad.reshape(8, 8, 8, L)
        pre[:, t * V : (t + 1) * V] = grad.T.astype(BF16)
    weight_sums(pre, columns, sums)
    pack_sums(sums, packed1, 0)
    total1.cores()

    hiddens.forward()
    total1.planes()
    hiddens.settle()
    halo_entries(table, hidden_near, chosen)
    build_columns(slots, table, shifted, columns)
    weight_sums(masked, columns, sums)
    pack_sums(sums, packed2, 0)
    total2.cores()
    total1.column()
    total2.planes()
    transpose(weights1)
    gather_gradients(faces, chosen, out2)
    returns2.start()
    total2.column()
    total1.planes_back()
    returns2.join()

    def forward(t):
        seen = occupancy[t : t + 1, :].astype(F32)
        value = lax.dot_general(
            side[...], columns[t * V : (t + 1) * V, :], (((1,), (1,)), ((), ())), preferred_element_type=F32
        )
        output[t] = ((features[t].astype(F32) * seen + value[0:C]) * seen).astype(BF16)

    forward(0)
    forward(1)
    total1.cores_back()
    total2.planes_back()
    returns2.add(grads)
    for t in range(B):
        seen = occupancy[t : t + 1, :].astype(F32)
        own = grads[t].reshape(V, L).T
        feature_grad[t] = ((out_grad[t].astype(F32) * seen + own[0:C]) * seen).astype(BF16)
    total1.end()
    total2.cores_back()
    total2.end()


VMEM_SPEC = pl.BlockSpec(memory_space=pltpu.VMEM)
SMEM_SPEC = pl.BlockSpec(memory_space=pltpu.SMEM)
ANY_SPEC = pl.BlockSpec(memory_space=pl.ANY)


def shape(dims, dtype):
    return jax.ShapeDtypeStruct(dims, dtype)


BLOCK = (8, 8, 8, L)
SCRATCH = [
    ((EMPTY + 1,) + BLOCK, F32),
    ((3, 10, 10, 8, L), F32),
    ((B * V, 27 * L), BF16),
    ((L, 27 * L), BF16),
    ((9 * L, 3 * L), BF16),
    ((800, 9 * L), BF16),
    ((B, 12, 12, 8, L), F32),
    ((10, 10, 8, L), F32),
    ((10, 10, 8, L), F32),
    ((10, 10, 8, L), F32),
    ((2, 10, 8, L), F32),
    ((2, 2, 10, 8, L), F32),
    ((EMPTY, FACES // 8, 8, L), F32),
    ((B,) + BLOCK, F32),
    ((B, V, L), F32),
    ((B, V, L), F32),
    ((SLOTS, 8, L), F32),
    ((SHELL // 8, 8, L), F32),
    ((L, B * V), BF16),
    ((L, B * V), BF16),
    ((WG, L), F32),
    ((ROWS, L), F32),
    ((ROWS, L), F32),
    ((27, C, C), BF16),
    ((27, C, C), BF16),
    ((3, MESSAGE, L), BF16),
    ((3, 2, MESSAGE, L), BF16),
    ((2 * TIGHT, L), BF16),
    ((3, 2, 2 * TIGHT, L), BF16),
] + 2 * [
    ((3, 2, 2 * TIGHT_FACES, L), BF16),
    ((2, 2 * TIGHT_FACES, L), BF16),
    ((2, 2 * TIGHT_FACES, L), BF16),
    ((3, 2 * TIGHT_FACES, L), BF16),
]


def local(nz, nxy, features, occupancy, conv1_weight, conv2_weight, out_grad, slots, send_blocks):
    dma = pltpu.SemaphoreType.DMA
    blocks = shape((B, C, V), BF16)
    output, feature_grad, reduced = pl.pallas_call(
        functools.partial(main_kernel, nz, nxy),
        out_shape=[blocks, blocks, shape((2 * ROWS, L), BF16)],
        in_specs=[SMEM_SPEC] * 2 + [VMEM_SPEC] * 3 + [ANY_SPEC] * 2,
        out_specs=[VMEM_SPEC] * 3,
        scratch_shapes=[pltpu.VMEM(dims, dtype) for dims, dtype in SCRATCH]
        + [dma((2, 2, 6)), dma((2, 2, 6)), dma((2, 5)), dma((2, 5)), dma((2,))] + 2 * sum_scratch(nz, nxy),
        compiler_params=pltpu.CompilerParams(
            collective_id=0, has_side_effects=True, vmem_limit_bytes=VMEM_LIMIT
        ),
    )(slots, send_blocks.reshape(3, 4).T, features, occupancy, out_grad, conv1_weight, conv2_weight)
    scale = (B * V * 2 * nz * nxy) ** -0.5
    return pl.pallas_call(
        functools.partial(last_kernel, scale),
        out_shape=[blocks, blocks] + [shape((27, C, C), F32)] * 2,
        in_specs=[VMEM_SPEC] * 3,
        out_specs=[VMEM_SPEC] * 4,
        compiler_params=pltpu.CompilerParams(vmem_limit_bytes=VMEM_LIMIT),
    )(reduced, output, feature_grad)


def solution(mesh):
    both = ("wide", "narrow")
    n_wide = mesh.shape["wide"]
    nxy = 16 if n_wide % 16 == 0 else n_wide // 2
    return jax.shard_map(
        functools.partial(local, n_wide // nxy, nxy),
        mesh=mesh,
        in_specs=(P(both, None, None), P(both, None), P(), P(), P(both, None, None), P(both, None),
                  P(both, None, None, None)),
        out_specs=(P(both, None, None), P(both, None, None), P(), P()),
        check_vma=False,
    )
```

```python
import functools

import jax
import jax.numpy as jnp
from jax import lax
from jax.experimental import pallas as pl
from jax.experimental.pallas import tpu as pltpu
from jax.sharding import PartitionSpec as P

MESH = pl.DeviceIdType.MESH
F32 = jnp.float32
BF16 = jnp.bfloat16
C = 96
L = 128
V = 512
B = 2
SLOTS = 12
EMPTY = 14
SHELL = 320
TIGHT = SHELL * 3 // 4
OFFSETS = [(a, b, e) for a in (-1, 0, 1) for b in (-1, 0, 1) for e in (-1, 0, 1)]
PAIRS = [(a, b) for a in (-1, 0, 1) for b in (-1, 0, 1)]
PLACE = {-1: slice(0, 1), 0: slice(1, 9), 1: slice(9, 10)}
LAYER = {-1: slice(7, 8), 0: slice(0, 8), 1: slice(0, 1)}
HALF = 1024
ROWS = 2 * HALF
WG = 27 * C
QUARTER = WG // 4
MESSAGE = 2 * TIGHT + 16
FACES = 384
TIGHT_FACES = FACES * 3 // 4
VMEM_LIMIT = 56 * 1024 * 1024


def direction(a, b, e):
    return 9 * (a + 1) + 3 * (b + 1) + e + 1


def depth_index(shape):
    return lax.broadcasted_iota(jnp.int32, shape, len(shape) - 2)


def roll_depth(value, shift):
    return pltpu.roll(value, shift % 8, value.ndim - 2)


def to_rows(value):
    wide = jnp.concatenate([value, jnp.zeros((L - C, V), F32)], axis=0)
    return wide.T


def squeeze(rows):
    q = rows.shape[0] // 4
    lane = lax.broadcasted_iota(jnp.int32, (q, L), 1)
    last = rows[3 * q :]
    parts = [jnp.where(lane < C, rows[i * q : (i + 1) * q], pltpu.roll(last, C - 32 * i, 1)) for i in range(3)]
    return jnp.concatenate(parts, axis=0)


def stretch(rows):
    q = rows.shape[0] // 3
    lane = lax.broadcasted_iota(jnp.int32, (q, L), 1)
    parts, last = [], jnp.zeros((q, L), F32)
    for i in range(3):
        part = rows[i * q : (i + 1) * q]
        parts.append(jnp.where(lane < C, part, 0.0))
        last = jnp.where(lane // 32 == i, pltpu.roll(part, 32 + 32 * i, 1), last)
    return jnp.concatenate(parts + [last], axis=0)


def pack_shell(table, entry, shell):
    shell[0:8] = table[entry, 0]
    shell[8:16] = table[entry, 7]
    shell[16:22] = table[entry, 1:7, 0]
    shell[22:28] = table[entry, 1:7, 7]
    for at, z in ((28, 0), (34, 7)):
        shell[at : at + 6] = table[entry, 1:7, :, z, :]
    return squeeze(shell[...].reshape(SHELL, L)).astype(BF16)


def unpack_shell(shell, table, entry):
    table[entry, 0] = shell[0:8]
    table[entry, 7] = shell[8:16]
    table[entry, 1:7, 0] = shell[16:22]
    table[entry, 1:7, 7] = shell[22:28]
    table[entry, 1:7, :, 0, :] = shell[28:34]
    table[entry, 1:7, :, 7, :] = shell[34:40]


def add_faces(faces, grads, t):
    grads[t, 0] += faces[0:8]
    grads[t, 7] += faces[8:16]
    grads[t, :, 0] += faces[16:24]
    grads[t, :, 7] += faces[24:32]
    grads[t, :, :, 0, :] += faces[32:40]
    grads[t, :, :, 7, :] += faces[40:48]


def pack_own(table, shell, out, t):
    out[t * TIGHT : (t + 1) * TIGHT] = pack_shell(table, t, shell)


def gather_gradients(faces, chosen, out):
    for g in range(3):
        for m in range(2):
            for t in range(B):
                total = 0.0
                for c in range(2):
                    slot = 4 * g + 2 * m + c
                    total += jnp.where(chosen[slot] == float(t), faces[B + slot], 0.0)
                out[g, m, t * TIGHT_FACES : (t + 1) * TIGHT_FACES] = squeeze(total.reshape(FACES, L)).astype(BF16)


def halo_entries(table, halo, chosen):
    for source in range(SLOTS // 2):
        blocks = []
        for t in range(B):
            rows = halo[source // 2, source % 2, t * TIGHT : (t + 1) * TIGHT].astype(F32)
            blocks.append(stretch(rows).reshape(SHELL // 8, 8, L))
        for c in range(2):
            slot = 2 * source + c
            unpack_shell(jnp.where(chosen[slot] == 0.0, blocks[0], blocks[1]), table, B + slot)


def build_columns(slots, table, shifted, columns):
    def one(t, carry):
        for a, b in PAIRS:
            def source(e):
                return table[slots[t, direction(a, b, e)], LAYER[a], LAYER[b]]

            here = source(0)
            z = depth_index(here.shape)
            shifted[1, PLACE[a], PLACE[b]] = here
            shifted[0, PLACE[a], PLACE[b]] = roll_depth(jnp.where(z == 7, source(-1), here), 1)
            shifted[2, PLACE[a], PLACE[b]] = roll_depth(jnp.where(z == 0, source(1), here), -1)
        rows = pl.ds(pl.multiple_of(t * V, V), V)
        for o, (a, b, e) in enumerate(OFFSETS):
            part = shifted[e + 1, a + 1 : a + 9, b + 1 : b + 9]
            columns[rows, o * L : (o + 1) * L] = part.reshape(V, L).astype(BF16)
        return carry

    lax.fori_loop(0, B, one, 0)


def side_weights(weights, side):
    side[...] = jnp.zeros_like(side)
    for o in range(27):
        side[0:C, o * L : o * L + C] = weights[o]


def back_weights(weights, back):
    back[...] = jnp.zeros_like(back)
    for o in range(27):
        k, e = o // 3, o % 3
        back[k * L : k * L + C, e * L : e * L + C] = weights[o]


def spread(t, padded, around, back, middle, low, high, planes, edges):
    for k, (a, b) in enumerate(PAIRS):
        part = padded[t, 1 - a : 11 - a, 1 - b : 11 - b]
        around[:, k * L : (k + 1) * L] = part.reshape(800, L).astype(BF16)
    by_depth = jnp.dot(around[...], back[...], preferred_element_type=F32).reshape(10, 10, 8, 3 * L)
    low[...] = by_depth[..., 0:L]
    high[...] = by_depth[..., 2 * L : 3 * L]
    down = roll_depth(low[...], -1)
    up = roll_depth(high[...], 1)
    z = depth_index(up.shape)
    middle[...] = by_depth[..., L : 2 * L] + jnp.where(z != 0, up, 0.0) + jnp.where(z != 7, down, 0.0)
    y = depth_index((10, 8, L))
    for i, (source, at) in enumerate(((low, 0), (high, 7))):
        planes[i] = source[:, 1:9, at, :]
        for j, (column, row) in enumerate(((0, 7), (9, 0))):
            edge = source[:, column, at : at + 1, :]
            edges[i, j] = jnp.where(y == row, edge, 0.0)


def scatter(t, slots, middle, planes, edges, faces):
    def one(entry, carry):
        def weight(a, b, e):
            return (slots[t, direction(a, b, e)] == entry).astype(F32)

        for x, (a, px) in ((0, (1, 9)), (8, (-1, 0))):
            faces[entry, x : x + 8] += weight(a, 0, 0) * middle[px, 1:9]
            faces[entry, x] += weight(a, 1, 0) * middle[px, 9]
            faces[entry, x + 7] += weight(a, -1, 0) * middle[px, 0]
        faces[entry, 16:24] += weight(0, 1, 0) * middle[1:9, 9]
        faces[entry, 24:32] += weight(0, -1, 0) * middle[1:9, 0]
        for at, e, i in ((32, 1, 1), (40, -1, 0)):
            for a, x, px in ((0, slice(at, at + 8), slice(1, 9)), (1, at, 9), (-1, at + 7, 0)):
                total = weight(a, 0, e) * planes[i, px]
                total += weight(a, -1, e) * edges[i, 0, px] + weight(a, 1, e) * edges[i, 1, px]
                faces[entry, x] += total
        return carry

    lax.fori_loop(0, EMPTY, one, 0)


def weight_sums(left, columns, out):
    for o in range(0, 27, 3):
        sums = jnp.dot(left[...], columns[:, o * L : (o + 3) * L], preferred_element_type=F32)
        for i in range(3):
            row = (o + i) * C
            out[row : row + C] = sums[0:C, i * L : (i + 1) * L]


def pack_sums(sums, packed, at):
    last = sums[3 * QUARTER : WG]
    lane = lax.broadcasted_iota(jnp.int32, (QUARTER, L), 1)
    for i in range(3):
        moved = pltpu.roll(last, C - 32 * i, 1)
        rows = slice(i * QUARTER, (i + 1) * QUARTER)
        packed[at + i * QUARTER : at + (i + 1) * QUARTER] = jnp.where(lane < C, sums[rows], moved)
    packed[at + 3 * QUARTER : at + ROWS] = jnp.zeros((ROWS - 3 * QUARTER, L), F32)


def last_kernel(scale, packed, output, grad, output_out, grad_out, first, second):
    output_out[...] = output[...]
    grad_out[...] = grad[...]
    lane = lax.broadcasted_iota(jnp.int32, (QUARTER, L), 1)
    for i, out in enumerate((first, second)):
        whole = packed[i * ROWS : (i + 1) * ROWS].astype(F32) * scale
        last = jnp.zeros((QUARTER, L), F32)
        for k in range(3):
            part = whole[k * QUARTER : (k + 1) * QUARTER]
            last = jnp.where(lane // 32 == k, pltpu.roll(part, 32 + 32 * k, 1), last)
        for r in range(0, WG, 24):
            part = whole[r : r + 24] if r < 3 * QUARTER else last[r - 3 * QUARTER : r - 3 * QUARTER + 24]
            out[r // C, r % C : r % C + 24, :] = part[:, 0:C]


def send(source, dest, sems, peer):
    copy = pltpu.make_async_remote_copy(
        src_ref=source, dst_ref=dest, send_sem=sems[0], recv_sem=sems[1], device_id=peer, device_id_type=MESH
    )
    copy.start()
    return copy


def greet(peers):
    barrier = pltpu.get_barrier_semaphore()
    for peer in peers:
        pl.semaphore_signal(barrier, inc=1, device_id=peer, device_id_type=MESH)


def neighbours(n_wide):
    w, n = lax.axis_index("wide"), lax.axis_index("narrow")
    ahead, behind = lax.rem(w + 1, n_wide), lax.rem(w + n_wide - 1, n_wide)
    return w, n, ahead, behind


class Shells:
    def __init__(self, n_wide, halo, sems):
        self.w, self.n, ahead, behind = neighbours(n_wide)
        self.partner = (self.w, 1 - self.n)
        self.peers = [(behind, self.n), self.partner, (ahead, self.n)]
        self.halo, self.sems, self.copies = halo, sems, {}

    def pair(self, k, i):
        return self.sems.at[0, k, i], self.sems.at[1, k, i]

    def rows(self, k):
        return pl.ds(k * TIGHT, TIGHT if k == 0 else self.halo.shape[2] - TIGHT)

    def start(self, sources, k):
        self.copies[k] = [
            send(sources[g].at[self.rows(k)], self.halo.at[g, self.n, self.rows(k)], self.pair(k, g), self.peers[g])
            for g in range(3)
        ]

    def forward(self):
        self.across = []
        for k in range(B):
            for g in (0, 2):
                self.copies[k][g].wait()
                got = self.halo.at[g, self.n, self.rows(k)]
                self.across.append(send(got, got, self.pair(k, 3 + g), self.partner))

    def settle(self):
        for k in range(B):
            self.copies[k][1].wait()
        for copy in self.across:
            copy.wait()


class Returns:
    def __init__(self, n_wide, out, got, joined, arrived, sems):
        self.w, self.n, ahead, behind = neighbours(n_wide)
        self.partner = (self.w, 1 - self.n)
        self.to = {0: (ahead, self.n), 2: (behind, self.n)}
        self.out, self.got, self.joined, self.arrived, self.sems = out, got, joined, arrived, sems

    def pair(self, i):
        return self.sems.at[0, i], self.sems.at[1, i]

    def start(self):
        self.joins = [
            send(self.out.at[g, 1 - self.n], self.got.at[i], self.pair(i), self.partner) for i, g in enumerate((0, 2))
        ]
        self.backs = [send(self.out.at[1, 1 - self.n], self.arrived.at[1], self.pair(2), self.partner)]

    def join(self):
        for i, g in enumerate((0, 2)):
            self.joins[i].wait()
            self.joined[i] = (self.out[g, self.n].astype(F32) + self.got[i].astype(F32)).astype(BF16)
            self.backs.append(send(self.joined.at[i], self.arrived.at[g], self.pair(3 + i), self.to[g]))

    def add(self, grads):
        for copy in self.backs:
            copy.wait()
        for t in range(B):
            for g in range(3):
                faces = stretch(self.arrived[g, t * TIGHT_FACES : (t + 1) * TIGHT_FACES].astype(F32))
                add_faces(faces.reshape(FACES // 8, 8, L), grads, t)


class Sum:
    def __init__(self, nz, nxy, src, whole, at, scratch):
        self.nz, self.nxy, self.src, self.whole, self.at = nz, nxy, src, whole, at
        (self.half, self.got1, self.got2, self.got3,
         self.sem1, self.sem2, self.sem3, self.sem4, self.sem5) = scratch
        w, self.n = lax.axis_index("wide"), lax.axis_index("narrow")
        self.z, self.xy = w // nxy, lax.rem(w, nxy)
        self.plane = HALF // nxy
        self.partner = (w, 1 - self.n)
        nx = 4 if nxy % 4 == 0 else nxy
        ny = nxy // nx
        x, y = lax.rem(self.xy, nx), self.xy // nx

        def place(dx, dy):
            return lax.rem(y + dy + ny, ny) * nx + lax.rem(x + dx + nx, nx)

        def hops(step, size):
            return min(step, size - step)

        steps = [(dx, dy) for dx in range(nx) for dy in range(ny) if dx or dy]
        steps.sort(key=lambda step: -hops(step[0], nx) - hops(step[1], ny))
        self.to = [place(dx, dy) for dx, dy in steps]
        self.origin = [place(-dx, -dy) for dx, dy in steps]
        self.in_plane = [(self.z * nxy + to, self.n) for to in self.to]
        rises = sorted(range(1, nz), key=lambda rise: -hops(rise, nz))
        self.in_column = [(lax.rem(self.z + rise, nz) * nxy + self.xy, self.n) for rise in rises]

    def peers(self):
        return [self.partner] + self.in_plane + self.in_column

    def rows(self, at, size):
        return pl.ds(pl.multiple_of(at, size), size)

    def pair(self, sems, d):
        return sems.at[0, d], sems.at[1, d]

    def cores(self):
        theirs = self.src.at[self.rows((1 - self.n) * HALF, HALF)]
        self.copies = [send(theirs, self.got1, self.pair(self.sem1, 0), self.partner)]

    def wait(self):
        for copy in self.copies:
            copy.wait()

    def planes(self):
        self.wait()
        mine = self.src[self.rows(self.n * HALF, HALF), :]
        self.half[...] = (mine + self.got1[...]).astype(BF16)
        self.copies = []
        for d, peer in enumerate(self.in_plane):
            part = self.half.at[self.rows(self.to[d] * self.plane, self.plane)]
            self.copies.append(send(part, self.got2.at[d], self.pair(self.sem2, d), peer))

    def column(self):
        self.wait()
        total = self.half[self.rows(self.xy * self.plane, self.plane), :].astype(F32)
        for d in range(self.nxy - 1):
            total += self.got2[d].astype(F32)
        own = self.got3.at[self.z]
        own[...] = total.astype(BF16)
        self.copies = [send(own, own, self.pair(self.sem3, d), peer) for d, peer in enumerate(self.in_column)]

    def planes_back(self):
        self.wait()
        total = self.got3[0].astype(F32)
        for z in range(1, self.nz):
            total += self.got3[z].astype(F32)
        own = self.rows(self.at + self.n * HALF + self.xy * self.plane, self.plane)
        self.whole[own, :] = total.astype(BF16)
        own = self.whole.at[own]
        self.copies = [send(own, own, self.pair(self.sem4, d), peer) for d, peer in enumerate(self.in_plane)]
        self.across = [send(own, own, self.pair(self.sem5, self.nxy - 1), self.partner)]

    def cores_back(self):
        for d, copy in enumerate(self.copies):
            copy.wait()
            got = self.whole.at[self.rows(self.at + self.n * HALF + self.origin[d] * self.plane, self.plane)]
            self.across.append(send(got, got, self.pair(self.sem5, d), self.partner))

    def end(self):
        for copy in self.across:
            copy.wait()


def sum_scratch(nz, nxy):
    plane = HALF // nxy
    sems = [pltpu.SemaphoreType.DMA((2, count)) for count in (1, nxy - 1, nz - 1, nxy - 1, nxy)]
    return [
        pltpu.VMEM((HALF, L), BF16),
        pltpu.VMEM((HALF, L), F32),
        pltpu.VMEM((nxy - 1, plane, L), BF16),
        pltpu.VMEM((nz, plane, L), BF16),
    ] + sems


def main_kernel(nz, nxy, slots, plan, far_features, far_occupancy, far_out_grad, far_weights1, far_weights2,
                output, feature_grad, reduced,
                table, shifted, columns, side, back, around, padded, middle, low, high, planes, edges, faces, grads,
                mask, slope, chosen, shell, masked, pre, sums, packed1, packed2, features, occupancy, out_grad, weights1, weights2,
                messages, near, hidden_shells, hidden_near,
                out1, got1, joined1, arrived1, out2, got2, joined2, arrived2,
                near_sems, hidden_sems, back_sems1, back_sems2, load_sems, *scratch):
    n_wide = nz * nxy
    n = lax.axis_index("narrow")
    actives = Shells(n_wide, near, near_sems)
    hiddens = Shells(n_wide, hidden_near, hidden_sems)
    returns1 = Returns(n_wide, out1, got1, joined1, arrived1, back_sems1)
    returns2 = Returns(n_wide, out2, got2, joined2, arrived2, back_sems2)
    total1 = Sum(nz, nxy, packed1, reduced, 0, scratch[: len(scratch) // 2])
    total2 = Sum(nz, nxy, packed2, reduced, ROWS, scratch[len(scratch) // 2 :])
    everyone = [actives.peers[0], actives.peers[2]] + total1.peers()
    greet(everyone)
    far = (far_occupancy, far_features, far_out_grad, far_weights2, far_weights1)
    loads = []
    for i, (source, dest) in enumerate(zip(far, (occupancy, features, out_grad, weights2, weights1))):
        loads.append(pltpu.make_async_copy(source, dest, load_sems.at[i]))
        loads[i].start()
    loads[0].wait()
    loads[1].wait()

    for t in range(B):
        seen = occupancy[t : t + 1, :].astype(F32)
        table[t] = to_rows(features[t].astype(F32) * seen).reshape(8, 8, 8, L)
    row = lax.broadcasted_iota(jnp.int32, (16, L), 0)
    for t in range(B):
        pack_own(table, shell, messages.at[0], t)
    for g in range(3):
        if g > 0:
            messages[g, 0 : 2 * TIGHT] = messages[0, 0 : 2 * TIGHT]
        rows = jnp.zeros((16, L), F32)
        for i in range(4):
            rows = jnp.where(row == i, plan[i, g].astype(F32), rows)
        messages[g, 2 * TIGHT : MESSAGE] = rows.astype(BF16)
    pl.semaphore_wait(pltpu.get_barrier_semaphore(), len(everyone))
    for t in range(B):
        actives.start([messages.at[g] for g in range(3)], t)

    loads[2].wait()
    padded[...] = jnp.zeros_like(padded)
    masked[C:L] = jnp.zeros((L - C, B * V), BF16)
    for t in range(B):
        seen = occupancy[t : t + 1, :].astype(F32)
        mask[t] = jnp.broadcast_to(seen, (L, V)).T
        own = out_grad[t].astype(F32) * seen
        masked[0:C, t * V : (t + 1) * V] = own.astype(BF16)
        padded[t, 2:10, 2:10] = to_rows(own).reshape(8, 8, 8, L)

    def transpose(weights):
        back_weights(weights, back)
        faces[...] = jnp.zeros_like(faces)

        def one(t, carry):
            spread(t, padded, around, back, middle, low, high, planes, edges)
            scatter(t, slots, middle, planes, edges, faces)
            grads[t] = middle[1:9, 1:9]
            return carry

        lax.fori_loop(0, B, one, 0)
        for t in range(B):
            add_faces(faces[t], grads, t)

    loads[3].wait()
    transpose(weights2)
    loads[4].wait()
    side_weights(weights1, side)
    table[EMPTY] = jnp.zeros((8, 8, 8, L), F32)
    actives.forward()
    actives.settle()
    for source in range(SLOTS // 2):
        rows = near[source // 2, source % 2, 2 * TIGHT : MESSAGE].astype(F32)
        for c in range(2):
            row = jnp.where(n == 0, rows[c : c + 1], rows[2 + c : 3 + c])
            chosen[2 * source + c] = jnp.broadcast_to(row, (8, L))
    gather_gradients(faces, chosen, out1)
    returns1.start()

    halo_entries(table, near, chosen)
    returns1.join()
    build_columns(slots, table, shifted, columns)
    for t in range(B):
        value = lax.dot_general(
            columns[t * V : (t + 1) * V, :], side[...], (((1,), (1,)), ((), ())), preferred_element_type=F32
        )
        seen = mask[t]
        gate = jax.nn.sigmoid(value)
        table[t] = (value * gate * seen).astype(BF16).astype(F32).reshape(8, 8, 8, L)
        pack_own(table, shell, hidden_shells, t)
        hiddens.start([hidden_shells] * 3, t)
        slope[t] = seen * gate * (1.0 + value * (1.0 - gate))
    side_weights(weights2, side)
    returns1.add(grads)
    for t in range(B):
        grad = grads[t].reshape(V, L) * slope[t]
        padded[t, 2:10, 2:10] = grad.reshape(8, 8, 8, L)
        pre[:, t * V : (t + 1) * V] = grad.T.astype(BF16)
    weight_sums(pre, columns, sums)
    pack_sums(sums, packed1, 0)
    total1.cores()

    hiddens.forward()
    total1.planes()
    hiddens.settle()
    halo_entries(table, hidden_near, chosen)
    build_columns(slots, table, shifted, columns)
    weight_sums(masked, columns, sums)
    pack_sums(sums, packed2, 0)
    total2.cores()

    def forward(t):
        seen = occupancy[t : t + 1, :].astype(F32)
        value = lax.dot_general(
            side[...], columns[t * V : (t + 1) * V, :], (((1,), (1,)), ((), ())), preferred_element_type=F32
        )
        output[t] = ((features[t].astype(F32) * seen + value[0:C]) * seen).astype(BF16)

    forward(0)
    total2.planes()
    total1.column()
    transpose(weights1)
    gather_gradients(faces, chosen, out2)
    returns2.start()
    total2.column()
    returns2.join()
    forward(1)
    total1.planes_back()
    total2.planes_back()
    returns2.add(grads)
    for t in range(B):
        seen = occupancy[t : t + 1, :].astype(F32)
        own = grads[t].reshape(V, L).T
        feature_grad[t] = ((out_grad[t].astype(F32) * seen + own[0:C]) * seen).astype(BF16)
    total1.cores_back()
    total2.cores_back()
    total1.end()
    total2.end()


VMEM_SPEC = pl.BlockSpec(memory_space=pltpu.VMEM)
SMEM_SPEC = pl.BlockSpec(memory_space=pltpu.SMEM)
ANY_SPEC = pl.BlockSpec(memory_space=pl.ANY)


def shape(dims, dtype):
    return jax.ShapeDtypeStruct(dims, dtype)


BLOCK = (8, 8, 8, L)
SCRATCH = [
    ((EMPTY + 1,) + BLOCK, F32),
    ((3, 10, 10, 8, L), F32),
    ((B * V, 27 * L), BF16),
    ((L, 27 * L), BF16),
    ((9 * L, 3 * L), BF16),
    ((800, 9 * L), BF16),
    ((B, 12, 12, 8, L), F32),
    ((10, 10, 8, L), F32),
    ((10, 10, 8, L), F32),
    ((10, 10, 8, L), F32),
    ((2, 10, 8, L), F32),
    ((2, 2, 10, 8, L), F32),
    ((EMPTY, FACES // 8, 8, L), F32),
    ((B,) + BLOCK, F32),
    ((B, V, L), F32),
    ((B, V, L), F32),
    ((SLOTS, 8, L), F32),
    ((SHELL // 8, 8, L), F32),
    ((L, B * V), BF16),
    ((L, B * V), BF16),
    ((WG, L), F32),
    ((ROWS, L), F32),
    ((ROWS, L), F32),
    ((B, C, V), BF16),
    ((B, V), jnp.int32),
    ((B, C, V), BF16),
    ((27, C, C), BF16),
    ((27, C, C), BF16),
    ((3, MESSAGE, L), BF16),
    ((3, 2, MESSAGE, L), BF16),
    ((2 * TIGHT, L), BF16),
    ((3, 2, 2 * TIGHT, L), BF16),
] + 2 * [
    ((3, 2, 2 * TIGHT_FACES, L), BF16),
    ((2, 2 * TIGHT_FACES, L), BF16),
    ((2, 2 * TIGHT_FACES, L), BF16),
    ((3, 2 * TIGHT_FACES, L), BF16),
]


def local(nz, nxy, features, occupancy, conv1_weight, conv2_weight, out_grad, slots, send_blocks):
    dma = pltpu.SemaphoreType.DMA
    blocks = shape((B, C, V), BF16)
    output, feature_grad, reduced = pl.pallas_call(
        functools.partial(main_kernel, nz, nxy),
        out_shape=[blocks, blocks, shape((2 * ROWS, L), BF16)],
        in_specs=[SMEM_SPEC] * 2 + [ANY_SPEC] * 5,
        out_specs=[VMEM_SPEC] * 3,
        scratch_shapes=[pltpu.VMEM(dims, dtype) for dims, dtype in SCRATCH]
        + [dma((2, 2, 6)), dma((2, 2, 6)), dma((2, 5)), dma((2, 5)), dma((5,))] + 2 * sum_scratch(nz, nxy),
        compiler_params=pltpu.CompilerParams(
            collective_id=0, has_side_effects=True, vmem_limit_bytes=VMEM_LIMIT
        ),
    )(slots, send_blocks.reshape(3, 4).T, features, occupancy, out_grad, conv1_weight, conv2_weight)
    scale = (B * V * 2 * nz * nxy) ** -0.5
    return pl.pallas_call(
        functools.partial(last_kernel, scale),
        out_shape=[blocks, blocks] + [shape((27, C, C), F32)] * 2,
        in_specs=[VMEM_SPEC] * 3,
        out_specs=[VMEM_SPEC] * 4,
        compiler_params=pltpu.CompilerParams(vmem_limit_bytes=VMEM_LIMIT),
    )(reduced, output, feature_grad)


def solution(mesh):
    both = ("wide", "narrow")
    n_wide = mesh.shape["wide"]
    nxy = 16 if n_wide % 16 == 0 else n_wide // 2
    return jax.shard_map(
        functools.partial(local, n_wide // nxy, nxy),
        mesh=mesh,
        in_specs=(P(both, None, None), P(both, None), P(), P(), P(both, None, None), P(both, None),
                  P(both, None, None, None)),
        out_specs=(P(both, None, None), P(both, None, None), P(), P()),
        check_vma=False,
    )
```

```python
import functools

import jax
import jax.numpy as jnp
from jax import lax
from jax.experimental import pallas as pl
from jax.experimental.pallas import tpu as pltpu
from jax.sharding import PartitionSpec as P

MESH = pl.DeviceIdType.MESH
F32 = jnp.float32
BF16 = jnp.bfloat16
C = 96
L = 128
V = 512
B = 2
SLOTS = 12
EMPTY = 14
SHELL = 320
TIGHT = SHELL * 3 // 4
OFFSETS = [(a, b, e) for a in (-1, 0, 1) for b in (-1, 0, 1) for e in (-1, 0, 1)]
PAIRS = [(a, b) for a in (-1, 0, 1) for b in (-1, 0, 1)]
PLACE = {-1: slice(0, 1), 0: slice(1, 9), 1: slice(9, 10)}
LAYER = {-1: slice(7, 8), 0: slice(0, 8), 1: slice(0, 1)}
HALF = 1024
ROWS = 2 * HALF
WG = 27 * C
QUARTER = WG // 4
MESSAGE = 2 * TIGHT + 16
FACES = 384
TIGHT_FACES = FACES * 3 // 4
VMEM_LIMIT = 44 * 1024 * 1024
LAST_LIMIT = 12 * 1024 * 1024


def direction(a, b, e):
    return 9 * (a + 1) + 3 * (b + 1) + e + 1


def depth_index(shape):
    return lax.broadcasted_iota(jnp.int32, shape, len(shape) - 2)


def roll_depth(value, shift):
    return pltpu.roll(value, shift % 8, value.ndim - 2)


def to_rows(value):
    wide = jnp.concatenate([value, jnp.zeros((L - C, V), F32)], axis=0)
    return wide.T


def squeeze(rows):
    q = rows.shape[0] // 4
    lane = lax.broadcasted_iota(jnp.int32, (q, L), 1)
    last = rows[3 * q :]
    parts = [jnp.where(lane < C, rows[i * q : (i + 1) * q], pltpu.roll(last, C - 32 * i, 1)) for i in range(3)]
    return jnp.concatenate(parts, axis=0)


def stretch(rows):
    q = rows.shape[0] // 3
    lane = lax.broadcasted_iota(jnp.int32, (q, L), 1)
    parts, last = [], jnp.zeros((q, L), F32)
    for i in range(3):
        part = rows[i * q : (i + 1) * q]
        parts.append(jnp.where(lane < C, part, 0.0))
        last = jnp.where(lane // 32 == i, pltpu.roll(part, 32 + 32 * i, 1), last)
    return jnp.concatenate(parts + [last], axis=0)


def pack_shell(table, entry, shell):
    shell[0:8] = table[entry, 0]
    shell[8:16] = table[entry, 7]
    shell[16:22] = table[entry, 1:7, 0]
    shell[22:28] = table[entry, 1:7, 7]
    for at, z in ((28, 0), (34, 7)):
        shell[at : at + 6] = table[entry, 1:7, :, z, :]
    return squeeze(shell[...].reshape(SHELL, L)).astype(BF16)


def unpack_shell(shell, table, entry):
    table[entry, 0] = shell[0:8]
    table[entry, 7] = shell[8:16]
    table[entry, 1:7, 0] = shell[16:22]
    table[entry, 1:7, 7] = shell[22:28]
    table[entry, 1:7, :, 0, :] = shell[28:34]
    table[entry, 1:7, :, 7, :] = shell[34:40]


def add_faces(faces, grads, t):
    grads[t, 0] += faces[0:8]
    grads[t, 7] += faces[8:16]
    grads[t, :, 0] += faces[16:24]
    grads[t, :, 7] += faces[24:32]
    grads[t, :, :, 0, :] += faces[32:40]
    grads[t, :, :, 7, :] += faces[40:48]


def pack_own(table, shell, out, t):
    out[t * TIGHT : (t + 1) * TIGHT] = pack_shell(table, t, shell)


def gather_gradients(faces, chosen, out):
    for g in range(3):
        for m in range(2):
            for t in range(B):
                total = 0.0
                for c in range(2):
                    slot = 4 * g + 2 * m + c
                    total += jnp.where(chosen[slot] == float(t), faces[B + slot], 0.0)
                out[g, m, t * TIGHT_FACES : (t + 1) * TIGHT_FACES] = squeeze(total.reshape(FACES, L)).astype(BF16)


def halo_entries(table, halo, chosen):
    for source in range(SLOTS // 2):
        blocks = []
        for t in range(B):
            rows = halo[source // 2, source % 2, t * TIGHT : (t + 1) * TIGHT].astype(F32)
            blocks.append(stretch(rows).reshape(SHELL // 8, 8, L))
        for c in range(2):
            slot = 2 * source + c
            unpack_shell(jnp.where(chosen[slot] == 0.0, blocks[0], blocks[1]), table, B + slot)


def build_columns(slots, table, shifted, columns):
    def one(t, carry):
        for a, b in PAIRS:
            def source(e):
                return table[slots[t, direction(a, b, e)], LAYER[a], LAYER[b]]

            here = source(0)
            z = depth_index(here.shape)
            shifted[1, PLACE[a], PLACE[b]] = here
            shifted[0, PLACE[a], PLACE[b]] = roll_depth(jnp.where(z == 7, source(-1), here), 1)
            shifted[2, PLACE[a], PLACE[b]] = roll_depth(jnp.where(z == 0, source(1), here), -1)
        rows = pl.ds(pl.multiple_of(t * V, V), V)
        for o, (a, b, e) in enumerate(OFFSETS):
            part = shifted[e + 1, a + 1 : a + 9, b + 1 : b + 9]
            columns[rows, o * L : (o + 1) * L] = part.reshape(V, L).astype(BF16)
        return carry

    lax.fori_loop(0, B, one, 0)


def side_weights(weights, side):
    side[...] = jnp.zeros_like(side)
    for o in range(27):
        side[0:C, o * L : o * L + C] = weights[o]


def back_weights(weights, back):
    back[...] = jnp.zeros_like(back)
    for o in range(27):
        k, e = o // 3, o % 3
        back[k * L : k * L + C, e * L : e * L + C] = weights[o]


def spread(t, padded, around, back, middle, low, high, planes, edges):
    for k, (a, b) in enumerate(PAIRS):
        part = padded[t, 1 - a : 11 - a, 1 - b : 11 - b]
        around[:, k * L : (k + 1) * L] = part.reshape(800, L).astype(BF16)
    by_depth = jnp.dot(around[...], back[...], preferred_element_type=F32).reshape(10, 10, 8, 3 * L)
    low[...] = by_depth[..., 0:L]
    high[...] = by_depth[..., 2 * L : 3 * L]
    down = roll_depth(low[...], -1)
    up = roll_depth(high[...], 1)
    z = depth_index(up.shape)
    middle[...] = by_depth[..., L : 2 * L] + jnp.where(z != 0, up, 0.0) + jnp.where(z != 7, down, 0.0)
    y = depth_index((10, 8, L))
    for i, (source, at) in enumerate(((low, 0), (high, 7))):
        planes[i] = source[:, 1:9, at, :]
        for j, (column, row) in enumerate(((0, 7), (9, 0))):
            edge = source[:, column, at : at + 1, :]
            edges[i, j] = jnp.where(y == row, edge, 0.0)


def scatter(t, slots, middle, planes, edges, faces):
    def one(entry, carry):
        def weight(a, b, e):
            return (slots[t, direction(a, b, e)] == entry).astype(F32)

        for x, (a, px) in ((0, (1, 9)), (8, (-1, 0))):
            faces[entry, x : x + 8] += weight(a, 0, 0) * middle[px, 1:9]
            faces[entry, x] += weight(a, 1, 0) * middle[px, 9]
            faces[entry, x + 7] += weight(a, -1, 0) * middle[px, 0]
        faces[entry, 16:24] += weight(0, 1, 0) * middle[1:9, 9]
        faces[entry, 24:32] += weight(0, -1, 0) * middle[1:9, 0]
        for at, e, i in ((32, 1, 1), (40, -1, 0)):
            for a, x, px in ((0, slice(at, at + 8), slice(1, 9)), (1, at, 9), (-1, at + 7, 0)):
                total = weight(a, 0, e) * planes[i, px]
                total += weight(a, -1, e) * edges[i, 0, px] + weight(a, 1, e) * edges[i, 1, px]
                faces[entry, x] += total
        return carry

    lax.fori_loop(0, EMPTY, one, 0)


def weight_sums(left, columns, out):
    for o in range(0, 27, 3):
        sums = jnp.dot(left[...], columns[:, o * L : (o + 3) * L], preferred_element_type=F32)
        for i in range(3):
            row = (o + i) * C
            out[row : row + C] = sums[0:C, i * L : (i + 1) * L]


def pack_sums(sums, packed, at):
    last = sums[3 * QUARTER : WG]
    lane = lax.broadcasted_iota(jnp.int32, (QUARTER, L), 1)
    for i in range(3):
        moved = pltpu.roll(last, C - 32 * i, 1)
        rows = slice(i * QUARTER, (i + 1) * QUARTER)
        packed[at + i * QUARTER : at + (i + 1) * QUARTER] = jnp.where(lane < C, sums[rows], moved)
    packed[at + 3 * QUARTER : at + ROWS] = jnp.zeros((ROWS - 3 * QUARTER, L), F32)


def last_kernel(scale, packed, output, grad, output_out, grad_out, first, second):
    output_out[...] = output[...]
    grad_out[...] = grad[...]
    lane = lax.broadcasted_iota(jnp.int32, (QUARTER, L), 1)
    for i, out in enumerate((first, second)):
        whole = packed[i * ROWS : (i + 1) * ROWS].astype(F32) * scale
        last = jnp.zeros((QUARTER, L), F32)
        for k in range(3):
            part = whole[k * QUARTER : (k + 1) * QUARTER]
            last = jnp.where(lane // 32 == k, pltpu.roll(part, 32 + 32 * k, 1), last)
        for r in range(0, WG, 24):
            part = whole[r : r + 24] if r < 3 * QUARTER else last[r - 3 * QUARTER : r - 3 * QUARTER + 24]
            out[r // C, r % C : r % C + 24, :] = part[:, 0:C]


def send(source, dest, sems, peer):
    copy = pltpu.make_async_remote_copy(
        src_ref=source, dst_ref=dest, send_sem=sems[0], recv_sem=sems[1], device_id=peer, device_id_type=MESH
    )
    copy.start()
    return copy


def greet(peers):
    barrier = pltpu.get_barrier_semaphore()
    for peer in peers:
        pl.semaphore_signal(barrier, inc=1, device_id=peer, device_id_type=MESH)


def neighbours(n_wide):
    w, n = lax.axis_index("wide"), lax.axis_index("narrow")
    ahead, behind = lax.rem(w + 1, n_wide), lax.rem(w + n_wide - 1, n_wide)
    return w, n, ahead, behind


class Shells:
    def __init__(self, n_wide, halo, sems):
        self.w, self.n, ahead, behind = neighbours(n_wide)
        self.partner = (self.w, 1 - self.n)
        self.peers = [(behind, self.n), self.partner, (ahead, self.n)]
        self.halo, self.sems, self.copies = halo, sems, {}

    def pair(self, k, i):
        return self.sems.at[0, k, i], self.sems.at[1, k, i]

    def rows(self, k):
        return pl.ds(k * TIGHT, TIGHT if k == 0 else self.halo.shape[2] - TIGHT)

    def start(self, sources, k):
        self.copies[k] = [
            send(sources[g].at[self.rows(k)], self.halo.at[g, self.n, self.rows(k)], self.pair(k, g), self.peers[g])
            for g in range(3)
        ]

    def forward(self):
        self.across = []
        for k in range(B):
            for g in (0, 2):
                self.copies[k][g].wait()
                got = self.halo.at[g, self.n, self.rows(k)]
                self.across.append(send(got, got, self.pair(k, 3 + g), self.partner))

    def settle(self):
        for k in range(B):
            self.copies[k][1].wait()
        for copy in self.across:
            copy.wait()


class Returns:
    def __init__(self, n_wide, out, got, joined, arrived, sems):
        self.w, self.n, ahead, behind = neighbours(n_wide)
        self.partner = (self.w, 1 - self.n)
        self.to = {0: (ahead, self.n), 2: (behind, self.n)}
        self.out, self.got, self.joined, self.arrived, self.sems = out, got, joined, arrived, sems

    def pair(self, i):
        return self.sems.at[0, i], self.sems.at[1, i]

    def start(self):
        self.joins = [
            send(self.out.at[g, 1 - self.n], self.got.at[i], self.pair(i), self.partner) for i, g in enumerate((0, 2))
        ]
        self.backs = [send(self.out.at[1, 1 - self.n], self.arrived.at[1], self.pair(2), self.partner)]

    def join(self):
        for i, g in enumerate((0, 2)):
            self.joins[i].wait()
            self.joined[i] = (self.out[g, self.n].astype(F32) + self.got[i].astype(F32)).astype(BF16)
            self.backs.append(send(self.joined.at[i], self.arrived.at[g], self.pair(3 + i), self.to[g]))

    def add(self, grads):
        for copy in self.backs:
            copy.wait()
        for t in range(B):
            for g in range(3):
                faces = stretch(self.arrived[g, t * TIGHT_FACES : (t + 1) * TIGHT_FACES].astype(F32))
                add_faces(faces.reshape(FACES // 8, 8, L), grads, t)


class Sum:
    def __init__(self, nz, nxy, src, whole, at, scratch):
        self.nz, self.nxy, self.src, self.whole, self.at = nz, nxy, src, whole, at
        (self.half, self.got1, self.got2, self.got3,
         self.sem1, self.sem2, self.sem3, self.sem4, self.sem5) = scratch
        w, self.n = lax.axis_index("wide"), lax.axis_index("narrow")
        self.z, self.xy = w // nxy, lax.rem(w, nxy)
        self.plane = HALF // nxy
        self.partner = (w, 1 - self.n)
        nx = 4 if nxy % 4 == 0 else nxy
        ny = nxy // nx
        x, y = lax.rem(self.xy, nx), self.xy // nx

        def place(dx, dy):
            return lax.rem(y + dy + ny, ny) * nx + lax.rem(x + dx + nx, nx)

        def hops(step, size):
            return min(step, size - step)

        steps = [(dx, dy) for dx in range(nx) for dy in range(ny) if dx or dy]
        steps.sort(key=lambda step: -hops(step[0], nx) - hops(step[1], ny))
        self.to = [place(dx, dy) for dx, dy in steps]
        self.origin = [place(-dx, -dy) for dx, dy in steps]
        self.in_plane = [(self.z * nxy + to, self.n) for to in self.to]
        rises = sorted(range(1, nz), key=lambda rise: -hops(rise, nz))
        self.in_column = [(lax.rem(self.z + rise, nz) * nxy + self.xy, self.n) for rise in rises]

    def peers(self):
        return self.in_column + self.in_plane + [self.partner]

    def rows(self, at, size):
        return pl.ds(pl.multiple_of(at, size), size)

    def pair(self, sems, d):
        return sems.at[0, d], sems.at[1, d]

    def cores(self):
        theirs = self.src.at[self.rows((1 - self.n) * HALF, HALF)]
        self.copies = [send(theirs, self.got1, self.pair(self.sem1, 0), self.partner)]

    def wait(self):
        for copy in self.copies:
            copy.wait()

    def planes(self):
        self.wait()
        mine = self.src[self.rows(self.n * HALF, HALF), :]
        self.half[...] = (mine + self.got1[...]).astype(BF16)
        self.copies = []
        for d, peer in enumerate(self.in_plane):
            part = self.half.at[self.rows(self.to[d] * self.plane, self.plane)]
            self.copies.append(send(part, self.got2.at[d], self.pair(self.sem2, d), peer))

    def column(self):
        self.wait()
        total = self.half[self.rows(self.xy * self.plane, self.plane), :].astype(F32)
        for d in range(self.nxy - 1):
            total += self.got2[d].astype(F32)
        own = self.got3.at[self.z]
        own[...] = total.astype(BF16)
        self.copies = [send(own, own, self.pair(self.sem3, d), peer) for d, peer in enumerate(self.in_column)]

    def planes_back(self):
        self.wait()
        total = self.got3[0].astype(F32)
        for z in range(1, self.nz):
            total += self.got3[z].astype(F32)
        own = self.rows(self.at + self.n * HALF + self.xy * self.plane, self.plane)
        self.whole[own, :] = total.astype(BF16)
        own = self.whole.at[own]
        self.copies = [send(own, own, self.pair(self.sem4, d), peer) for d, peer in enumerate(self.in_plane)]
        self.across = [send(own, own, self.pair(self.sem5, self.nxy - 1), self.partner)]

    def cores_back(self):
        for d, copy in enumerate(self.copies):
            copy.wait()
            got = self.whole.at[self.rows(self.at + self.n * HALF + self.origin[d] * self.plane, self.plane)]
            self.across.append(send(got, got, self.pair(self.sem5, d), self.partner))

    def end(self):
        for copy in self.across:
            copy.wait()


def sum_scratch(nz, nxy):
    plane = HALF // nxy
    sems = [pltpu.SemaphoreType.DMA((2, count)) for count in (1, nxy - 1, nz - 1, nxy - 1, nxy)]
    return [
        pltpu.VMEM((HALF, L), BF16),
        pltpu.VMEM((HALF, L), F32),
        pltpu.VMEM((nxy - 1, plane, L), BF16),
        pltpu.VMEM((nz, plane, L), BF16),
    ] + sems


def main_kernel(nz, nxy, far_slots, far_plan, far_features, far_occupancy, far_out_grad, far_weights1, far_weights2,
                output, feature_grad, reduced,
                table, shifted, columns, side, back, around, padded, middle, low, high, planes, edges, faces, grads,
                mask, slope, chosen, shell, masked, pre, sums, packed1, packed2, features, occupancy, out_grad, weights1, weights2,
                messages, near, hidden_shells, hidden_near,
                out1, got1, joined1, arrived1, out2, got2, joined2, arrived2,
                near_sems, hidden_sems, back_sems1, back_sems2, load_sems, slots, plan, *scratch):
    n_wide = nz * nxy
    n = lax.axis_index("narrow")
    actives = Shells(n_wide, near, near_sems)
    hiddens = Shells(n_wide, hidden_near, hidden_sems)
    returns1 = Returns(n_wide, out1, got1, joined1, arrived1, back_sems1)
    returns2 = Returns(n_wide, out2, got2, joined2, arrived2, back_sems2)
    total1 = Sum(nz, nxy, packed1, reduced, 0, scratch[: len(scratch) // 2])
    total2 = Sum(nz, nxy, packed2, reduced, ROWS, scratch[len(scratch) // 2 :])
    everyone = total1.peers() + [actives.peers[0], actives.peers[2]]
    greet(everyone)
    far = (far_occupancy, far_features, far_plan, far_out_grad, far_weights2, far_slots, far_weights1)
    loads = []
    for i, (source, dest) in enumerate(zip(far, (occupancy, features, plan, out_grad, weights2, slots, weights1))):
        loads.append(pltpu.make_async_copy(source, dest, load_sems.at[i]))
        loads[i].start()
    loads[0].wait()
    loads[1].wait()

    for t in range(B):
        seen = occupancy[t : t + 1, :].astype(F32)
        table[t] = to_rows(features[t].astype(F32) * seen).reshape(8, 8, 8, L)
    row = lax.broadcasted_iota(jnp.int32, (16, L), 0)
    loads[2].wait()
    for t in range(B):
        pack_own(table, shell, messages.at[0], t)
    for g in range(3):
        if g > 0:
            messages[g, 0 : 2 * TIGHT] = messages[0, 0 : 2 * TIGHT]
        rows = jnp.zeros((16, L), F32)
        for i in range(4):
            rows = jnp.where(row == i, plan[i, g].astype(F32), rows)
        messages[g, 2 * TIGHT : MESSAGE] = rows.astype(BF16)
    pl.semaphore_wait(pltpu.get_barrier_semaphore(), len(everyone))
    for t in range(B):
        actives.start([messages.at[g] for g in range(3)], t)

    loads[3].wait()
    padded[...] = jnp.zeros_like(padded)
    masked[C:L] = jnp.zeros((L - C, B * V), BF16)
    for t in range(B):
        seen = occupancy[t : t + 1, :].astype(F32)
        mask[t] = jnp.broadcast_to(seen, (L, V)).T
        own = out_grad[t].astype(F32) * seen
        masked[0:C, t * V : (t + 1) * V] = own.astype(BF16)
        padded[t, 2:10, 2:10] = to_rows(own).reshape(8, 8, 8, L)

    def transpose(weights):
        back_weights(weights, back)
        faces[...] = jnp.zeros_like(faces)

        def one(t, carry):
            spread(t, padded, around, back, middle, low, high, planes, edges)
            scatter(t, slots, middle, planes, edges, faces)
            grads[t] = middle[1:9, 1:9]
            return carry

        lax.fori_loop(0, B, one, 0)
        for t in range(B):
            add_faces(faces[t], grads, t)

    loads[4].wait()
    loads[5].wait()
    transpose(weights2)
    loads[6].wait()
    side_weights(weights1, side)
    table[EMPTY] = jnp.zeros((8, 8, 8, L), F32)
    actives.forward()
    actives.settle()
    for source in range(SLOTS // 2):
        rows = near[source // 2, source % 2, 2 * TIGHT : MESSAGE].astype(F32)
        for c in range(2):
            row = jnp.where(n == 0, rows[c : c + 1], rows[2 + c : 3 + c])
            chosen[2 * source + c] = jnp.broadcast_to(row, (8, L))
    gather_gradients(faces, chosen, out1)
    returns1.start()

    halo_entries(table, near, chosen)
    build_columns(slots, table, shifted, columns)
    returns1.join()
    for t in range(B):
        value = lax.dot_general(
            columns[t * V : (t + 1) * V, :], side[...], (((1,), (1,)), ((), ())), preferred_element_type=F32
        )
        seen = mask[t]
        gate = jax.nn.sigmoid(value)
        table[t] = (value * gate * seen).astype(BF16).astype(F32).reshape(8, 8, 8, L)
        pack_own(table, shell, hidden_shells, t)
        hiddens.start([hidden_shells] * 3, t)
        slope[t] = seen * gate * (1.0 + value * (1.0 - gate))
    side_weights(weights2, side)
    returns1.add(grads)
    for t in range(B):
        grad = grads[t].reshape(V, L) * slope[t]
        padded[t, 2:10, 2:10] = grad.reshape(8, 8, 8, L)
        pre[:, t * V : (t + 1) * V] = grad.T.astype(BF16)
    weight_sums(pre, columns, sums)
    pack_sums(sums, packed1, 0)
    total1.cores()

    hiddens.forward()
    total1.planes()
    hiddens.settle()
    halo_entries(table, hidden_near, chosen)
    build_columns(slots, table, shifted, columns)
    weight_sums(masked, columns, sums)
    pack_sums(sums, packed2, 0)
    total2.cores()

    def forward(t):
        seen = occupancy[t : t + 1, :].astype(F32)
        value = lax.dot_general(
            side[...], columns[t * V : (t + 1) * V, :], (((1,), (1,)), ((), ())), preferred_element_type=F32
        )
        output[t] = ((features[t].astype(F32) * seen + value[0:C]) * seen).astype(BF16)

    forward(0)
    total2.planes()
    total1.column()
    transpose(weights1)
    gather_gradients(faces, chosen, out2)
    returns2.start()
    total2.column()
    returns2.join()
    forward(1)
    total1.planes_back()
    total2.planes_back()
    returns2.add(grads)
    for t in range(B):
        seen = occupancy[t : t + 1, :].astype(F32)
        own = grads[t].reshape(V, L).T
        feature_grad[t] = ((out_grad[t].astype(F32) * seen + own[0:C]) * seen).astype(BF16)
    total1.cores_back()
    total2.cores_back()
    total1.end()
    total2.end()


VMEM_SPEC = pl.BlockSpec(memory_space=pltpu.VMEM)
HBM_SPEC = pl.BlockSpec(memory_space=pltpu.HBM)


def shape(dims, dtype):
    return jax.ShapeDtypeStruct(dims, dtype)


BLOCK = (8, 8, 8, L)
SCRATCH = [
    ((EMPTY + 1,) + BLOCK, F32),
    ((3, 10, 10, 8, L), F32),
    ((B * V, 27 * L), BF16),
    ((L, 27 * L), BF16),
    ((9 * L, 3 * L), BF16),
    ((800, 9 * L), BF16),
    ((B, 12, 12, 8, L), F32),
    ((10, 10, 8, L), F32),
    ((10, 10, 8, L), F32),
    ((10, 10, 8, L), F32),
    ((2, 10, 8, L), F32),
    ((2, 2, 10, 8, L), F32),
    ((EMPTY, FACES // 8, 8, L), F32),
    ((B,) + BLOCK, F32),
    ((B, V, L), F32),
    ((B, V, L), F32),
    ((SLOTS, 8, L), F32),
    ((SHELL // 8, 8, L), F32),
    ((L, B * V), BF16),
    ((L, B * V), BF16),
    ((WG, L), F32),
    ((ROWS, L), F32),
    ((ROWS, L), F32),
    ((B, C, V), BF16),
    ((B, V), jnp.int32),
    ((B, C, V), BF16),
    ((27, C, C), BF16),
    ((27, C, C), BF16),
    ((3, MESSAGE, L), BF16),
    ((3, 2, MESSAGE, L), BF16),
    ((2 * TIGHT, L), BF16),
    ((3, 2, 2 * TIGHT, L), BF16),
] + 2 * [
    ((3, 2, 2 * TIGHT_FACES, L), BF16),
    ((2, 2 * TIGHT_FACES, L), BF16),
    ((2, 2 * TIGHT_FACES, L), BF16),
    ((3, 2 * TIGHT_FACES, L), BF16),
]


def local(nz, nxy, features, occupancy, conv1_weight, conv2_weight, out_grad, slots, send_blocks):
    dma = pltpu.SemaphoreType.DMA
    blocks = shape((B, C, V), BF16)
    inputs = (slots, send_blocks.reshape(3, 4).T, features, occupancy, out_grad, conv1_weight, conv2_weight)
    output, feature_grad, reduced = pl.pallas_call(
        functools.partial(main_kernel, nz, nxy),
        out_shape=[blocks, blocks, shape((2 * ROWS, L), BF16)],
        in_specs=[HBM_SPEC] * 7,
        out_specs=[VMEM_SPEC] * 3,
        scratch_shapes=[pltpu.VMEM(dims, dtype) for dims, dtype in SCRATCH]
        + [dma((2, 2, 6)), dma((2, 2, 6)), dma((2, 5)), dma((2, 5)), dma((7,)), pltpu.SMEM((B, 27), jnp.int32), pltpu.SMEM((4, 3), jnp.int32)] + 2 * sum_scratch(nz, nxy),
        compiler_params=pltpu.CompilerParams(
            collective_id=0, has_side_effects=True, vmem_limit_bytes=VMEM_LIMIT
        ),
    )(*(pltpu.with_memory_space_constraint(x, pltpu.HBM) for x in inputs))
    scale = (B * V * 2 * nz * nxy) ** -0.5
    return pl.pallas_call(
        functools.partial(last_kernel, scale),
        out_shape=[blocks, blocks] + [shape((27, C, C), F32)] * 2,
        in_specs=[VMEM_SPEC] * 3,
        out_specs=[VMEM_SPEC] * 4,
        compiler_params=pltpu.CompilerParams(vmem_limit_bytes=LAST_LIMIT),
    )(reduced, output, feature_grad)


def solution(mesh):
    both = ("wide", "narrow")
    n_wide = mesh.shape["wide"]
    nxy = 16 if n_wide % 16 == 0 else n_wide // 2
    return jax.shard_map(
        functools.partial(local, n_wide // nxy, nxy),
        mesh=mesh,
        in_specs=(P(both, None, None), P(both, None), P(), P(), P(both, None, None), P(both, None),
                  P(both, None, None, None)),
        out_specs=(P(both, None, None), P(both, None, None), P(), P()),
        check_vma=False,
    )
```

```python
import functools

import jax
import jax.numpy as jnp
from jax import lax
from jax.experimental import pallas as pl
from jax.experimental.pallas import tpu as pltpu
from jax.sharding import PartitionSpec as P

MESH = pl.DeviceIdType.MESH
F32 = jnp.float32
BF16 = jnp.bfloat16
C = 96
L = 128
V = 512
B = 2
SLOTS = 12
EMPTY = 14
SHELL = 320
TIGHT = SHELL * 3 // 4
OFFSETS = [(a, b, e) for a in (-1, 0, 1) for b in (-1, 0, 1) for e in (-1, 0, 1)]
PAIRS = [(a, b) for a in (-1, 0, 1) for b in (-1, 0, 1)]
PLACE = {-1: slice(0, 1), 0: slice(1, 9), 1: slice(9, 10)}
LAYER = {-1: slice(7, 8), 0: slice(0, 8), 1: slice(0, 1)}
HALF = 1024
ROWS = 2 * HALF
WG = 27 * C
QUARTER = WG // 4
MESSAGE = 2 * TIGHT + 16
FACES = 384
TIGHT_FACES = FACES * 3 // 4
VMEM_LIMIT = 44 * 1024 * 1024
LAST_LIMIT = 12 * 1024 * 1024


def direction(a, b, e):
    return 9 * (a + 1) + 3 * (b + 1) + e + 1


def depth_index(shape):
    return lax.broadcasted_iota(jnp.int32, shape, len(shape) - 2)


def roll_depth(value, shift):
    return pltpu.roll(value, shift % 8, value.ndim - 2)


def to_rows(value):
    wide = jnp.concatenate([value, jnp.zeros((L - C, V), F32)], axis=0)
    return wide.T


def squeeze(rows):
    q = rows.shape[0] // 4
    lane = lax.broadcasted_iota(jnp.int32, (q, L), 1)
    last = rows[3 * q :]
    parts = [jnp.where(lane < C, rows[i * q : (i + 1) * q], pltpu.roll(last, C - 32 * i, 1)) for i in range(3)]
    return jnp.concatenate(parts, axis=0)


def stretch(rows):
    q = rows.shape[0] // 3
    lane = lax.broadcasted_iota(jnp.int32, (q, L), 1)
    parts, last = [], jnp.zeros((q, L), F32)
    for i in range(3):
        part = rows[i * q : (i + 1) * q]
        parts.append(jnp.where(lane < C, part, 0.0))
        last = jnp.where(lane // 32 == i, pltpu.roll(part, 32 + 32 * i, 1), last)
    return jnp.concatenate(parts + [last], axis=0)


def pack_shell(table, entry, shell):
    shell[0:8] = table[entry, 0]
    shell[8:16] = table[entry, 7]
    shell[16:22] = table[entry, 1:7, 0]
    shell[22:28] = table[entry, 1:7, 7]
    for at, z in ((28, 0), (34, 7)):
        shell[at : at + 6] = table[entry, 1:7, :, z, :]
    return squeeze(shell[...].reshape(SHELL, L)).astype(BF16)


def unpack_shell(shell, table, entry):
    table[entry, 0] = shell[0:8]
    table[entry, 7] = shell[8:16]
    table[entry, 1:7, 0] = shell[16:22]
    table[entry, 1:7, 7] = shell[22:28]
    table[entry, 1:7, :, 0, :] = shell[28:34]
    table[entry, 1:7, :, 7, :] = shell[34:40]


def add_faces(faces, grads, t):
    grads[t, 0] += faces[0:8]
    grads[t, 7] += faces[8:16]
    grads[t, :, 0] += faces[16:24]
    grads[t, :, 7] += faces[24:32]
    grads[t, :, :, 0, :] += faces[32:40]
    grads[t, :, :, 7, :] += faces[40:48]


def pack_own(table, shell, out, t):
    out[t * TIGHT : (t + 1) * TIGHT] = pack_shell(table, t, shell)


def gather_gradients(faces, chosen, out):
    for g in range(3):
        for m in range(2):
            for t in range(B):
                total = 0.0
                for c in range(2):
                    slot = 4 * g + 2 * m + c
                    total += jnp.where(chosen[slot] == float(t), faces[B + slot], 0.0)
                out[g, m, t * TIGHT_FACES : (t + 1) * TIGHT_FACES] = squeeze(total.reshape(FACES, L)).astype(BF16)


def halo_entries(table, halo, chosen):
    for source in range(SLOTS // 2):
        blocks = []
        for t in range(B):
            rows = halo[source // 2, source % 2, t * TIGHT : (t + 1) * TIGHT].astype(F32)
            blocks.append(stretch(rows).reshape(SHELL // 8, 8, L))
        for c in range(2):
            slot = 2 * source + c
            unpack_shell(jnp.where(chosen[slot] == 0.0, blocks[0], blocks[1]), table, B + slot)


def build_columns(slots, table, shifted, columns):
    def one(t, carry):
        for a, b in PAIRS:
            def source(e):
                return table[slots[t, direction(a, b, e)], LAYER[a], LAYER[b]]

            here = source(0)
            z = depth_index(here.shape)
            shifted[1, PLACE[a], PLACE[b]] = here
            shifted[0, PLACE[a], PLACE[b]] = roll_depth(jnp.where(z == 7, source(-1), here), 1)
            shifted[2, PLACE[a], PLACE[b]] = roll_depth(jnp.where(z == 0, source(1), here), -1)
        rows = pl.ds(pl.multiple_of(t * V, V), V)
        for o, (a, b, e) in enumerate(OFFSETS):
            part = shifted[e + 1, a + 1 : a + 9, b + 1 : b + 9]
            columns[rows, o * L : (o + 1) * L] = part.reshape(V, L).astype(BF16)
        return carry

    lax.fori_loop(0, B, one, 0)


def side_weights(weights, side):
    side[...] = jnp.zeros_like(side)
    for o in range(27):
        side[0:C, o * L : o * L + C] = weights[o]


def back_weights(weights, back):
    back[...] = jnp.zeros_like(back)
    for o in range(27):
        k, e = o // 3, o % 3
        back[k * L : k * L + C, e * L : e * L + C] = weights[o]


def spread(t, padded, around, back, middle, low, high, planes, edges):
    for k, (a, b) in enumerate(PAIRS):
        part = padded[t, 1 - a : 11 - a, 1 - b : 11 - b]
        around[:, k * L : (k + 1) * L] = part.reshape(800, L).astype(BF16)
    by_depth = jnp.dot(around[...], back[...], preferred_element_type=F32).reshape(10, 10, 8, 3 * L)
    low[...] = by_depth[..., 0:L]
    high[...] = by_depth[..., 2 * L : 3 * L]
    down = roll_depth(low[...], -1)
    up = roll_depth(high[...], 1)
    z = depth_index(up.shape)
    middle[...] = by_depth[..., L : 2 * L] + jnp.where(z != 0, up, 0.0) + jnp.where(z != 7, down, 0.0)
    y = depth_index((10, 8, L))
    for i, (source, at) in enumerate(((low, 0), (high, 7))):
        planes[i] = source[:, 1:9, at, :]
        for j, (column, row) in enumerate(((0, 7), (9, 0))):
            edge = source[:, column, at : at + 1, :]
            edges[i, j] = jnp.where(y == row, edge, 0.0)


def scatter(t, slots, middle, planes, edges, faces):
    def one(entry, carry):
        def weight(a, b, e):
            return (slots[t, direction(a, b, e)] == entry).astype(F32)

        for x, (a, px) in ((0, (1, 9)), (8, (-1, 0))):
            faces[entry, x : x + 8] += weight(a, 0, 0) * middle[px, 1:9]
            faces[entry, x] += weight(a, 1, 0) * middle[px, 9]
            faces[entry, x + 7] += weight(a, -1, 0) * middle[px, 0]
        faces[entry, 16:24] += weight(0, 1, 0) * middle[1:9, 9]
        faces[entry, 24:32] += weight(0, -1, 0) * middle[1:9, 0]
        for at, e, i in ((32, 1, 1), (40, -1, 0)):
            for a, x, px in ((0, slice(at, at + 8), slice(1, 9)), (1, at, 9), (-1, at + 7, 0)):
                total = weight(a, 0, e) * planes[i, px]
                total += weight(a, -1, e) * edges[i, 0, px] + weight(a, 1, e) * edges[i, 1, px]
                faces[entry, x] += total
        return carry

    lax.fori_loop(0, EMPTY, one, 0)


def weight_sums(left, columns, out):
    for o in range(0, 27, 3):
        sums = jnp.dot(left[...], columns[:, o * L : (o + 3) * L], preferred_element_type=F32)
        for i in range(3):
            row = (o + i) * C
            out[row : row + C] = sums[0:C, i * L : (i + 1) * L]


def pack_sums(sums, packed, at):
    last = sums[3 * QUARTER : WG]
    lane = lax.broadcasted_iota(jnp.int32, (QUARTER, L), 1)
    for i in range(3):
        moved = pltpu.roll(last, C - 32 * i, 1)
        rows = slice(i * QUARTER, (i + 1) * QUARTER)
        packed[at + i * QUARTER : at + (i + 1) * QUARTER] = jnp.where(lane < C, sums[rows], moved)
    packed[at + 3 * QUARTER : at + ROWS] = jnp.zeros((ROWS - 3 * QUARTER, L), F32)


def last_kernel(scale, packed, output, grad, output_out, grad_out, first, second):
    output_out[...] = output[...]
    grad_out[...] = grad[...]
    lane = lax.broadcasted_iota(jnp.int32, (QUARTER, L), 1)
    for i, out in enumerate((first, second)):
        whole = packed[i * ROWS : (i + 1) * ROWS].astype(F32) * scale
        last = jnp.zeros((QUARTER, L), F32)
        for k in range(3):
            part = whole[k * QUARTER : (k + 1) * QUARTER]
            last = jnp.where(lane // 32 == k, pltpu.roll(part, 32 + 32 * k, 1), last)
        for r in range(0, WG, 24):
            part = whole[r : r + 24] if r < 3 * QUARTER else last[r - 3 * QUARTER : r - 3 * QUARTER + 24]
            out[r // C, r % C : r % C + 24, :] = part[:, 0:C]


def send(source, dest, sems, peer):
    copy = pltpu.make_async_remote_copy(
        src_ref=source, dst_ref=dest, send_sem=sems[0], recv_sem=sems[1], device_id=peer, device_id_type=MESH
    )
    copy.start()
    return copy


def greet(peers):
    barrier = pltpu.get_barrier_semaphore()
    for peer in peers:
        pl.semaphore_signal(barrier, inc=1, device_id=peer, device_id_type=MESH)


def neighbours(n_wide):
    w, n = lax.axis_index("wide"), lax.axis_index("narrow")
    ahead, behind = lax.rem(w + 1, n_wide), lax.rem(w + n_wide - 1, n_wide)
    return w, n, ahead, behind


class Shells:
    def __init__(self, n_wide, halo, sems, parts):
        self.w, self.n, ahead, behind = neighbours(n_wide)
        self.partner = (self.w, 1 - self.n)
        self.parts = [pl.ds(start, size) for start, size in parts]
        self.peers = [(behind, self.n), self.partner, (ahead, self.n)]
        self.halo, self.sems, self.copies, self.across = halo, sems, {}, {}

    def pair(self, k, i):
        return self.sems.at[0, k, i], self.sems.at[1, k, i]

    def start(self, sources, k):
        rows = self.parts[k]
        self.copies[k] = [
            send(sources[g].at[rows], self.halo.at[g, self.n, rows], self.pair(k, g), self.peers[g]) for g in range(3)
        ]

    def forward(self, k):
        self.across[k] = []
        for g in (0, 2):
            self.copies[k][g].wait()
            got = self.halo.at[g, self.n, self.parts[k]]
            self.across[k].append(send(got, got, self.pair(k, 3 + g), self.partner))

    def settle(self, k):
        self.copies[k][1].wait()
        for copy in self.across[k]:
            copy.wait()


class Returns:
    def __init__(self, n_wide, out, got, joined, arrived, sems):
        self.w, self.n, ahead, behind = neighbours(n_wide)
        self.partner = (self.w, 1 - self.n)
        self.to = {0: (ahead, self.n), 2: (behind, self.n)}
        self.out, self.got, self.joined, self.arrived, self.sems = out, got, joined, arrived, sems

    def pair(self, i):
        return self.sems.at[0, i], self.sems.at[1, i]

    def start(self):
        self.joins = [
            send(self.out.at[g, 1 - self.n], self.got.at[i], self.pair(i), self.partner) for i, g in enumerate((0, 2))
        ]
        self.backs = [send(self.out.at[1, 1 - self.n], self.arrived.at[1], self.pair(2), self.partner)]

    def join(self):
        for i, g in enumerate((0, 2)):
            self.joins[i].wait()
            self.joined[i] = (self.out[g, self.n].astype(F32) + self.got[i].astype(F32)).astype(BF16)
            self.backs.append(send(self.joined.at[i], self.arrived.at[g], self.pair(3 + i), self.to[g]))

    def add(self, grads):
        for copy in self.backs:
            copy.wait()
        for t in range(B):
            for g in range(3):
                faces = stretch(self.arrived[g, t * TIGHT_FACES : (t + 1) * TIGHT_FACES].astype(F32))
                add_faces(faces.reshape(FACES // 8, 8, L), grads, t)


class Sum:
    def __init__(self, nz, nxy, src, whole, at, scratch):
        self.nz, self.nxy, self.src, self.whole, self.at = nz, nxy, src, whole, at
        (self.half, self.got1, self.got2, self.got3,
         self.sem1, self.sem2, self.sem3, self.sem4, self.sem5) = scratch
        w, self.n = lax.axis_index("wide"), lax.axis_index("narrow")
        self.z, self.xy = w // nxy, lax.rem(w, nxy)
        self.plane = HALF // nxy
        self.partner = (w, 1 - self.n)
        nx = 4 if nxy % 4 == 0 else nxy
        ny = nxy // nx
        x, y = lax.rem(self.xy, nx), self.xy // nx

        def place(dx, dy):
            return lax.rem(y + dy + ny, ny) * nx + lax.rem(x + dx + nx, nx)

        def hops(step, size):
            return min(step, size - step)

        steps = [(dx, dy) for dx in range(nx) for dy in range(ny) if dx or dy]
        steps.sort(key=lambda step: -hops(step[0], nx) - hops(step[1], ny))
        self.to = [place(dx, dy) for dx, dy in steps]
        self.origin = [place(-dx, -dy) for dx, dy in steps]
        self.in_plane = [(self.z * nxy + to, self.n) for to in self.to]
        rises = sorted(range(1, nz), key=lambda rise: -hops(rise, nz))
        self.in_column = [(lax.rem(self.z + rise, nz) * nxy + self.xy, self.n) for rise in rises]

    def peers(self):
        return self.in_column + self.in_plane + [self.partner]

    def rows(self, at, size):
        return pl.ds(pl.multiple_of(at, size), size)

    def pair(self, sems, d):
        return sems.at[0, d], sems.at[1, d]

    def cores(self):
        theirs = self.src.at[self.rows((1 - self.n) * HALF, HALF)]
        self.copies = [send(theirs, self.got1, self.pair(self.sem1, 0), self.partner)]

    def wait(self):
        for copy in self.copies:
            copy.wait()

    def planes(self):
        self.wait()
        mine = self.src[self.rows(self.n * HALF, HALF), :]
        self.half[...] = (mine + self.got1[...]).astype(BF16)
        self.copies = []
        for d, peer in enumerate(self.in_plane):
            part = self.half.at[self.rows(self.to[d] * self.plane, self.plane)]
            self.copies.append(send(part, self.got2.at[d], self.pair(self.sem2, d), peer))

    def column(self):
        self.wait()
        total = self.half[self.rows(self.xy * self.plane, self.plane), :].astype(F32)
        for d in range(self.nxy - 1):
            total += self.got2[d].astype(F32)
        own = self.got3.at[self.z]
        own[...] = total.astype(BF16)
        self.copies = [send(own, own, self.pair(self.sem3, d), peer) for d, peer in enumerate(self.in_column)]

    def planes_back(self):
        self.wait()
        total = self.got3[0].astype(F32)
        for z in range(1, self.nz):
            total += self.got3[z].astype(F32)
        own = self.rows(self.at + self.n * HALF + self.xy * self.plane, self.plane)
        self.whole[own, :] = total.astype(BF16)
        own = self.whole.at[own]
        self.copies = [send(own, own, self.pair(self.sem4, d), peer) for d, peer in enumerate(self.in_plane)]
        self.across = [send(own, own, self.pair(self.sem5, self.nxy - 1), self.partner)]

    def cores_back(self):
        for d, copy in enumerate(self.copies):
            copy.wait()
            got = self.whole.at[self.rows(self.at + self.n * HALF + self.origin[d] * self.plane, self.plane)]
            self.across.append(send(got, got, self.pair(self.sem5, d), self.partner))

    def end(self):
        for copy in self.across:
            copy.wait()


def sum_scratch(nz, nxy):
    plane = HALF // nxy
    sems = [pltpu.SemaphoreType.DMA((2, count)) for count in (1, nxy - 1, nz - 1, nxy - 1, nxy)]
    return [
        pltpu.VMEM((HALF, L), BF16),
        pltpu.VMEM((HALF, L), F32),
        pltpu.VMEM((nxy - 1, plane, L), BF16),
        pltpu.VMEM((nz, plane, L), BF16),
    ] + sems


def main_kernel(nz, nxy, far_slots, far_plan, far_features, far_occupancy, far_out_grad, far_weights1, far_weights2,
                output, feature_grad, reduced,
                table, shifted, columns, side, back, around, padded, middle, low, high, planes, edges, faces, grads,
                mask, slope, chosen, shell, masked, pre, sums, packed1, packed2, features, occupancy, out_grad, weights1, weights2,
                messages, near, hidden_shells, hidden_near,
                out1, got1, joined1, arrived1, out2, got2, joined2, arrived2,
                near_sems, hidden_sems, back_sems1, back_sems2, load_sems, slots, plan, *scratch):
    n_wide = nz * nxy
    n = lax.axis_index("narrow")
    blocks = [(t * TIGHT, TIGHT) for t in range(B)]
    actives = Shells(n_wide, near, near_sems, [(B * TIGHT, 16)] + blocks)
    hiddens = Shells(n_wide, hidden_near, hidden_sems, blocks)
    returns1 = Returns(n_wide, out1, got1, joined1, arrived1, back_sems1)
    returns2 = Returns(n_wide, out2, got2, joined2, arrived2, back_sems2)
    total1 = Sum(nz, nxy, packed1, reduced, 0, scratch[: len(scratch) // 2])
    total2 = Sum(nz, nxy, packed2, reduced, ROWS, scratch[len(scratch) // 2 :])
    everyone = total1.peers() + [actives.peers[0], actives.peers[2]]
    greet(everyone)
    far = (far_occupancy, far_features, far_plan, far_out_grad, far_weights2, far_slots, far_weights1)
    loads = []
    for i, (source, dest) in enumerate(zip(far, (occupancy, features, plan, out_grad, weights2, slots, weights1))):
        loads.append(pltpu.make_async_copy(source, dest, load_sems.at[i]))
        loads[i].start()
    loads[0].wait()
    loads[1].wait()

    for t in range(B):
        seen = occupancy[t : t + 1, :].astype(F32)
        table[t] = to_rows(features[t].astype(F32) * seen).reshape(8, 8, 8, L)
    row = lax.broadcasted_iota(jnp.int32, (16, L), 0)
    loads[2].wait()
    for t in range(B):
        pack_own(table, shell, messages.at[0], t)
    for g in range(3):
        if g > 0:
            messages[g, 0 : 2 * TIGHT] = messages[0, 0 : 2 * TIGHT]
        rows = jnp.zeros((16, L), F32)
        for i in range(4):
            rows = jnp.where(row == i, plan[i, g].astype(F32), rows)
        messages[g, 2 * TIGHT : MESSAGE] = rows.astype(BF16)
    pl.semaphore_wait(pltpu.get_barrier_semaphore(), len(everyone))
    for k in range(1 + B):
        actives.start([messages.at[g] for g in range(3)], k)

    loads[3].wait()
    padded[...] = jnp.zeros_like(padded)
    masked[C:L] = jnp.zeros((L - C, B * V), BF16)
    for t in range(B):
        seen = occupancy[t : t + 1, :].astype(F32)
        mask[t] = jnp.broadcast_to(seen, (L, V)).T
        own = out_grad[t].astype(F32) * seen
        masked[0:C, t * V : (t + 1) * V] = own.astype(BF16)
        padded[t, 2:10, 2:10] = to_rows(own).reshape(8, 8, 8, L)

    def transpose(t):
        spread(t, padded, around, back, middle, low, high, planes, edges)
        scatter(t, slots, middle, planes, edges, faces)
        grads[t] = middle[1:9, 1:9]

    def add_own():
        for t in range(B):
            add_faces(faces[t], grads, t)

    loads[4].wait()
    loads[5].wait()
    back_weights(weights2, back)
    faces[...] = jnp.zeros_like(faces)
    transpose(0)
    transpose(1)
    add_own()
    loads[6].wait()
    side_weights(weights1, side)
    table[EMPTY] = jnp.zeros((8, 8, 8, L), F32)
    actives.forward(0)
    actives.settle(0)
    for source in range(SLOTS // 2):
        rows = near[source // 2, source % 2, 2 * TIGHT : MESSAGE].astype(F32)
        for c in range(2):
            row = jnp.where(n == 0, rows[c : c + 1], rows[2 + c : 3 + c])
            chosen[2 * source + c] = jnp.broadcast_to(row, (8, L))
    gather_gradients(faces, chosen, out1)
    returns1.start()

    for k in (1, 2):
        actives.forward(k)
    returns1.join()
    for k in (1, 2):
        actives.settle(k)
    halo_entries(table, near, chosen)
    build_columns(slots, table, shifted, columns)
    for t in range(B):
        value = lax.dot_general(
            columns[t * V : (t + 1) * V, :], side[...], (((1,), (1,)), ((), ())), preferred_element_type=F32
        )
        seen = mask[t]
        gate = jax.nn.sigmoid(value)
        table[t] = (value * gate * seen).astype(BF16).astype(F32).reshape(8, 8, 8, L)
        pack_own(table, shell, hidden_shells, t)
        hiddens.start([hidden_shells] * 3, t)
        slope[t] = seen * gate * (1.0 + value * (1.0 - gate))
    side_weights(weights2, side)
    returns1.add(grads)
    for t in range(B):
        grad = grads[t].reshape(V, L) * slope[t]
        padded[t, 2:10, 2:10] = grad.reshape(8, 8, 8, L)
        pre[:, t * V : (t + 1) * V] = grad.T.astype(BF16)
    weight_sums(pre, columns, sums)
    pack_sums(sums, packed1, 0)
    total1.cores()

    for t in range(B):
        hiddens.forward(t)
    total1.planes()
    for t in range(B):
        hiddens.settle(t)
    halo_entries(table, hidden_near, chosen)
    build_columns(slots, table, shifted, columns)
    weight_sums(masked, columns, sums)
    pack_sums(sums, packed2, 0)
    total2.cores()

    def forward(t):
        seen = occupancy[t : t + 1, :].astype(F32)
        value = lax.dot_general(
            side[...], columns[t * V : (t + 1) * V, :], (((1,), (1,)), ((), ())), preferred_element_type=F32
        )
        output[t] = ((features[t].astype(F32) * seen + value[0:C]) * seen).astype(BF16)

    forward(0)
    total2.planes()
    total1.column()
    back_weights(weights1, back)
    faces[...] = jnp.zeros_like(faces)
    for t in range(B):
        transpose(t)
    add_own()
    gather_gradients(faces, chosen, out2)
    returns2.start()
    total2.column()
    returns2.join()
    forward(1)
    total1.planes_back()
    total2.planes_back()
    returns2.add(grads)
    for t in range(B):
        seen = occupancy[t : t + 1, :].astype(F32)
        own = grads[t].reshape(V, L).T
        feature_grad[t] = ((out_grad[t].astype(F32) * seen + own[0:C]) * seen).astype(BF16)
    total1.cores_back()
    total2.cores_back()
    total1.end()
    total2.end()


VMEM_SPEC = pl.BlockSpec(memory_space=pltpu.VMEM)
HBM_SPEC = pl.BlockSpec(memory_space=pltpu.HBM)


def shape(dims, dtype):
    return jax.ShapeDtypeStruct(dims, dtype)


BLOCK = (8, 8, 8, L)
SCRATCH = [
    ((EMPTY + 1,) + BLOCK, F32),
    ((3, 10, 10, 8, L), F32),
    ((B * V, 27 * L), BF16),
    ((L, 27 * L), BF16),
    ((9 * L, 3 * L), BF16),
    ((800, 9 * L), BF16),
    ((B, 12, 12, 8, L), F32),
    ((10, 10, 8, L), F32),
    ((10, 10, 8, L), F32),
    ((10, 10, 8, L), F32),
    ((2, 10, 8, L), F32),
    ((2, 2, 10, 8, L), F32),
    ((EMPTY, FACES // 8, 8, L), F32),
    ((B,) + BLOCK, F32),
    ((B, V, L), F32),
    ((B, V, L), F32),
    ((SLOTS, 8, L), F32),
    ((SHELL // 8, 8, L), F32),
    ((L, B * V), BF16),
    ((L, B * V), BF16),
    ((WG, L), F32),
    ((ROWS, L), F32),
    ((ROWS, L), F32),
    ((B, C, V), BF16),
    ((B, V), jnp.int32),
    ((B, C, V), BF16),
    ((27, C, C), BF16),
    ((27, C, C), BF16),
    ((3, MESSAGE, L), BF16),
    ((3, 2, MESSAGE, L), BF16),
    ((2 * TIGHT, L), BF16),
    ((3, 2, 2 * TIGHT, L), BF16),
] + 2 * [
    ((3, 2, 2 * TIGHT_FACES, L), BF16),
    ((2, 2 * TIGHT_FACES, L), BF16),
    ((2, 2 * TIGHT_FACES, L), BF16),
    ((3, 2 * TIGHT_FACES, L), BF16),
]


def local(nz, nxy, features, occupancy, conv1_weight, conv2_weight, out_grad, slots, send_blocks):
    dma = pltpu.SemaphoreType.DMA
    blocks = shape((B, C, V), BF16)
    inputs = (slots, send_blocks.reshape(3, 4).T, features, occupancy, out_grad, conv1_weight, conv2_weight)
    output, feature_grad, reduced = pl.pallas_call(
        functools.partial(main_kernel, nz, nxy),
        out_shape=[blocks, blocks, shape((2 * ROWS, L), BF16)],
        in_specs=[HBM_SPEC] * 7,
        out_specs=[VMEM_SPEC] * 3,
        scratch_shapes=[pltpu.VMEM(dims, dtype) for dims, dtype in SCRATCH]
        + [dma((2, 3, 6)), dma((2, 2, 6)), dma((2, 5)), dma((2, 5)), dma((7,)), pltpu.SMEM((B, 27), jnp.int32), pltpu.SMEM((4, 3), jnp.int32)] + 2 * sum_scratch(nz, nxy),
        compiler_params=pltpu.CompilerParams(
            collective_id=0, has_side_effects=True, vmem_limit_bytes=VMEM_LIMIT
        ),
    )(*(pltpu.with_memory_space_constraint(x, pltpu.HBM) for x in inputs))
    scale = (B * V * 2 * nz * nxy) ** -0.5
    return pl.pallas_call(
        functools.partial(last_kernel, scale),
        out_shape=[blocks, blocks] + [shape((27, C, C), F32)] * 2,
        in_specs=[VMEM_SPEC] * 3,
        out_specs=[VMEM_SPEC] * 4,
        compiler_params=pltpu.CompilerParams(vmem_limit_bytes=LAST_LIMIT),
    )(reduced, output, feature_grad)


def solution(mesh):
    both = ("wide", "narrow")
    n_wide = mesh.shape["wide"]
    nxy = 16 if n_wide % 16 == 0 else n_wide // 2
    return jax.shard_map(
        functools.partial(local, n_wide // nxy, nxy),
        mesh=mesh,
        in_specs=(P(both, None, None), P(both, None), P(), P(), P(both, None, None), P(both, None),
                  P(both, None, None, None)),
        out_specs=(P(both, None, None), P(both, None, None), P(), P()),
        check_vma=False,
    )
```

```python
import functools

import jax
import jax.numpy as jnp
from jax import lax
from jax.experimental import pallas as pl
from jax.experimental.pallas import tpu as pltpu
from jax.sharding import PartitionSpec as P

MESH = pl.DeviceIdType.MESH
F32 = jnp.float32
BF16 = jnp.bfloat16
C = 96
L = 128
V = 512
B = 2
SLOTS = 12
EMPTY = 14
SHELL = 320
TIGHT = SHELL * 3 // 4
OFFSETS = [(a, b, e) for a in (-1, 0, 1) for b in (-1, 0, 1) for e in (-1, 0, 1)]
PAIRS = [(a, b) for a in (-1, 0, 1) for b in (-1, 0, 1)]
PLACE = {-1: slice(0, 1), 0: slice(1, 9), 1: slice(9, 10)}
LAYER = {-1: slice(7, 8), 0: slice(0, 8), 1: slice(0, 1)}
HALF = 1024
ROWS = 2 * HALF
WG = 27 * C
SPLIT = ((0, 14), (14, 27))
MESSAGE = 2 * TIGHT + 16
FACES = 384
TIGHT_FACES = FACES * 3 // 4
VMEM_LIMIT = 44 * 1024 * 1024
LAST_LIMIT = 12 * 1024 * 1024


def direction(a, b, e):
    return 9 * (a + 1) + 3 * (b + 1) + e + 1


def depth_index(shape):
    return lax.broadcasted_iota(jnp.int32, shape, len(shape) - 2)


def roll_depth(value, shift):
    return pltpu.roll(value, shift % 8, value.ndim - 2)


def to_rows(value):
    wide = jnp.concatenate([value, jnp.zeros((L - C, V), F32)], axis=0)
    return wide.T


def squeeze(rows):
    q = rows.shape[0] // 4
    lane = lax.broadcasted_iota(jnp.int32, (q, L), 1)
    last = rows[3 * q :]
    parts = [jnp.where(lane < C, rows[i * q : (i + 1) * q], pltpu.roll(last, C - 32 * i, 1)) for i in range(3)]
    return jnp.concatenate(parts, axis=0)


def stretch(rows):
    q = rows.shape[0] // 3
    lane = lax.broadcasted_iota(jnp.int32, (q, L), 1)
    parts, last = [], jnp.zeros((q, L), F32)
    for i in range(3):
        part = rows[i * q : (i + 1) * q]
        parts.append(jnp.where(lane < C, part, 0.0))
        last = jnp.where(lane // 32 == i, pltpu.roll(part, 32 + 32 * i, 1), last)
    return jnp.concatenate(parts + [last], axis=0)


def pack_shell(table, entry, shell):
    shell[0:8] = table[entry, 0]
    shell[8:16] = table[entry, 7]
    shell[16:22] = table[entry, 1:7, 0]
    shell[22:28] = table[entry, 1:7, 7]
    for at, z in ((28, 0), (34, 7)):
        shell[at : at + 6] = table[entry, 1:7, :, z, :]
    return squeeze(shell[...].reshape(SHELL, L)).astype(BF16)


def unpack_shell(shell, table, entry):
    table[entry, 0] = shell[0:8]
    table[entry, 7] = shell[8:16]
    table[entry, 1:7, 0] = shell[16:22]
    table[entry, 1:7, 7] = shell[22:28]
    table[entry, 1:7, :, 0, :] = shell[28:34]
    table[entry, 1:7, :, 7, :] = shell[34:40]


def add_faces(faces, grads, t):
    grads[t, 0] += faces[0:8]
    grads[t, 7] += faces[8:16]
    grads[t, :, 0] += faces[16:24]
    grads[t, :, 7] += faces[24:32]
    grads[t, :, :, 0, :] += faces[32:40]
    grads[t, :, :, 7, :] += faces[40:48]


def pack_own(table, shell, out, t):
    out[t * TIGHT : (t + 1) * TIGHT] = pack_shell(table, t, shell)


def gather_gradients(faces, chosen, out):
    for g in range(3):
        for m in range(2):
            for t in range(B):
                total = 0.0
                for c in range(2):
                    slot = 4 * g + 2 * m + c
                    total += jnp.where(chosen[slot] == float(t), faces[B + slot], 0.0)
                out[g, m, t * TIGHT_FACES : (t + 1) * TIGHT_FACES] = squeeze(total.reshape(FACES, L)).astype(BF16)


def halo_entries(table, halo, chosen):
    for source in range(SLOTS // 2):
        blocks = []
        for t in range(B):
            rows = halo[source // 2, source % 2, t * TIGHT : (t + 1) * TIGHT].astype(F32)
            blocks.append(stretch(rows).reshape(SHELL // 8, 8, L))
        for c in range(2):
            slot = 2 * source + c
            unpack_shell(jnp.where(chosen[slot] == 0.0, blocks[0], blocks[1]), table, B + slot)


def build_columns(slots, table, shifted, columns):
    def one(t, carry):
        for a, b in PAIRS:
            def source(e):
                return table[slots[t, direction(a, b, e)], LAYER[a], LAYER[b]]

            here = source(0)
            z = depth_index(here.shape)
            shifted[1, PLACE[a], PLACE[b]] = here
            shifted[0, PLACE[a], PLACE[b]] = roll_depth(jnp.where(z == 7, source(-1), here), 1)
            shifted[2, PLACE[a], PLACE[b]] = roll_depth(jnp.where(z == 0, source(1), here), -1)
        rows = pl.ds(pl.multiple_of(t * V, V), V)
        for o, (a, b, e) in enumerate(OFFSETS):
            part = shifted[e + 1, a + 1 : a + 9, b + 1 : b + 9]
            columns[rows, o * L : (o + 1) * L] = part.reshape(V, L).astype(BF16)
        return carry

    lax.fori_loop(0, B, one, 0)


def side_weights(weights, side):
    side[...] = jnp.zeros_like(side)
    for o in range(27):
        side[0:C, o * L : o * L + C] = weights[o]


def back_weights(weights, back):
    back[...] = jnp.zeros_like(back)
    for o in range(27):
        k, e = o // 3, o % 3
        back[k * L : k * L + C, e * L : e * L + C] = weights[o]


def spread(t, padded, around, back, middle, low, high, planes, edges):
    for k, (a, b) in enumerate(PAIRS):
        part = padded[t, 1 - a : 11 - a, 1 - b : 11 - b]
        around[:, k * L : (k + 1) * L] = part.reshape(800, L).astype(BF16)
    by_depth = jnp.dot(around[...], back[...], preferred_element_type=F32).reshape(10, 10, 8, 3 * L)
    low[...] = by_depth[..., 0:L]
    high[...] = by_depth[..., 2 * L : 3 * L]
    down = roll_depth(low[...], -1)
    up = roll_depth(high[...], 1)
    z = depth_index(up.shape)
    middle[...] = by_depth[..., L : 2 * L] + jnp.where(z != 0, up, 0.0) + jnp.where(z != 7, down, 0.0)
    y = depth_index((10, 8, L))
    for i, (source, at) in enumerate(((low, 0), (high, 7))):
        planes[i] = source[:, 1:9, at, :]
        for j, (column, row) in enumerate(((0, 7), (9, 0))):
            edge = source[:, column, at : at + 1, :]
            edges[i, j] = jnp.where(y == row, edge, 0.0)


def scatter(t, slots, middle, planes, edges, faces):
    def one(entry, carry):
        def weight(a, b, e):
            return (slots[t, direction(a, b, e)] == entry).astype(F32)

        for x, (a, px) in ((0, (1, 9)), (8, (-1, 0))):
            faces[entry, x : x + 8] += weight(a, 0, 0) * middle[px, 1:9]
            faces[entry, x] += weight(a, 1, 0) * middle[px, 9]
            faces[entry, x + 7] += weight(a, -1, 0) * middle[px, 0]
        faces[entry, 16:24] += weight(0, 1, 0) * middle[1:9, 9]
        faces[entry, 24:32] += weight(0, -1, 0) * middle[1:9, 0]
        for at, e, i in ((32, 1, 1), (40, -1, 0)):
            for a, x, px in ((0, slice(at, at + 8), slice(1, 9)), (1, at, 9), (-1, at + 7, 0)):
                total = weight(a, 0, e) * planes[i, px]
                total += weight(a, -1, e) * edges[i, 0, px] + weight(a, 1, e) * edges[i, 1, px]
                faces[entry, x] += total
        return carry

    lax.fori_loop(0, EMPTY, one, 0)


def half_sums(left, columns, sums, packed, h):
    start, end = SPLIT[h]
    for o in range(start, end, 3):
        count = min(3, end - o)
        part = jnp.dot(left[...], columns[:, o * L : (o + count) * L], preferred_element_type=F32)
        for i in range(count):
            sums[(o + i) * C : (o + i + 1) * C] = part[0:C, i * L : (i + 1) * L]
    size = (end - start) * C * 3 // 4
    packed[h * HALF : h * HALF + size] = squeeze(sums[start * C : end * C])
    packed[h * HALF + size : (h + 1) * HALF] = jnp.zeros((HALF - size, L), F32)


def weight_sums(n, left, columns, sums, packed, total):
    for mine in (False, True):
        for core in range(2):
            half = core if mine else 1 - core

            @pl.when(n == core)
            def _():
                half_sums(left, columns, sums, packed, half)

        if not mine:
            total.cores()


def last_kernel(scale, packed, output, grad, output_out, grad_out, first, second):
    output_out[...] = output[...]
    grad_out[...] = grad[...]
    for i, out in enumerate((first, second)):
        for h, (start, end) in enumerate(SPLIT):
            size = (end - start) * C
            at = i * ROWS + h * HALF
            rows = stretch((packed[at : at + HALF].astype(F32) * scale)[0 : size * 3 // 4])
            for r in range(0, size, 24):
                out[start + r // C, r % C : r % C + 24, :] = rows[r : r + 24, 0:C]


def send(source, dest, sems, peer):
    copy = pltpu.make_async_remote_copy(
        src_ref=source, dst_ref=dest, send_sem=sems[0], recv_sem=sems[1], device_id=peer, device_id_type=MESH
    )
    copy.start()
    return copy


def greet(peers):
    barrier = pltpu.get_barrier_semaphore()
    for peer in peers:
        pl.semaphore_signal(barrier, inc=1, device_id=peer, device_id_type=MESH)


def neighbours(n_wide):
    w, n = lax.axis_index("wide"), lax.axis_index("narrow")
    ahead, behind = lax.rem(w + 1, n_wide), lax.rem(w + n_wide - 1, n_wide)
    return w, n, ahead, behind


class Shells:
    def __init__(self, n_wide, halo, sems, parts):
        self.w, self.n, ahead, behind = neighbours(n_wide)
        self.partner = (self.w, 1 - self.n)
        self.parts = [pl.ds(start, size) for start, size in parts]
        self.peers = [(behind, self.n), self.partner, (ahead, self.n)]
        self.halo, self.sems, self.copies, self.across = halo, sems, {}, {}

    def pair(self, k, i):
        return self.sems.at[0, k, i], self.sems.at[1, k, i]

    def start(self, sources, k):
        rows = self.parts[k]
        self.copies[k] = [
            send(sources[g].at[rows], self.halo.at[g, self.n, rows], self.pair(k, g), self.peers[g]) for g in range(3)
        ]

    def forward(self, k):
        self.across[k] = []
        for g in (0, 2):
            self.copies[k][g].wait()
            got = self.halo.at[g, self.n, self.parts[k]]
            self.across[k].append(send(got, got, self.pair(k, 3 + g), self.partner))

    def settle(self, k):
        self.copies[k][1].wait()
        for copy in self.across[k]:
            copy.wait()


class Returns:
    def __init__(self, n_wide, out, got, joined, arrived, sems):
        self.w, self.n, ahead, behind = neighbours(n_wide)
        self.partner = (self.w, 1 - self.n)
        self.to = {0: (ahead, self.n), 2: (behind, self.n)}
        self.out, self.got, self.joined, self.arrived, self.sems = out, got, joined, arrived, sems

    def pair(self, i):
        return self.sems.at[0, i], self.sems.at[1, i]

    def start(self):
        self.joins = [
            send(self.out.at[g, 1 - self.n], self.got.at[i], self.pair(i), self.partner) for i, g in enumerate((0, 2))
        ]
        self.backs = [send(self.out.at[1, 1 - self.n], self.arrived.at[1], self.pair(2), self.partner)]

    def join(self):
        for i, g in enumerate((0, 2)):
            self.joins[i].wait()
            self.joined[i] = (self.out[g, self.n].astype(F32) + self.got[i].astype(F32)).astype(BF16)
            self.backs.append(send(self.joined.at[i], self.arrived.at[g], self.pair(3 + i), self.to[g]))

    def add(self, grads):
        for copy in self.backs:
            copy.wait()
        for t in range(B):
            for g in range(3):
                faces = stretch(self.arrived[g, t * TIGHT_FACES : (t + 1) * TIGHT_FACES].astype(F32))
                add_faces(faces.reshape(FACES // 8, 8, L), grads, t)


class Sum:
    def __init__(self, nz, nxy, src, whole, at, scratch):
        self.nz, self.nxy, self.src, self.whole, self.at = nz, nxy, src, whole, at
        (self.half, self.got1, self.got2, self.got3,
         self.sem1, self.sem2, self.sem3, self.sem4, self.sem5) = scratch
        w, self.n = lax.axis_index("wide"), lax.axis_index("narrow")
        self.z, self.xy = w // nxy, lax.rem(w, nxy)
        self.plane = HALF // nxy
        self.partner = (w, 1 - self.n)
        nx = 4 if nxy % 4 == 0 else nxy
        ny = nxy // nx
        x, y = lax.rem(self.xy, nx), self.xy // nx

        def place(dx, dy):
            return lax.rem(y + dy + ny, ny) * nx + lax.rem(x + dx + nx, nx)

        def hops(step, size):
            return min(step, size - step)

        steps = [(dx, dy) for dx in range(nx) for dy in range(ny) if dx or dy]
        steps.sort(key=lambda step: -hops(step[0], nx) - hops(step[1], ny))
        self.to = [place(dx, dy) for dx, dy in steps]
        self.origin = [place(-dx, -dy) for dx, dy in steps]
        self.in_plane = [(self.z * nxy + to, self.n) for to in self.to]
        rises = sorted(range(1, nz), key=lambda rise: -hops(rise, nz))
        self.in_column = [(lax.rem(self.z + rise, nz) * nxy + self.xy, self.n) for rise in rises]

    def peers(self):
        return self.in_column + self.in_plane + [self.partner]

    def rows(self, at, size):
        return pl.ds(pl.multiple_of(at, size), size)

    def pair(self, sems, d):
        return sems.at[0, d], sems.at[1, d]

    def cores(self):
        theirs = self.src.at[self.rows((1 - self.n) * HALF, HALF)]
        self.copies = [send(theirs, self.got1, self.pair(self.sem1, 0), self.partner)]

    def wait(self):
        for copy in self.copies:
            copy.wait()

    def planes(self):
        self.wait()
        mine = self.src[self.rows(self.n * HALF, HALF), :]
        self.half[...] = (mine + self.got1[...]).astype(BF16)
        self.copies = []
        for d, peer in enumerate(self.in_plane):
            part = self.half.at[self.rows(self.to[d] * self.plane, self.plane)]
            self.copies.append(send(part, self.got2.at[d], self.pair(self.sem2, d), peer))

    def column(self):
        self.wait()
        total = self.half[self.rows(self.xy * self.plane, self.plane), :].astype(F32)
        for d in range(self.nxy - 1):
            total += self.got2[d].astype(F32)
        own = self.got3.at[self.z]
        own[...] = total.astype(BF16)
        self.copies = [send(own, own, self.pair(self.sem3, d), peer) for d, peer in enumerate(self.in_column)]

    def planes_back(self):
        self.wait()
        total = self.got3[0].astype(F32)
        for z in range(1, self.nz):
            total += self.got3[z].astype(F32)
        own = self.rows(self.at + self.n * HALF + self.xy * self.plane, self.plane)
        self.whole[own, :] = total.astype(BF16)
        own = self.whole.at[own]
        self.copies = [send(own, own, self.pair(self.sem4, d), peer) for d, peer in enumerate(self.in_plane)]
        self.across = [send(own, own, self.pair(self.sem5, self.nxy - 1), self.partner)]

    def cores_back(self):
        for d, copy in enumerate(self.copies):
            copy.wait()
            got = self.whole.at[self.rows(self.at + self.n * HALF + self.origin[d] * self.plane, self.plane)]
            self.across.append(send(got, got, self.pair(self.sem5, d), self.partner))

    def end(self):
        for copy in self.across:
            copy.wait()


def sum_scratch(nz, nxy):
    plane = HALF // nxy
    sems = [pltpu.SemaphoreType.DMA((2, count)) for count in (1, nxy - 1, nz - 1, nxy - 1, nxy)]
    return [
        pltpu.VMEM((HALF, L), BF16),
        pltpu.VMEM((HALF, L), F32),
        pltpu.VMEM((nxy - 1, plane, L), BF16),
        pltpu.VMEM((nz, plane, L), BF16),
    ] + sems


def main_kernel(nz, nxy, far_slots, far_plan, far_features, far_occupancy, far_out_grad, far_weights1, far_weights2,
                output, feature_grad, reduced,
                table, shifted, columns, side, back, around, padded, middle, low, high, planes, edges, faces, grads,
                mask, slope, chosen, shell, masked, pre, sums, packed1, packed2, features, occupancy, out_grad, weights1, weights2,
                messages, near, hidden_shells, hidden_near,
                out1, got1, joined1, arrived1, out2, got2, joined2, arrived2,
                near_sems, hidden_sems, back_sems1, back_sems2, load_sems, slots, plan, *scratch):
    n_wide = nz * nxy
    n = lax.axis_index("narrow")
    blocks = [(t * TIGHT, TIGHT) for t in range(B)]
    actives = Shells(n_wide, near, near_sems, [(B * TIGHT, 16)] + blocks)
    hiddens = Shells(n_wide, hidden_near, hidden_sems, blocks)
    returns1 = Returns(n_wide, out1, got1, joined1, arrived1, back_sems1)
    returns2 = Returns(n_wide, out2, got2, joined2, arrived2, back_sems2)
    total1 = Sum(nz, nxy, packed1, reduced, 0, scratch[: len(scratch) // 2])
    total2 = Sum(nz, nxy, packed2, reduced, ROWS, scratch[len(scratch) // 2 :])
    everyone = total1.peers() + [actives.peers[0], actives.peers[2]]
    greet(everyone)
    far = (far_occupancy, far_features, far_plan, far_out_grad, far_weights2, far_slots, far_weights1)
    loads = []
    for i, (source, dest) in enumerate(zip(far, (occupancy, features, plan, out_grad, weights2, slots, weights1))):
        loads.append(pltpu.make_async_copy(source, dest, load_sems.at[i]))
        loads[i].start()
    loads[0].wait()
    loads[1].wait()

    for t in range(B):
        seen = occupancy[t : t + 1, :].astype(F32)
        table[t] = to_rows(features[t].astype(F32) * seen).reshape(8, 8, 8, L)
    row = lax.broadcasted_iota(jnp.int32, (16, L), 0)
    loads[2].wait()
    for t in range(B):
        pack_own(table, shell, messages.at[0], t)
    for g in range(3):
        if g > 0:
            messages[g, 0 : 2 * TIGHT] = messages[0, 0 : 2 * TIGHT]
        rows = jnp.zeros((16, L), F32)
        for i in range(4):
            rows = jnp.where(row == i, plan[i, g].astype(F32), rows)
        messages[g, 2 * TIGHT : MESSAGE] = rows.astype(BF16)

    loads[3].wait()
    padded[...] = jnp.zeros_like(padded)
    masked[C:L] = jnp.zeros((L - C, B * V), BF16)
    for t in range(B):
        seen = occupancy[t : t + 1, :].astype(F32)
        mask[t] = jnp.broadcast_to(seen, (L, V)).T
        own = out_grad[t].astype(F32) * seen
        masked[0:C, t * V : (t + 1) * V] = own.astype(BF16)
        padded[t, 2:10, 2:10] = to_rows(own).reshape(8, 8, 8, L)

    def transpose(t):
        spread(t, padded, around, back, middle, low, high, planes, edges)
        scatter(t, slots, middle, planes, edges, faces)
        grads[t] = middle[1:9, 1:9]

    def add_own():
        for t in range(B):
            add_faces(faces[t], grads, t)

    loads[4].wait()
    loads[5].wait()
    back_weights(weights2, back)
    faces[...] = jnp.zeros_like(faces)
    pl.semaphore_wait(pltpu.get_barrier_semaphore(), len(everyone))
    for k in range(1 + B):
        actives.start([messages.at[g] for g in range(3)], k)
    transpose(0)
    transpose(1)
    add_own()
    loads[6].wait()
    side_weights(weights1, side)
    table[EMPTY] = jnp.zeros((8, 8, 8, L), F32)
    actives.forward(0)
    actives.settle(0)
    for source in range(SLOTS // 2):
        rows = near[source // 2, source % 2, 2 * TIGHT : MESSAGE].astype(F32)
        for c in range(2):
            row = jnp.where(n == 0, rows[c : c + 1], rows[2 + c : 3 + c])
            chosen[2 * source + c] = jnp.broadcast_to(row, (8, L))
    gather_gradients(faces, chosen, out1)
    returns1.start()

    for k in (1, 2):
        actives.forward(k)
    returns1.join()
    for k in (1, 2):
        actives.settle(k)
    halo_entries(table, near, chosen)
    build_columns(slots, table, shifted, columns)
    for t in range(B):
        value = lax.dot_general(
            columns[t * V : (t + 1) * V, :], side[...], (((1,), (1,)), ((), ())), preferred_element_type=F32
        )
        seen = mask[t]
        gate = jax.nn.sigmoid(value)
        table[t] = (value * gate * seen).astype(BF16).astype(F32).reshape(8, 8, 8, L)
        pack_own(table, shell, hidden_shells, t)
        hiddens.start([hidden_shells] * 3, t)
        slope[t] = seen * gate * (1.0 + value * (1.0 - gate))
    side_weights(weights2, side)
    returns1.add(grads)
    for t in range(B):
        grad = grads[t].reshape(V, L) * slope[t]
        padded[t, 2:10, 2:10] = grad.reshape(8, 8, 8, L)
        pre[:, t * V : (t + 1) * V] = grad.T.astype(BF16)
    weight_sums(n, pre, columns, sums, packed1, total1)

    for t in range(B):
        hiddens.forward(t)
    total1.planes()
    for t in range(B):
        hiddens.settle(t)
    halo_entries(table, hidden_near, chosen)
    build_columns(slots, table, shifted, columns)
    weight_sums(n, masked, columns, sums, packed2, total2)

    def forward(t):
        seen = occupancy[t : t + 1, :].astype(F32)
        value = lax.dot_general(
            side[...], columns[t * V : (t + 1) * V, :], (((1,), (1,)), ((), ())), preferred_element_type=F32
        )
        output[t] = ((features[t].astype(F32) * seen + value[0:C]) * seen).astype(BF16)

    forward(0)
    total2.planes()
    total1.column()
    back_weights(weights1, back)
    faces[...] = jnp.zeros_like(faces)
    for t in range(B):
        transpose(t)
    add_own()
    gather_gradients(faces, chosen, out2)
    returns2.start()
    total2.column()
    returns2.join()
    forward(1)
    total1.planes_back()
    total2.planes_back()
    returns2.add(grads)
    for t in range(B):
        seen = occupancy[t : t + 1, :].astype(F32)
        own = grads[t].reshape(V, L).T
        feature_grad[t] = ((out_grad[t].astype(F32) * seen + own[0:C]) * seen).astype(BF16)
    total1.cores_back()
    total2.cores_back()
    total1.end()
    total2.end()


VMEM_SPEC = pl.BlockSpec(memory_space=pltpu.VMEM)
HBM_SPEC = pl.BlockSpec(memory_space=pltpu.HBM)


def shape(dims, dtype):
    return jax.ShapeDtypeStruct(dims, dtype)


BLOCK = (8, 8, 8, L)
SCRATCH = [
    ((EMPTY + 1,) + BLOCK, F32),
    ((3, 10, 10, 8, L), F32),
    ((B * V, 27 * L), BF16),
    ((L, 27 * L), BF16),
    ((9 * L, 3 * L), BF16),
    ((800, 9 * L), BF16),
    ((B, 12, 12, 8, L), F32),
    ((10, 10, 8, L), F32),
    ((10, 10, 8, L), F32),
    ((10, 10, 8, L), F32),
    ((2, 10, 8, L), F32),
    ((2, 2, 10, 8, L), F32),
    ((EMPTY, FACES // 8, 8, L), F32),
    ((B,) + BLOCK, F32),
    ((B, V, L), F32),
    ((B, V, L), F32),
    ((SLOTS, 8, L), F32),
    ((SHELL // 8, 8, L), F32),
    ((L, B * V), BF16),
    ((L, B * V), BF16),
    ((WG, L), F32),
    ((ROWS, L), F32),
    ((ROWS, L), F32),
    ((B, C, V), BF16),
    ((B, V), jnp.int32),
    ((B, C, V), BF16),
    ((27, C, C), BF16),
    ((27, C, C), BF16),
    ((3, MESSAGE, L), BF16),
    ((3, 2, MESSAGE, L), BF16),
    ((2 * TIGHT, L), BF16),
    ((3, 2, 2 * TIGHT, L), BF16),
] + 2 * [
    ((3, 2, 2 * TIGHT_FACES, L), BF16),
    ((2, 2 * TIGHT_FACES, L), BF16),
    ((2, 2 * TIGHT_FACES, L), BF16),
    ((3, 2 * TIGHT_FACES, L), BF16),
]


def local(nz, nxy, features, occupancy, conv1_weight, conv2_weight, out_grad, slots, send_blocks):
    dma = pltpu.SemaphoreType.DMA
    blocks = shape((B, C, V), BF16)
    inputs = (slots, send_blocks.reshape(3, 4).T, features, occupancy, out_grad, conv1_weight, conv2_weight)
    output, feature_grad, reduced = pl.pallas_call(
        functools.partial(main_kernel, nz, nxy),
        out_shape=[blocks, blocks, shape((2 * ROWS, L), BF16)],
        in_specs=[HBM_SPEC] * 7,
        out_specs=[VMEM_SPEC] * 3,
        scratch_shapes=[pltpu.VMEM(dims, dtype) for dims, dtype in SCRATCH]
        + [dma((2, 3, 6)), dma((2, 2, 6)), dma((2, 5)), dma((2, 5)), dma((7,)), pltpu.SMEM((B, 27), jnp.int32), pltpu.SMEM((4, 3), jnp.int32)] + 2 * sum_scratch(nz, nxy),
        compiler_params=pltpu.CompilerParams(
            collective_id=0, has_side_effects=True, vmem_limit_bytes=VMEM_LIMIT
        ),
    )(*(pltpu.with_memory_space_constraint(x, pltpu.HBM) for x in inputs))
    scale = (B * V * 2 * nz * nxy) ** -0.5
    return pl.pallas_call(
        functools.partial(last_kernel, scale),
        out_shape=[blocks, blocks] + [shape((27, C, C), F32)] * 2,
        in_specs=[VMEM_SPEC] * 3,
        out_specs=[VMEM_SPEC] * 4,
        compiler_params=pltpu.CompilerParams(vmem_limit_bytes=LAST_LIMIT),
    )(reduced, output, feature_grad)


def solution(mesh):
    both = ("wide", "narrow")
    n_wide = mesh.shape["wide"]
    nxy = 16 if n_wide % 16 == 0 else n_wide // 2
    return jax.shard_map(
        functools.partial(local, n_wide // nxy, nxy),
        mesh=mesh,
        in_specs=(P(both, None, None), P(both, None), P(), P(), P(both, None, None), P(both, None),
                  P(both, None, None, None)),
        out_specs=(P(both, None, None), P(both, None, None), P(), P()),
        check_vma=False,
    )
```

```python
import functools

import jax
import jax.numpy as jnp
from jax import lax
from jax.experimental import pallas as pl
from jax.experimental.pallas import tpu as pltpu
from jax.sharding import PartitionSpec as P

MESH = pl.DeviceIdType.MESH
F32 = jnp.float32
BF16 = jnp.bfloat16
C = 96
L = 128
V = 512
B = 2
SLOTS = 12
EMPTY = 14
SHELL = 320
TIGHT = SHELL * 3 // 4
OFFSETS = [(a, b, e) for a in (-1, 0, 1) for b in (-1, 0, 1) for e in (-1, 0, 1)]
PAIRS = [(a, b) for a in (-1, 0, 1) for b in (-1, 0, 1)]
PLACE = {-1: slice(0, 1), 0: slice(1, 9), 1: slice(9, 10)}
LAYER = {-1: slice(7, 8), 0: slice(0, 8), 1: slice(0, 1)}
HALF = 1024
ROWS = 2 * HALF
WG = 27 * C
SPLIT = ((0, 14), (14, 27))
MESSAGE = 2 * TIGHT + 16
FACES = 384
TIGHT_FACES = FACES * 3 // 4
VMEM_LIMIT = 44 * 1024 * 1024
LAST_LIMIT = 12 * 1024 * 1024


def direction(a, b, e):
    return 9 * (a + 1) + 3 * (b + 1) + e + 1


def depth_index(shape):
    return lax.broadcasted_iota(jnp.int32, shape, len(shape) - 2)


def roll_depth(value, shift):
    return pltpu.roll(value, shift % 8, value.ndim - 2)


def to_rows(value):
    wide = jnp.concatenate([value, jnp.zeros((L - C, V), F32)], axis=0)
    return wide.T


def squeeze(rows):
    q = rows.shape[0] // 4
    lane = lax.broadcasted_iota(jnp.int32, (q, L), 1)
    last = rows[3 * q :]
    parts = [jnp.where(lane < C, rows[i * q : (i + 1) * q], pltpu.roll(last, C - 32 * i, 1)) for i in range(3)]
    return jnp.concatenate(parts, axis=0)


def stretch(rows):
    q = rows.shape[0] // 3
    lane = lax.broadcasted_iota(jnp.int32, (q, L), 1)
    parts, last = [], jnp.zeros((q, L), F32)
    for i in range(3):
        part = rows[i * q : (i + 1) * q]
        parts.append(jnp.where(lane < C, part, 0.0))
        last = jnp.where(lane // 32 == i, pltpu.roll(part, 32 + 32 * i, 1), last)
    return jnp.concatenate(parts + [last], axis=0)


def pack_shell(table, entry, shell):
    shell[0:8] = table[entry, 0]
    shell[8:16] = table[entry, 7]
    shell[16:22] = table[entry, 1:7, 0]
    shell[22:28] = table[entry, 1:7, 7]
    for at, z in ((28, 0), (34, 7)):
        shell[at : at + 6] = table[entry, 1:7, :, z, :]
    return squeeze(shell[...].reshape(SHELL, L)).astype(BF16)


def unpack_shell(shell, table, entry):
    table[entry, 0] = shell[0:8]
    table[entry, 7] = shell[8:16]
    table[entry, 1:7, 0] = shell[16:22]
    table[entry, 1:7, 7] = shell[22:28]
    table[entry, 1:7, :, 0, :] = shell[28:34]
    table[entry, 1:7, :, 7, :] = shell[34:40]


def add_faces(faces, grads, t):
    grads[t, 0] += faces[0:8]
    grads[t, 7] += faces[8:16]
    grads[t, :, 0] += faces[16:24]
    grads[t, :, 7] += faces[24:32]
    grads[t, :, :, 0, :] += faces[32:40]
    grads[t, :, :, 7, :] += faces[40:48]


def pack_own(table, shell, out, t):
    out[t * TIGHT : (t + 1) * TIGHT] = pack_shell(table, t, shell)


def gather_gradients(faces, chosen, out):
    for g in range(3):
        for m in range(2):
            for t in range(B):
                total = 0.0
                for c in range(2):
                    slot = 4 * g + 2 * m + c
                    total += jnp.where(chosen[slot] == float(t), faces[B + slot], 0.0)
                out[g, m, t * TIGHT_FACES : (t + 1) * TIGHT_FACES] = squeeze(total.reshape(FACES, L)).astype(BF16)


def halo_entries(table, halo, chosen):
    for source in range(SLOTS // 2):
        blocks = []
        for t in range(B):
            rows = halo[source // 2, source % 2, t * TIGHT : (t + 1) * TIGHT].astype(F32)
            blocks.append(stretch(rows).reshape(SHELL // 8, 8, L))
        for c in range(2):
            slot = 2 * source + c
            unpack_shell(jnp.where(chosen[slot] == 0.0, blocks[0], blocks[1]), table, B + slot)


def build_columns(slots, table, shifted, columns):
    def one(t, carry):
        for a, b in PAIRS:
            def source(e):
                return table[slots[t, direction(a, b, e)], LAYER[a], LAYER[b]]

            here = source(0)
            z = depth_index(here.shape)
            shifted[1, PLACE[a], PLACE[b]] = here
            shifted[0, PLACE[a], PLACE[b]] = roll_depth(jnp.where(z == 7, source(-1), here), 1)
            shifted[2, PLACE[a], PLACE[b]] = roll_depth(jnp.where(z == 0, source(1), here), -1)
        rows = pl.ds(pl.multiple_of(t * V, V), V)
        for o, (a, b, e) in enumerate(OFFSETS):
            part = shifted[e + 1, a + 1 : a + 9, b + 1 : b + 9]
            columns[rows, o * L : (o + 1) * L] = part.reshape(V, L).astype(BF16)
        return carry

    lax.fori_loop(0, B, one, 0)


def side_weights(weights, side):
    side[...] = jnp.zeros_like(side)
    for o in range(27):
        side[0:C, o * L : o * L + C] = weights[o]


def back_weights(weights, back):
    back[...] = jnp.zeros_like(back)
    for o in range(27):
        k, e = o // 3, o % 3
        back[k * L : k * L + C, e * L : e * L + C] = weights[o]


def spread(t, padded, around, back, middle, low, high, planes, edges):
    for k, (a, b) in enumerate(PAIRS):
        part = padded[t, 1 - a : 11 - a, 1 - b : 11 - b]
        around[:, k * L : (k + 1) * L] = part.reshape(800, L).astype(BF16)
    by_depth = jnp.dot(around[...], back[...], preferred_element_type=F32).reshape(10, 10, 8, 3 * L)
    low[...] = by_depth[..., 0:L]
    high[...] = by_depth[..., 2 * L : 3 * L]
    down = roll_depth(low[...], -1)
    up = roll_depth(high[...], 1)
    z = depth_index(up.shape)
    middle[...] = by_depth[..., L : 2 * L] + jnp.where(z != 0, up, 0.0) + jnp.where(z != 7, down, 0.0)
    y = depth_index((10, 8, L))
    for i, (source, at) in enumerate(((low, 0), (high, 7))):
        planes[i] = source[:, 1:9, at, :]
        for j, (column, row) in enumerate(((0, 7), (9, 0))):
            edge = source[:, column, at : at + 1, :]
            edges[i, j] = jnp.where(y == row, edge, 0.0)


def scatter(t, slots, middle, planes, edges, faces):
    def one(entry, carry):
        def weight(a, b, e):
            return (slots[t, direction(a, b, e)] == entry).astype(F32)

        for x, (a, px) in ((0, (1, 9)), (8, (-1, 0))):
            faces[entry, x : x + 8] += weight(a, 0, 0) * middle[px, 1:9]
            faces[entry, x] += weight(a, 1, 0) * middle[px, 9]
            faces[entry, x + 7] += weight(a, -1, 0) * middle[px, 0]
        faces[entry, 16:24] += weight(0, 1, 0) * middle[1:9, 9]
        faces[entry, 24:32] += weight(0, -1, 0) * middle[1:9, 0]
        for at, e, i in ((32, 1, 1), (40, -1, 0)):
            for a, x, px in ((0, slice(at, at + 8), slice(1, 9)), (1, at, 9), (-1, at + 7, 0)):
                total = weight(a, 0, e) * planes[i, px]
                total += weight(a, -1, e) * edges[i, 0, px] + weight(a, 1, e) * edges[i, 1, px]
                faces[entry, x] += total
        return carry

    lax.fori_loop(0, EMPTY, one, 0)


def half_sums(left, columns, sums, packed, h):
    start, end = SPLIT[h]
    for o in range(start, end, 3):
        count = min(3, end - o)
        part = jnp.dot(left[...], columns[:, o * L : (o + count) * L], preferred_element_type=F32)
        for i in range(count):
            sums[(o + i) * C : (o + i + 1) * C] = part[0:C, i * L : (i + 1) * L]
    size = (end - start) * C * 3 // 4
    packed[h * HALF : h * HALF + size] = squeeze(sums[start * C : end * C])
    packed[h * HALF + size : (h + 1) * HALF] = jnp.zeros((HALF - size, L), F32)


def weight_sums(n, left, columns, sums, packed, total):
    for mine in (False, True):
        for core in range(2):
            half = core if mine else 1 - core

            @pl.when(n == core)
            def _():
                half_sums(left, columns, sums, packed, half)

        if not mine:
            total.cores()


def last_kernel(scale, packed, output, grad, output_out, grad_out, first, second):
    output_out[...] = output[...]
    grad_out[...] = grad[...]
    for i, out in enumerate((first, second)):
        for h, (start, end) in enumerate(SPLIT):
            size = (end - start) * C
            at = i * ROWS + h * HALF
            rows = stretch((packed[at : at + HALF].astype(F32) * scale)[0 : size * 3 // 4])
            for r in range(0, size, 24):
                out[start + r // C, r % C : r % C + 24, :] = rows[r : r + 24, 0:C]


def send(source, dest, sems, peer):
    copy = pltpu.make_async_remote_copy(
        src_ref=source, dst_ref=dest, send_sem=sems[0], recv_sem=sems[1], device_id=peer, device_id_type=MESH
    )
    copy.start()
    return copy


def greet(peers):
    barrier = pltpu.get_barrier_semaphore()
    for peer in peers:
        pl.semaphore_signal(barrier, inc=1, device_id=peer, device_id_type=MESH)


def neighbours(n_wide):
    w, n = lax.axis_index("wide"), lax.axis_index("narrow")
    ahead, behind = lax.rem(w + 1, n_wide), lax.rem(w + n_wide - 1, n_wide)
    return w, n, ahead, behind


class Shells:
    def __init__(self, n_wide, halo, sems, parts):
        self.w, self.n, ahead, behind = neighbours(n_wide)
        self.partner = (self.w, 1 - self.n)
        self.parts = [pl.ds(start, size) for start, size in parts]
        self.peers = [(behind, self.n), self.partner, (ahead, self.n)]
        self.halo, self.sems, self.copies, self.across = halo, sems, {}, {}

    def pair(self, k, i):
        return self.sems.at[0, k, i], self.sems.at[1, k, i]

    def start(self, sources, k):
        rows = self.parts[k]
        self.copies[k] = [
            send(sources[g].at[rows], self.halo.at[g, self.n, rows], self.pair(k, g), self.peers[g]) for g in range(3)
        ]

    def forward(self, k):
        self.across[k] = []
        for g in (0, 2):
            self.copies[k][g].wait()
            got = self.halo.at[g, self.n, self.parts[k]]
            self.across[k].append(send(got, got, self.pair(k, 3 + g), self.partner))

    def settle(self, k):
        self.copies[k][1].wait()
        for copy in self.across[k]:
            copy.wait()


class Returns:
    def __init__(self, n_wide, out, got, joined, arrived, sems):
        self.w, self.n, ahead, behind = neighbours(n_wide)
        self.partner = (self.w, 1 - self.n)
        self.to = {0: (ahead, self.n), 2: (behind, self.n)}
        self.out, self.got, self.joined, self.arrived, self.sems = out, got, joined, arrived, sems

    def pair(self, i):
        return self.sems.at[0, i], self.sems.at[1, i]

    def start(self):
        self.joins = [
            send(self.out.at[g, 1 - self.n], self.got.at[i], self.pair(i), self.partner) for i, g in enumerate((0, 2))
        ]
        self.backs = [send(self.out.at[1, 1 - self.n], self.arrived.at[1], self.pair(2), self.partner)]

    def join(self):
        for i, g in enumerate((0, 2)):
            self.joins[i].wait()
            self.joined[i] = (self.out[g, self.n].astype(F32) + self.got[i].astype(F32)).astype(BF16)
            self.backs.append(send(self.joined.at[i], self.arrived.at[g], self.pair(3 + i), self.to[g]))

    def add(self, grads):
        for copy in self.backs:
            copy.wait()
        for t in range(B):
            for g in range(3):
                faces = stretch(self.arrived[g, t * TIGHT_FACES : (t + 1) * TIGHT_FACES].astype(F32))
                add_faces(faces.reshape(FACES // 8, 8, L), grads, t)


class Sum:
    def __init__(self, nz, nxy, src, whole, at, scratch):
        self.nz, self.nxy, self.src, self.whole, self.at = nz, nxy, src, whole, at
        (self.half, self.got1, self.got2, self.got3,
         self.sem1, self.sem2, self.sem3, self.sem4, self.sem5) = scratch
        w, self.n = lax.axis_index("wide"), lax.axis_index("narrow")
        self.z, self.xy = w // nxy, lax.rem(w, nxy)
        self.plane = HALF // nxy
        self.partner = (w, 1 - self.n)
        nx = 4 if nxy % 4 == 0 else nxy
        ny = nxy // nx
        x, y = lax.rem(self.xy, nx), self.xy // nx

        def place(dx, dy):
            return lax.rem(y + dy + ny, ny) * nx + lax.rem(x + dx + nx, nx)

        def hops(step, size):
            return min(step, size - step)

        steps = [(dx, dy) for dx in range(nx) for dy in range(ny) if dx or dy]
        steps.sort(key=lambda step: -hops(step[0], nx) - hops(step[1], ny))
        self.to = [place(dx, dy) for dx, dy in steps]
        self.origin = [place(-dx, -dy) for dx, dy in steps]
        self.in_plane = [(self.z * nxy + to, self.n) for to in self.to]
        rises = sorted(range(1, nz), key=lambda rise: -hops(rise, nz))
        self.in_column = [(lax.rem(self.z + rise, nz) * nxy + self.xy, self.n) for rise in rises]

    def peers(self):
        return self.in_column + self.in_plane + [self.partner]

    def rows(self, at, size):
        return pl.ds(pl.multiple_of(at, size), size)

    def pair(self, sems, d):
        return sems.at[0, d], sems.at[1, d]

    def cores(self):
        theirs = self.src.at[self.rows((1 - self.n) * HALF, HALF)]
        self.copies = [send(theirs, self.got1, self.pair(self.sem1, 0), self.partner)]

    def wait(self):
        for copy in self.copies:
            copy.wait()

    def planes(self):
        self.wait()
        mine = self.src[self.rows(self.n * HALF, HALF), :]
        self.half[...] = (mine + self.got1[...]).astype(BF16)
        self.copies = []
        for d, peer in enumerate(self.in_plane):
            part = self.half.at[self.rows(self.to[d] * self.plane, self.plane)]
            self.copies.append(send(part, self.got2.at[d], self.pair(self.sem2, d), peer))

    def column(self):
        self.wait()
        total = self.half[self.rows(self.xy * self.plane, self.plane), :].astype(F32)
        for d in range(self.nxy - 1):
            total += self.got2[d].astype(F32)
        own = self.got3.at[self.z]
        own[...] = total.astype(BF16)
        self.copies = [send(own, own, self.pair(self.sem3, d), peer) for d, peer in enumerate(self.in_column)]

    def planes_back(self):
        self.wait()
        total = self.got3[0].astype(F32)
        for z in range(1, self.nz):
            total += self.got3[z].astype(F32)
        own = self.rows(self.at + self.n * HALF + self.xy * self.plane, self.plane)
        self.whole[own, :] = total.astype(BF16)
        own = self.whole.at[own]
        self.copies = [send(own, own, self.pair(self.sem4, d), peer) for d, peer in enumerate(self.in_plane)]
        self.across = [send(own, own, self.pair(self.sem5, self.nxy - 1), self.partner)]

    def cores_back(self):
        for d, copy in enumerate(self.copies):
            copy.wait()
            got = self.whole.at[self.rows(self.at + self.n * HALF + self.origin[d] * self.plane, self.plane)]
            self.across.append(send(got, got, self.pair(self.sem5, d), self.partner))

    def end(self):
        for copy in self.across:
            copy.wait()


def sum_scratch(nz, nxy):
    plane = HALF // nxy
    sems = [pltpu.SemaphoreType.DMA((2, count)) for count in (1, nxy - 1, nz - 1, nxy - 1, nxy)]
    return [
        pltpu.VMEM((HALF, L), BF16),
        pltpu.VMEM((HALF, L), F32),
        pltpu.VMEM((nxy - 1, plane, L), BF16),
        pltpu.VMEM((nz, plane, L), BF16),
    ] + sems


def main_kernel(nz, nxy, far_slots, far_plan, far_features, far_occupancy, far_out_grad, far_weights1, far_weights2,
                output, feature_grad, reduced,
                table, shifted, columns, side, back, around, padded, middle, low, high, planes, edges, faces, grads,
                mask, slope, chosen, shell, masked, pre, sums, packed1, packed2, features, occupancy, out_grad, weights1, weights2,
                messages, near, hidden_shells, hidden_near,
                out1, got1, joined1, arrived1, out2, got2, joined2, arrived2,
                near_sems, hidden_sems, back_sems1, back_sems2, load_sems, slots, plan, *scratch):
    n_wide = nz * nxy
    n = lax.axis_index("narrow")
    blocks = [(t * TIGHT, TIGHT) for t in range(B)]
    actives = Shells(n_wide, near, near_sems, [(B * TIGHT, 16)] + blocks)
    hiddens = Shells(n_wide, hidden_near, hidden_sems, blocks)
    returns1 = Returns(n_wide, out1, got1, joined1, arrived1, back_sems1)
    returns2 = Returns(n_wide, out2, got2, joined2, arrived2, back_sems2)
    total1 = Sum(nz, nxy, packed1, reduced, 0, scratch[: len(scratch) // 2])
    total2 = Sum(nz, nxy, packed2, reduced, ROWS, scratch[len(scratch) // 2 :])
    everyone = total1.peers() + [actives.peers[0], actives.peers[2]]
    greet(everyone)
    far = (far_occupancy, far_features, far_plan, far_out_grad, far_weights2, far_slots, far_weights1)
    loads = []
    for i, (source, dest) in enumerate(zip(far, (occupancy, features, plan, out_grad, weights2, slots, weights1))):
        loads.append(pltpu.make_async_copy(source, dest, load_sems.at[i]))
        loads[i].start()
    loads[0].wait()
    loads[1].wait()

    for t in range(B):
        seen = occupancy[t : t + 1, :].astype(F32)
        table[t] = to_rows(features[t].astype(F32) * seen).reshape(8, 8, 8, L)
    row = lax.broadcasted_iota(jnp.int32, (16, L), 0)
    loads[2].wait()
    for t in range(B):
        pack_own(table, shell, messages.at[0], t)
    for g in range(3):
        if g > 0:
            messages[g, 0 : 2 * TIGHT] = messages[0, 0 : 2 * TIGHT]
        rows = jnp.zeros((16, L), F32)
        for i in range(4):
            rows = jnp.where(row == i, plan[i, g].astype(F32), rows)
        messages[g, 2 * TIGHT : MESSAGE] = rows.astype(BF16)

    loads[3].wait()
    padded[...] = jnp.zeros_like(padded)
    masked[C:L] = jnp.zeros((L - C, B * V), BF16)
    for t in range(B):
        seen = occupancy[t : t + 1, :].astype(F32)
        mask[t] = jnp.broadcast_to(seen, (L, V)).T
        own = out_grad[t].astype(F32) * seen
        masked[0:C, t * V : (t + 1) * V] = own.astype(BF16)
        padded[t, 2:10, 2:10] = to_rows(own).reshape(8, 8, 8, L)

    def transpose(t):
        spread(t, padded, around, back, middle, low, high, planes, edges)
        scatter(t, slots, middle, planes, edges, faces)
        grads[t] = middle[1:9, 1:9]

    def add_own():
        for t in range(B):
            add_faces(faces[t], grads, t)

    loads[4].wait()
    loads[5].wait()
    back_weights(weights2, back)
    faces[...] = jnp.zeros_like(faces)
    pl.semaphore_wait(pltpu.get_barrier_semaphore(), len(everyone))
    for k in range(1 + B):
        actives.start([messages.at[g] for g in range(3)], k)
    transpose(0)
    transpose(1)
    add_own()
    loads[6].wait()
    side_weights(weights1, side)
    table[EMPTY] = jnp.zeros((8, 8, 8, L), F32)
    actives.forward(0)
    actives.settle(0)
    for source in range(SLOTS // 2):
        rows = near[source // 2, source % 2, 2 * TIGHT : MESSAGE].astype(F32)
        for c in range(2):
            row = jnp.where(n == 0, rows[c : c + 1], rows[2 + c : 3 + c])
            chosen[2 * source + c] = jnp.broadcast_to(row, (8, L))
    gather_gradients(faces, chosen, out1)
    returns1.start()

    for k in (1, 2):
        actives.forward(k)
    returns1.join()
    for k in (1, 2):
        actives.settle(k)
    halo_entries(table, near, chosen)
    build_columns(slots, table, shifted, columns)
    for t in range(B):
        value = lax.dot_general(
            columns[t * V : (t + 1) * V, :], side[...], (((1,), (1,)), ((), ())), preferred_element_type=F32
        )
        seen = mask[t]
        gate = jax.nn.sigmoid(value)
        table[t] = (value * gate * seen).astype(BF16).astype(F32).reshape(8, 8, 8, L)
        pack_own(table, shell, hidden_shells, t)
        hiddens.start([hidden_shells] * 3, t)
        slope[t] = seen * gate * (1.0 + value * (1.0 - gate))
    side_weights(weights2, side)
    returns1.add(grads)
    for t in range(B):
        grad = grads[t].reshape(V, L) * slope[t]
        padded[t, 2:10, 2:10] = grad.reshape(8, 8, 8, L)
        pre[:, t * V : (t + 1) * V] = grad.T.astype(BF16)
    weight_sums(n, pre, columns, sums, packed1, total1)

    for t in range(B):
        hiddens.forward(t)
    total1.planes()
    for t in range(B):
        hiddens.settle(t)
    halo_entries(table, hidden_near, chosen)
    build_columns(slots, table, shifted, columns)
    weight_sums(n, masked, columns, sums, packed2, total2)

    def forward(t):
        seen = occupancy[t : t + 1, :].astype(F32)
        value = lax.dot_general(
            side[...], columns[t * V : (t + 1) * V, :], (((1,), (1,)), ((), ())), preferred_element_type=F32
        )
        output[t] = ((features[t].astype(F32) * seen + value[0:C]) * seen).astype(BF16)

    forward(0)
    total2.planes()
    total1.column()
    back_weights(weights1, back)
    faces[...] = jnp.zeros_like(faces)
    for t in range(B):
        transpose(t)
    total2.column()
    gather_gradients(faces, chosen, out2)
    returns2.start()
    total1.planes_back()
    returns2.join()
    add_own()
    forward(1)
    total2.planes_back()
    returns2.add(grads)
    for t in range(B):
        seen = occupancy[t : t + 1, :].astype(F32)
        own = grads[t].reshape(V, L).T
        feature_grad[t] = ((out_grad[t].astype(F32) * seen + own[0:C]) * seen).astype(BF16)
    total1.cores_back()
    total2.cores_back()
    total1.end()
    total2.end()


VMEM_SPEC = pl.BlockSpec(memory_space=pltpu.VMEM)
HBM_SPEC = pl.BlockSpec(memory_space=pltpu.HBM)


def shape(dims, dtype):
    return jax.ShapeDtypeStruct(dims, dtype)


BLOCK = (8, 8, 8, L)
SCRATCH = [
    ((EMPTY + 1,) + BLOCK, F32),
    ((3, 10, 10, 8, L), F32),
    ((B * V, 27 * L), BF16),
    ((L, 27 * L), BF16),
    ((9 * L, 3 * L), BF16),
    ((800, 9 * L), BF16),
    ((B, 12, 12, 8, L), F32),
    ((10, 10, 8, L), F32),
    ((10, 10, 8, L), F32),
    ((10, 10, 8, L), F32),
    ((2, 10, 8, L), F32),
    ((2, 2, 10, 8, L), F32),
    ((EMPTY, FACES // 8, 8, L), F32),
    ((B,) + BLOCK, F32),
    ((B, V, L), F32),
    ((B, V, L), F32),
    ((SLOTS, 8, L), F32),
    ((SHELL // 8, 8, L), F32),
    ((L, B * V), BF16),
    ((L, B * V), BF16),
    ((WG, L), F32),
    ((ROWS, L), F32),
    ((ROWS, L), F32),
    ((B, C, V), BF16),
    ((B, V), jnp.int32),
    ((B, C, V), BF16),
    ((27, C, C), BF16),
    ((27, C, C), BF16),
    ((3, MESSAGE, L), BF16),
    ((3, 2, MESSAGE, L), BF16),
    ((2 * TIGHT, L), BF16),
    ((3, 2, 2 * TIGHT, L), BF16),
] + 2 * [
    ((3, 2, 2 * TIGHT_FACES, L), BF16),
    ((2, 2 * TIGHT_FACES, L), BF16),
    ((2, 2 * TIGHT_FACES, L), BF16),
    ((3, 2 * TIGHT_FACES, L), BF16),
]


def local(nz, nxy, features, occupancy, conv1_weight, conv2_weight, out_grad, slots, send_blocks):
    dma = pltpu.SemaphoreType.DMA
    blocks = shape((B, C, V), BF16)
    inputs = (slots, send_blocks.reshape(3, 4).T, features, occupancy, out_grad, conv1_weight, conv2_weight)
    output, feature_grad, reduced = pl.pallas_call(
        functools.partial(main_kernel, nz, nxy),
        out_shape=[blocks, blocks, shape((2 * ROWS, L), BF16)],
        in_specs=[HBM_SPEC] * 7,
        out_specs=[VMEM_SPEC] * 3,
        scratch_shapes=[pltpu.VMEM(dims, dtype) for dims, dtype in SCRATCH]
        + [dma((2, 3, 6)), dma((2, 2, 6)), dma((2, 5)), dma((2, 5)), dma((7,)), pltpu.SMEM((B, 27), jnp.int32), pltpu.SMEM((4, 3), jnp.int32)] + 2 * sum_scratch(nz, nxy),
        compiler_params=pltpu.CompilerParams(
            collective_id=0, has_side_effects=True, vmem_limit_bytes=VMEM_LIMIT
        ),
    )(*(pltpu.with_memory_space_constraint(x, pltpu.HBM) for x in inputs))
    scale = (B * V * 2 * nz * nxy) ** -0.5
    return pl.pallas_call(
        functools.partial(last_kernel, scale),
        out_shape=[blocks, blocks] + [shape((27, C, C), F32)] * 2,
        in_specs=[VMEM_SPEC] * 3,
        out_specs=[VMEM_SPEC] * 4,
        compiler_params=pltpu.CompilerParams(vmem_limit_bytes=LAST_LIMIT),
    )(reduced, output, feature_grad)


def solution(mesh):
    both = ("wide", "narrow")
    n_wide = mesh.shape["wide"]
    nxy = 16 if n_wide % 16 == 0 else n_wide // 2
    return jax.shard_map(
        functools.partial(local, n_wide // nxy, nxy),
        mesh=mesh,
        in_specs=(P(both, None, None), P(both, None), P(), P(), P(both, None, None), P(both, None),
                  P(both, None, None, None)),
        out_specs=(P(both, None, None), P(both, None, None), P(), P()),
        check_vma=False,
    )
```
